128 devices in a mesh: cells: 32 (over x, z, core), split: 4 (over y).
Axes of the slice: x: 4, y: 4, z: 4, core: 2. Of those that a mesh axis runs over, the one named last changes fastest.
Arguments:
- voltage: float32 [4, 32, 131072], P('split', None, 'cells'), may hold values from -4 to 4
- gate_state: float32 [4, 32, 131072], P('split', None, 'cells'), may hold values from 0 to 1
- stimulus: float32 [4, 32, 131072], P('split', None, 'cells'), may hold values from -6 to 6
- gate_rate: float32 [4, 32, 131072], P('split', None, 'cells'), may hold values from 0.05 to 1
- gate_conductance: float32 [4, 32, 131072], P('split', None, 'cells'), may hold values from 0.2 to 2
- soma_voltage: float32 [131072], P('cells'), may hold values from -4 to 4
- soma_stimulus: float32 [131072], P('cells'), may hold values from -12 to 12
- axial_conductance: float32 [4, 32], replicated, may hold values from 0.5 to 4
- gap_source: int32 [262144], P(('cells', 'split')), may hold values from 0 to 131071
- gap_route: int32 [262144, 1], P(('cells', 'split')), may hold values from 0 to 127; in each aligned block of 2048 rows (0 to 2047, 2048 to 4095, ...) at most 32 rows name the same one
- gap_target: int32 [262144], P(('cells', 'split')), may hold values from 0 to 131071
- gap_conductance: float32 [262144], P(('cells', 'split')), may hold values from 0.05 to 0.5
- vox_index: int32 [4, 4, 131072], P('split', None, 'cells'), may hold values from 0 to 65535, as said below
- field_resist: float32 [65536], P(('cells', 'split')), may hold values from 0.5 to 5
Outputs:
- voltage_out: float32 [4, 32, 131072], P('split', None, 'cells')
- gate_out: float32 [4, 32, 131072], P('split', None, 'cells')
- soma_out: float32 [131072], P('cells')
- field_potential: float32 [65536], P(('cells', 'split'))
The draws below stay inside these ranges and needn't reach their ends.
Inputs may be any that keep to these rules, and one draw needn't show every extreme that they name: `gap_route`: among the rows of one device at most 32 name the same device, and some device is named by exactly 32 rows of one device. `vox_index`: among the 16384 blocks of one device at most 256 fall on voxels of one owner; on every device exactly 256 fall on one owner, and the others are spread evenly over the remaining owners.
All inputs are finite; a program needn't handle non-finite values.
Results may differ from the reference program's by a relative error of at most 0.0001.
Values sent between devices are 32-bit elements; how exact they have to be, the bound alone decides.
No kernel may reach another device: no remote copies, remote signals or barrier semaphores. Data moves between devices by JAX's collectives and lax.ppermute only.
A program may use at most 128 MiB of HBM per device.

```python
import math
import jax
import jax.numpy as jnp
import numpy as np
from jax import lax

COMP = 32
BLK = 8
SUB = 2
CELL_DEV = 4096
GJ_DEV = 2048
VOX_DEV = 512
BRANCHES = 4
NBLK = 4
CELLS = 131072
GJ_ROWS = 262144
CAP = 32
VOX = 65536
N_SPLIT = 4
DEVICES = 128


def draw_vox_index(key, part):
    key = jax.random.fold_in(key, 7)
    local_blocks = NBLK * CELL_DEV
    device_count = DEVICES
    heavy_cap = max(2, 2 * local_blocks // device_count)
    first_key, second_key, third_key = jax.random.split(key, 3)
    heavy = jax.random.randint(first_key, (device_count,), 0, device_count)
    places = jnp.arange(local_blocks, dtype=jnp.int32)
    cycled = (places - heavy_cap) % (device_count - 1)
    others = cycled[None, :] + (cycled[None, :] >= heavy[:, None]).astype(jnp.int32)
    owners = jnp.where(places[None, :] < heavy_cap, heavy[:, None], others)
    orders = jax.vmap(lambda single: jax.random.permutation(single, local_blocks))(jax.random.split(second_key, device_count))
    owners = jnp.take_along_axis(owners, orders, axis=1)
    within = jax.random.randint(third_key, (device_count, local_blocks), 0, VOX_DEV)
    voxels = owners * VOX_DEV + within
    group_count = device_count // BRANCHES
    shaped = voxels.reshape(group_count, BRANCHES, NBLK, CELL_DEV).transpose(1, 2, 0, 3)
    return shaped.reshape(BRANCHES, NBLK, group_count * CELL_DEV).astype(jnp.int32)


def plant(array, rng, low, largest):
    place = [jax.random.randint(jax.random.fold_in(rng, axis), (), 0, length) for axis, length in enumerate(array.shape)]
    widest = array.shape.index(max(array.shape))
    neighbour = place[:widest] + [(place[widest] + 1) % array.shape[widest]] + place[widest + 1:]
    return array.at[tuple(place)].set(low).at[tuple(neighbour)].set(largest)


def level_of(own_key, extent, pieces, smallest, top_value):
    loudness, own = 1.0, jax.random.fold_in(own_key, 6)
    for position, blocks in pieces:
        heights = jnp.exp(jax.random.uniform(jax.random.fold_in(own, position), (blocks,), jnp.float32, smallest / len(pieces), top_value / len(pieces)))
        loudness = loudness * jnp.repeat(heights, extent[position] // blocks).reshape([-1 if axis == position else 1 for axis in range(len(extent))])
    return loudness


def shared_out(rng, own, number, rows, number_of, top, reach, slope):
    sequence = jax.random.permutation(rng, number_of)
    packed, usual = portions_of(number_of, rows * top, reach, slope, True), portions_of(number_of, rows * top, reach, slope, False)
    places = jnp.arange(number_of)

    def named(lengths, offset_by):
        used = int((lengths > 0).sum())
        fixed = max(1, used // 4)
        passed = fixed + (places - fixed + offset_by * (used - fixed)) % max(1, number_of - fixed)
        return jnp.zeros((number_of,), jnp.int32).at[sequence[jnp.where(places < fixed, places, passed)]].set(jnp.asarray(lengths, jnp.int32))

    lengths = jnp.where(number % 4 == 0, named(packed, number // 4), named(usual, number - number // 4 - 1))
    mixed = jax.random.permutation(jax.random.fold_in(own, 3), number_of)
    giver, sink = mixed[0:number_of // 2 * 2:2], mixed[1:number_of // 2 * 2:2]
    slack = jnp.minimum(lengths[giver] - 1, reach - lengths[sink]) // 2
    slack = jnp.where((giver == sequence[0]) | (sink == sequence[0]) | (lengths[sink] == 0), 0, jnp.maximum(slack, 0))
    passed = jax.random.randint(jax.random.fold_in(own, 4), (number_of // 2,), 0, 1 << 20) % (slack + 1)
    lengths = lengths.at[giver].add(-passed).at[sink].add(passed)
    members = jnp.searchsorted(jnp.cumsum(lengths), jnp.arange(rows * top), side="right").astype(jnp.int32)
    grid = members.reshape(top, rows).T
    grid = grid[jax.random.permutation(jax.random.fold_in(own, 1), rows)]
    offset_by = jax.random.randint(jax.random.fold_in(own, 2), (rows, 1), 0, top)
    return jnp.take_along_axis(grid, (jnp.arange(top)[None, :] + offset_by) % top, axis=1)


def portions_of(amount, total, reach, slope, full):
    portions = [(1 << 20) // math.isqrt(standing ** slope) + 1 for standing in range(1, amount + 1)]
    largest = reach if full else min(reach, max(-(-total // amount), total * portions[0] // sum(portions)))
    least = 1 if total - largest >= amount - 1 else 0
    counts, rest = [largest] + [least] * (amount - 1), total - largest - least * (amount - 1)
    while rest > 0:
        movable = [i for i in range(1, amount) if counts[i] < largest] or [i for i in range(1, amount) if counts[i] < reach]
        mass, left = sum([portions[i] for i in movable]), rest
        for i in movable:
            extra = min(reach - counts[i], max(1, left * portions[i] // mass), rest)
            counts[i] = counts[i] + extra
            rest = rest - extra
    return np.array(counts)


def gaussian(rng, extent, spread, bound, cuts=(), held_as=jnp.bfloat16):
    array = spread * jax.random.normal(rng, extent, jnp.float32)
    if cuts:
        array = array * level_of(rng, extent, cuts, -0.22, 0.18)
    return jnp.clip(array, -bound, bound).astype(held_as)


def setup_inputs(seed: int = 0) -> dict:
    arg_keys = jax.random.split(jax.random.key(seed), 15)
    voltage = gaussian(arg_keys[0], (BRANCHES, COMP, CELLS), 1.0, 4.0, ((0, 4), (2, 32)), jnp.float32)
    gate_state = jnp.clip(1.0 * jax.random.uniform(arg_keys[1], (BRANCHES, COMP, CELLS), jnp.float32) ** level_of(arg_keys[1], (BRANCHES, COMP, CELLS), ((0, 4), (2, 32)), -0.2, 0.2), 0.0, 1.0)
    stimulus = gaussian(arg_keys[2], (BRANCHES, COMP, CELLS), 1.0, 6.0, ((0, 4), (2, 32)), jnp.float32)
    gate_rate = jnp.clip(jnp.exp(math.log(1.0) - 2.9957323 * jax.random.uniform(arg_keys[3], (BRANCHES, COMP, CELLS), jnp.float32) ** level_of(arg_keys[3], (BRANCHES, COMP, CELLS), ((0, 4), (2, 32)), -0.2, 0.2)), 0.05, 1.0)
    gate_conductance = jnp.clip(jnp.exp(math.log(2.0) - 2.3025851 * jax.random.uniform(arg_keys[4], (BRANCHES, COMP, CELLS), jnp.float32) ** level_of(arg_keys[4], (BRANCHES, COMP, CELLS), ((0, 4), (2, 32)), -0.2, 0.2)), 0.2, 2.0)
    soma_voltage = gaussian(arg_keys[5], (CELLS,), 1.0, 4.0, ((0, 32),), jnp.float32)
    soma_stimulus = gaussian(arg_keys[6], (CELLS,), 2.0, 12.0, ((0, 32),), jnp.float32)
    axial_conductance = jnp.clip(jnp.exp(jax.random.uniform(arg_keys[7], (BRANCHES, COMP), jnp.float32, math.log(0.5), math.log(4.0))), 0.5, 4.0)
    gap_source = plant(jax.random.randint(arg_keys[8], (GJ_ROWS,), 0, COMP * CELL_DEV), jax.random.fold_in(arg_keys[8], 1), 0, (COMP * CELL_DEV) - 1).astype(jnp.int32)
    gap_route_keys = jax.random.split(jax.random.fold_in(arg_keys[9], 1), GJ_ROWS // GJ_DEV)
    gap_route_turns = jax.random.permutation(jax.random.fold_in(arg_keys[9], 3), GJ_ROWS // GJ_DEV)
    gap_route = jax.vmap(lambda own, number: shared_out(jax.random.fold_in(arg_keys[9], 2), own, number, GJ_DEV, DEVICES, 1, CAP, 2))(gap_route_keys, gap_route_turns).reshape((GJ_ROWS, 1))
    gap_target = plant(jax.random.randint(arg_keys[10], (GJ_ROWS,), 0, COMP * CELL_DEV), jax.random.fold_in(arg_keys[10], 1), 0, (COMP * CELL_DEV) - 1).astype(jnp.int32)
    gap_conductance = jnp.clip(jnp.exp(math.log(0.5) - 2.3025851 * jax.random.uniform(arg_keys[11], (GJ_ROWS,), jnp.float32) ** level_of(arg_keys[11], (GJ_ROWS,), ((0, 128),), -0.2, 0.2)), 0.05, 0.5)
    vox_index = draw_vox_index(jax.random.fold_in(arg_keys[14], 71), 0)
    field_resist = jnp.clip(jnp.exp(math.log(5.0) - 2.3025851 * jax.random.uniform(arg_keys[13], (VOX,), jnp.float32) ** level_of(arg_keys[13], (VOX,), ((0, 128),), -0.2, 0.2)), 0.5, 5.0)
    return {"voltage": voltage, "gate_state": gate_state, "stimulus": stimulus, "gate_rate": gate_rate, "gate_conductance": gate_conductance, "soma_voltage": soma_voltage, "soma_stimulus": soma_stimulus, "axial_conductance": axial_conductance, "gap_source": gap_source, "gap_route": gap_route, "gap_target": gap_target, "gap_conductance": gap_conductance, "vox_index": vox_index, "field_resist": field_resist}


membrane_diag = 4.0
soma_diag = 8.0
reversal = -1.0
ephaptic = 0.5

def branch_inverses(axial_conductance):
    comp_count = axial_conductance.shape[1]
    beyond = jnp.concatenate([axial_conductance[:, 1:], jnp.zeros((axial_conductance.shape[0], 1), axial_conductance.dtype)], axis=1)
    diagonal = membrane_diag + axial_conductance + beyond

    def single_inverse(diag_row, off_row):
        matrix = jnp.diag(diag_row) - jnp.diag(off_row[:-1], 1) - jnp.diag(off_row[:-1], -1)
        factor = jnp.linalg.cholesky(matrix)
        identity = jnp.eye(comp_count, dtype=diag_row.dtype)
        lower_inv = lax.linalg.triangular_solve(factor, identity, left_side=True, lower=True)
        return jnp.dot(lower_inv.T, lower_inv, precision=lax.Precision.HIGHEST)
    return jax.vmap(single_inverse)(diagonal, beyond)

def reference(voltage, gate_state, stimulus, gate_rate, gate_conductance, soma_voltage, soma_stimulus, axial_conductance, gap_source, gap_route, gap_target, gap_conductance, vox_index, field_resist):
    inverses = branch_inverses(axial_conductance)
    head_axial = axial_conductance[:, 0]
    shared = jnp.sum(head_axial * head_axial * inverses[:, 0, 0])
    soma_total = soma_diag + jnp.sum(head_axial)
    row_ids = jnp.arange(gap_source.shape[0], dtype=jnp.int32)
    owner_device = row_ids // GJ_DEV
    source_index = owner_device % N_SPLIT * (COMP * CELLS) + gap_source // CELL_DEV * CELLS + owner_device // N_SPLIT * CELL_DEV + gap_source % CELL_DEV
    destination = gap_route[:, 0]
    target_index = destination % N_SPLIT * (COMP * CELLS) + gap_target // CELL_DEV * CELLS + destination // N_SPLIT * CELL_DEV + gap_target % CELL_DEV
    total_comps = N_SPLIT * COMP * CELLS
    weight_total = jax.ops.segment_sum(gap_conductance, target_index, num_segments=total_comps).reshape(voltage.shape)
    field_scale = VOX_DEV / (COMP * CELL_DEV)
    volts_now = voltage
    gating = gate_state
    soma = soma_voltage
    phi_comp = jnp.zeros_like(voltage)
    potential = jnp.zeros_like(field_resist)
    for substep in range(SUB):
        flat_volts = volts_now.reshape(-1)
        gap_in = jax.ops.segment_sum(gap_conductance * flat_volts[source_index], target_index, num_segments=total_comps).reshape(voltage.shape) - weight_total * volts_now
        settle = jax.nn.sigmoid(2.0 * volts_now)
        gating = settle + (gating - settle) * jnp.exp(-gate_rate * (1.0 + volts_now * volts_now))
        current = gate_conductance * gating * (volts_now - reversal)
        block_sums = current.reshape(N_SPLIT, NBLK, BLK, CELLS).sum(axis=2)
        voxel = jax.ops.segment_sum(block_sums.reshape(-1), vox_index.reshape(-1), num_segments=VOX)
        potential = field_resist * voxel * field_scale
        rhs = membrane_diag * volts_now + stimulus - current + gap_in - ephaptic * phi_comp
        solved = jnp.einsum('bij,bjc->bic', inverses, rhs, precision=lax.Precision.HIGHEST)
        partial_value = jnp.sum(head_axial[:, None] * solved[:, 0, :], axis=0)
        soma = (soma_diag * soma + soma_stimulus + partial_value) / (soma_total - shared)
        volts_now = solved + head_axial[:, None, None] * inverses[:, :, 0:1] * soma[None, None, :]
        looked = potential[vox_index]
        phi_comp = jnp.broadcast_to(looked[:, :, None, :], (N_SPLIT, NBLK, BLK, CELLS)).reshape(voltage.shape)
    return (volts_now, gating, soma, potential)
```

```python
import jax
import jax.numpy as jnp
from jax import lax
from jax.experimental import pallas as pl
from jax.experimental.pallas import tpu as pltpu
from jax.sharding import PartitionSpec as P

SUB = 2
CAP = 32
LOW = 512
STEP = 512

membrane_diag = 4.0
soma_diag = 8.0
reversal = -1.0
ephaptic = 0.5

f32 = jnp.float32
bf16 = jnp.bfloat16
AXES = ("cells", "split")
PARAMS = pltpu.CompilerParams(vmem_limit_bytes=48 * 2**20)
LANES = (((1,), (1,)), ((), ()))


def halves(x):
    high = x.astype(bf16)
    return high, (x - high.astype(f32)).astype(bf16)


def hits(row, size):
    rows = lax.broadcasted_iota(jnp.int16, (size, row.shape[1]), 0)
    return rows == row.astype(jnp.int16)


def chosen(mask, row):
    return jnp.where(mask, row, jnp.zeros((), bf16))


def hot(row, size):
    return jnp.where(hits(row, size), jnp.ones((), bf16), jnp.zeros((), bf16))


def comp_digits(index, cell_dev, comp_count):
    chunks = cell_dev // LOW
    low = index % LOW
    chunk = (index // LOW) % chunks
    return chunk * comp_count + index // cell_dev, low


def inverse_kernel(axial_ref, inverse_ref, soma_ref):
    n = axial_ref.shape[0]
    lanes = axial_ref.shape[1]
    axial = axial_ref[...]
    row = [axial[i : i + 1, :] for i in range(n)]
    lane = lax.broadcasted_iota(jnp.int32, (1, lanes), 1)
    pivot = [None] * n
    ratio = [None] * n
    pivot[n - 1] = membrane_diag + row[n - 1]
    ratio[n - 1] = row[n - 1] / pivot[n - 1]
    for i in range(n - 2, -1, -1):
        pivot[i] = membrane_diag + row[i] + row[i + 1] - row[i + 1] * ratio[i + 1]
        ratio[i] = row[i] / pivot[i]
    upper = [None] * n
    upper[n - 1] = jnp.where(lane == n - 1, 1.0, 0.0)
    for i in range(n - 2, -1, -1):
        upper[i] = jnp.where(lane == i, 1.0, 0.0) + ratio[i + 1] * upper[i + 1]
    result = upper[0] / pivot[0]
    inverse_ref[0:1, :] = result
    for i in range(1, n):
        result = upper[i] / pivot[i] + ratio[i] * result
        inverse_ref[i : i + 1, :] = result
    branch = (lane >= n) & (lane < n + 4)
    total = soma_diag + jnp.sum(jnp.where(branch, row[0], 0.0), axis=1, keepdims=True)
    shared = jnp.sum(jnp.where(branch, row[0] * ratio[0], 0.0), axis=1, keepdims=True)
    head = row[0][:, 0:1]
    soma_ref[0:1, :] = jnp.broadcast_to(total - shared, (1, lanes))
    soma_ref[1:2, :] = jnp.broadcast_to(head, (1, lanes))


def membrane(volts, gating, rate, cond):
    settle = jax.nn.sigmoid(2.0 * volts)
    gating = settle + (gating - settle) * jnp.exp(-rate * (1.0 + volts * volts))
    return gating, cond * gating * (volts - reversal)


def fill_table(table_ref, volts, comp_count, cell_dev):
    chunks = cell_dev // LOW
    high, low = halves(volts)
    for j in range(chunks):
        at = j * comp_count
        table_ref[at : at + comp_count, :] = high[:, j * LOW : (j + 1) * LOW]
        at += chunks * comp_count
        table_ref[at : at + comp_count, :] = low[:, j * LOW : (j + 1) * LOW]


def pick_rows(table_ref, source, comp_count, cell_dev):
    size = table_ref.shape[0] // 2
    pieces = []
    for at in range(0, source.shape[1], STEP):
        high, low = comp_digits(source[:, at : at + STEP], cell_dev, comp_count)
        found = jnp.dot(table_ref[...], hot(low, LOW), preferred_element_type=f32)
        rows = lax.broadcasted_iota(jnp.int32, (size, STEP), 0)
        both = jnp.where(rows == high, found[:size] + found[size:], 0.0)
        pieces.append(jnp.sum(both, axis=0, keepdims=True))
    return jnp.concatenate(pieces, axis=1)


def add_voxels(sums_ref, vox_ref, current_ref, block_size, devices):
    block_count = vox_ref.shape[0]
    sums_ref[...] = jnp.zeros_like(sums_ref)

    def add(c, unused):
        cols = pl.ds(pl.multiple_of(c * STEP, STEP), STEP)
        owners, voxels = [], []
        for k in range(block_count):
            index = vox_ref[k : k + 1, cols]
            rows = slice(k * block_size, (k + 1) * block_size)
            high, low = halves(jnp.sum(current_ref[rows, cols], axis=0, keepdims=True))
            mask = hits(index // LOW, devices)
            owners.append(jnp.concatenate([chosen(mask, high), chosen(mask, low)], axis=0))
            voxels.append(hot(index % LOW, LOW))
        sums_ref[...] += lax.dot_general(
            jnp.concatenate(owners, axis=1),
            jnp.concatenate(voxels, axis=1),
            LANES,
            preferred_element_type=f32,
        )
        return unused

    lax.fori_loop(0, vox_ref.shape[1] // STEP, add, 0)


def put_voxels(send_ref, sums_ref, devices, stride):
    sums = sums_ref[:devices, :] + sums_ref[devices:, :]
    for j in range(LOW // 128):
        send_ref[pl.ds(j, devices, stride=stride), :] = sums[:, j * 128 : (j + 1) * 128]


def slot_rows(values, dest_hot, rank_mask):
    parts = []
    for value in values:
        high, low = halves(value)
        parts += [chosen(rank_mask, high), chosen(rank_mask, low)]
    laid = lax.dot_general(
        jnp.concatenate(parts, axis=0), dest_hot, LANES, preferred_element_type=f32
    )
    return [
        laid[(2 * q) * CAP : (2 * q + 1) * CAP] + laid[(2 * q + 1) * CAP : (2 * q + 2) * CAP]
        for q in range(len(values))
    ]


def first_kernel(
    devices, stride,
    volts_ref, gate_ref, rate_ref, cond_ref, vox_ref,
    source_ref, route_ref, target_ref, weight_ref,
    send_ref, rank_ref, gate_out, current_out,
    table_ref, sums_ref,
):
    comp_count, cell_dev = volts_ref.shape
    rows = source_ref.shape[1]
    span = 256
    earlier = jnp.where(
        lax.broadcasted_iota(jnp.int32, (span, span), 0)
        < lax.broadcasted_iota(jnp.int32, (span, span), 1),
        1.0, 0.0,
    ).astype(bf16)
    before = jnp.zeros((devices, 1), f32)
    ranks, dests = [], []
    for at in range(0, rows, span):
        dest = hot(route_ref[:, at : at + span], devices)
        count = jnp.dot(dest, earlier, preferred_element_type=f32) + before
        full = dest.astype(f32)
        ranks.append(jnp.sum(full * count, axis=0, keepdims=True))
        before = count[:, span - 1 : span] + full[:, span - 1 : span]
        dests.append(dest)
    rank = jnp.concatenate(ranks, axis=1).astype(jnp.int32)
    rank_ref[...] = rank
    dest_hot = jnp.concatenate(dests, axis=1)
    volts = volts_ref[...]
    fill_table(table_ref, volts, comp_count, cell_dev)
    weight = weight_ref[...]
    sent = weight * pick_rows(table_ref, source_ref[...], comp_count, cell_dev)
    slots = slot_rows([target_ref[...].astype(f32), weight, sent], dest_hot, hits(rank, CAP))
    slots.append(jnp.zeros((128 - 3 * CAP, devices), f32))
    send_ref[pl.ds(LOW // 128, devices, stride=stride), :] = jnp.concatenate(slots, axis=0).T
    gating, current = membrane(volts, gate_ref[...], rate_ref[...], cond_ref[...])
    gate_out[...] = gating
    current_out[...] = current
    add_voxels(sums_ref, vox_ref, current_out, comp_count // vox_ref.shape[0], devices)
    put_voxels(send_ref, sums_ref, devices, stride)


def scatter_slots(target, values, comp_count, cell_dev):
    size = cell_dev // LOW * comp_count
    lefts, rights = [], []
    for k in range(0, CAP, 2):
        pair = lambda x: jnp.concatenate([x[k : k + 1], x[k + 1 : k + 2]], axis=1)
        high, low = comp_digits(pair(target), cell_dev, comp_count)
        mask = hits(high, size)
        parts = []
        for value in values:
            parts += [chosen(mask, half) for half in halves(pair(value))]
        lefts.append(jnp.concatenate(parts, axis=0))
        rights.append(hot(low, LOW))
    laid = lax.dot_general(
        jnp.concatenate(lefts, axis=1),
        jnp.concatenate(rights, axis=1),
        LANES,
        preferred_element_type=f32,
    )
    out = []
    for q in range(len(values)):
        total = laid[2 * q * size : (2 * q + 1) * size] + laid[(2 * q + 1) * size : (2 * q + 2) * size]
        out.append(total)
    return out


def as_cells(total, comp_count):
    chunks = total.shape[0] // comp_count
    return jnp.concatenate(
        [total[j * comp_count : (j + 1) * comp_count] for j in range(chunks)], axis=1
    )


def second_kernel(
    devices, stride, field_scale,
    recv_ref, volts_ref, stim_ref, current_ref, inverse_ref, soma_ref, resist_ref,
    solved_ref, partial_ref, weight_ref, target_ref, potential_ref,
):
    comp_count, cell_dev = volts_ref.shape
    for j in range(LOW // 128):
        own = jnp.sum(recv_ref[pl.ds(j, devices, stride=stride), :], axis=0, keepdims=True)
        potential_ref[j : j + 1, :] = resist_ref[j : j + 1, :] * own * field_scale
    slots = recv_ref[pl.ds(LOW // 128, devices, stride=stride), :].T
    target = slots[:CAP].astype(jnp.int32)
    target_ref[...] = target
    weight_total, gap = scatter_slots(
        target, [slots[CAP : 2 * CAP], slots[2 * CAP : 3 * CAP]], comp_count, cell_dev
    )
    weight_total = as_cells(weight_total, comp_count)
    weight_ref[...] = weight_total
    volts = volts_ref[...]
    gap_in = as_cells(gap, comp_count) - weight_total * volts
    rhs = membrane_diag * volts + stim_ref[...] - current_ref[...] + gap_in
    solved = jnp.dot(
        inverse_ref[:, :comp_count], rhs, precision=lax.Precision.HIGHEST,
        preferred_element_type=f32,
    )
    solved_ref[...] = solved
    partial_ref[...] = soma_ref[1:2, 0:1] * solved[0:1, :]


def next_soma(soma, stimulus, partials, total):
    partial = (partials[0] + partials[1]) + (partials[2] + partials[3])
    return (soma_diag * soma + stimulus + partial) / total


def third_kernel(
    devices, stride,
    solved_ref, p0_ref, p1_ref, p2_ref, p3_ref, soma_v_ref, soma_stim_ref,
    inverse_ref, soma_ref, gate_ref, rate_ref, cond_ref, stim_ref, weight_total_ref,
    vox_ref, source_ref, route_ref, rank_ref, weight_ref, potential_ref,
    send_ref, gate_out, soma_out, base_ref,
    table_ref, sums_ref, current_ref,
):
    comp_count, cell_dev = solved_ref.shape
    soma = next_soma(
        soma_v_ref[...], soma_stim_ref[...],
        [p0_ref[...], p1_ref[...], p2_ref[...], p3_ref[...]], soma_ref[0:1, 0:1],
    )
    soma_out[...] = soma
    volts = solved_ref[...] + soma_ref[1:2, 0:1] * inverse_ref[:, 0:1] * soma
    fill_table(table_ref, volts, comp_count, cell_dev)
    gating, current = membrane(volts, gate_ref[...], rate_ref[...], cond_ref[...])
    gate_out[...] = gating
    current_ref[...] = current
    base_ref[...] = membrane_diag * volts + stim_ref[...] - current - weight_total_ref[...] * volts
    sent = weight_ref[...] * pick_rows(table_ref, source_ref[...], comp_count, cell_dev)
    slots = slot_rows([sent], hot(route_ref[...], devices), hits(rank_ref[...], CAP))
    slots.append(jnp.zeros((128 - CAP, devices), f32))
    parts = LOW // 128
    send_ref[pl.ds(2 * parts, devices, stride=stride), :] = jnp.concatenate(slots, axis=0).T
    add_voxels(sums_ref, vox_ref, current_ref, comp_count // vox_ref.shape[0], devices)
    put_voxels(send_ref, sums_ref, devices, stride)
    for j in range(parts):
        send_ref[pl.ds(parts + j, devices, stride=stride), :] = jnp.broadcast_to(
            potential_ref[j : j + 1, :], (devices, 128)
        )


def fourth_kernel(
    devices, stride, field_scale,
    recv_ref, target_ref, base_ref, vox_ref, inverse_ref, soma_ref, resist_ref,
    solved_ref, partial_ref, potential_ref,
    rhs_ref,
):
    comp_count, cell_dev = base_ref.shape
    block_count = vox_ref.shape[0]
    block_size = comp_count // block_count
    parts = LOW // 128
    for j in range(parts):
        own = jnp.sum(recv_ref[pl.ds(j, devices, stride=stride), :], axis=0, keepdims=True)
        potential_ref[j : j + 1, :] = resist_ref[j : j + 1, :] * own * field_scale
    slots = recv_ref[pl.ds(2 * parts, devices, stride=stride), :].T
    (gap,) = scatter_slots(target_ref[...], [slots[:CAP]], comp_count, cell_dev)
    rhs_ref[...] = base_ref[...] + as_cells(gap, comp_count)
    table = jnp.concatenate(
        [recv_ref[pl.ds(parts + j, devices, stride=stride), :] for j in range(parts)], axis=1
    )
    table = jnp.concatenate(halves(table), axis=0)

    def look(c, unused):
        cols = pl.ds(pl.multiple_of(c * STEP, STEP), STEP)
        for k in range(block_count):
            index = vox_ref[k : k + 1, cols]
            found = jnp.dot(table, hot(index % LOW, LOW), preferred_element_type=f32)
            owners = lax.broadcasted_iota(jnp.int32, (devices, STEP), 0)
            both = jnp.where(owners == index // LOW, found[:devices] + found[devices:], 0.0)
            phi = jnp.sum(both, axis=0, keepdims=True)
            rows = slice(k * block_size, (k + 1) * block_size)
            rhs_ref[rows, cols] = rhs_ref[rows, cols] - ephaptic * phi
        return unused

    lax.fori_loop(0, cell_dev // STEP, look, 0)
    solved = jnp.dot(
        inverse_ref[:, :comp_count], rhs_ref[...], precision=lax.Precision.HIGHEST,
        preferred_element_type=f32,
    )
    solved_ref[...] = solved
    partial_ref[...] = soma_ref[1:2, 0:1] * solved[0:1, :]


def last_kernel(
    solved_ref, p0_ref, p1_ref, p2_ref, p3_ref, soma_v_ref, soma_stim_ref,
    inverse_ref, soma_ref, volts_ref, soma_out,
):
    soma = next_soma(
        soma_v_ref[...], soma_stim_ref[...],
        [p0_ref[...], p1_ref[...], p2_ref[...], p3_ref[...]], soma_ref[0:1, 0:1],
    )
    soma_out[...] = soma
    volts_ref[...] = solved_ref[...] + soma_ref[1:2, 0:1] * inverse_ref[:, 0:1] * soma


def call(kernel, outs, scratch=()):
    shapes = [jax.ShapeDtypeStruct(shape, dtype) for shape, dtype in outs]
    return pl.pallas_call(
        kernel, out_shape=shapes, scratch_shapes=list(scratch), compiler_params=PARAMS
    )


def bind(kernel, *sizes):
    def bound(*refs):
        kernel(*sizes, *refs)

    return bound


def exchange(send, devices):
    flat = lax.all_to_all(
        send.reshape(devices, send.size // devices), AXES, split_axis=0, concat_axis=0, tiled=True
    )
    return flat.reshape(send.shape)


def split_terms(partial, n_split):
    terms = [partial]
    for k in range(1, n_split):
        pairs = [(i, (i + k) % n_split) for i in range(n_split)]
        terms.append(lax.ppermute(partial, "split", pairs))
    return terms


def per_device(
    voltage, gate_state, stimulus, gate_rate, gate_conductance, soma_voltage, soma_stimulus,
    axial_conductance, gap_source, gap_route, gap_target, gap_conductance, vox_index, field_resist,
):
    n_split = lax.axis_size("split")
    devices = lax.axis_size("cells") * n_split
    comp_count, cell_dev = voltage.shape[1:]
    rows = gap_source.shape[0]
    vox_dev = field_resist.shape[0]
    field_scale = vox_dev / (comp_count * cell_dev)
    volts, gate, stim = voltage[0], gate_state[0], stimulus[0]
    rate, cond, vox = gate_rate[0], gate_conductance[0], vox_index[0]
    source = gap_source.reshape(1, rows)
    route = gap_route.reshape(1, rows)
    target = gap_target.reshape(1, rows)
    weight = gap_conductance.reshape(1, rows)
    soma_v = soma_voltage.reshape(1, cell_dev)
    soma_stim = soma_stimulus.reshape(1, cell_dev)
    resist = field_resist.reshape(vox_dev // 128, 128)

    own = lax.dynamic_index_in_dim(axial_conductance, lax.axis_index("split"), 0, keepdims=False)
    own = own[:, None]
    axial = jnp.concatenate(
        [
            jnp.broadcast_to(own, (comp_count, comp_count)),
            axial_conductance.T,
            jnp.broadcast_to(own, (comp_count, 128 - comp_count - n_split)),
        ],
        axis=1,
    )
    inverse, soma_consts = call(
        inverse_kernel, [((comp_count, 128), f32), ((2, 128), f32)]
    )(axial)

    full = ((comp_count, cell_dev), f32)
    line = ((1, cell_dev), f32)
    parts = vox_dev // 128
    table = pltpu.VMEM((2 * cell_dev // LOW * comp_count, LOW), bf16)
    sums = pltpu.VMEM((2 * devices, LOW), f32)

    stride = parts + 1
    send, rank, gate, current = call(
        bind(first_kernel, devices, stride),
        [((devices * stride, 128), f32), ((1, rows), jnp.int32), full, full],
        [table, sums],
    )(volts, gate, rate, cond, vox, source, route, target, weight)
    received = exchange(send, devices)
    solved, partial, weight_total, slot_target, potential = call(
        bind(second_kernel, devices, stride, field_scale),
        [full, line, full, ((CAP, devices), jnp.int32), ((parts, 128), f32)],
    )(received, volts, stim, current, inverse, soma_consts, resist)

    stride = 2 * parts + 1
    send, gate, soma, base = call(
        bind(third_kernel, devices, stride),
        [((devices * stride, 128), f32), full, line, full],
        [table, sums, pltpu.VMEM((comp_count, cell_dev), f32)],
    )(
        solved, *split_terms(partial, n_split), soma_v, soma_stim, inverse, soma_consts,
        gate, rate, cond, stim, weight_total, vox, source, route, rank, weight, potential,
    )
    received = exchange(send, devices)
    solved, partial, potential = call(
        bind(fourth_kernel, devices, stride, field_scale),
        [full, line, ((parts, 128), f32)],
        [pltpu.VMEM((comp_count, cell_dev), f32)],
    )(received, slot_target, base, vox, inverse, soma_consts, resist)

    volts, soma = call(last_kernel, [full, line])(
        solved, *split_terms(partial, n_split), soma, soma_stim, inverse, soma_consts
    )
    return volts[None], gate[None], soma.reshape(cell_dev), potential.reshape(vox_dev)


def solution(mesh):
    wide = P("split", None, "cells")
    every = P(AXES)
    in_specs = (
        wide, wide, wide, wide, wide, P("cells"), P("cells"), P(),
        every, P(AXES, None), every, every, wide, every,
    )
    out_specs = (wide, wide, P("cells"), every)
    return jax.shard_map(
        per_device, mesh=mesh, in_specs=in_specs, out_specs=out_specs, check_vma=False
    )
```

```python
import jax
import jax.numpy as jnp
from jax import lax
from jax.experimental import pallas as pl
from jax.experimental.pallas import tpu as pltpu
from jax.sharding import PartitionSpec as P

SUB = 2
CAP = 32
LOW = 512
STEP = 512

membrane_diag = 4.0
soma_diag = 8.0
reversal = -1.0
ephaptic = 0.5

f32 = jnp.float32
bf16 = jnp.bfloat16
AXES = ("cells", "split")
VMEM_BYTES = 48 * 2**20
LANES = (((1,), (1,)), ((), ()))


def halves(x):
    high = x.astype(bf16)
    return high, (x - high.astype(f32)).astype(bf16)


def hits(row, size):
    rows = lax.broadcasted_iota(jnp.int16, (size, row.shape[1]), 0)
    return rows == row.astype(jnp.int16)


def chosen(mask, row):
    return jnp.where(mask, row, jnp.zeros((), bf16))


def hot(row, size):
    return jnp.where(hits(row, size), jnp.ones((), bf16), jnp.zeros((), bf16))


def comp_digits(index, cell_dev, comp_count):
    chunks = cell_dev // LOW
    low = index % LOW
    chunk = (index // LOW) % chunks
    return chunk * comp_count + index // cell_dev, low


def write_inverse(axial, branch, inverse_ref, soma_ref):
    branches, n = axial.shape
    lanes = 128
    index = lax.broadcasted_iota(jnp.int32, (lanes, n), 0)
    table = jnp.zeros((lanes, n), f32)
    for b in range(branches):
        mine = (index == n + b) | ((index < n) | (index >= n + branches)) & (branch == b)
        table = jnp.where(mine, axial[b : b + 1, :], table)
    table = jnp.concatenate([table, jnp.zeros((lanes, lanes - n), f32)], axis=1).T
    row = [table[i : i + 1, :] for i in range(n)]
    lane = lax.broadcasted_iota(jnp.int32, (1, lanes), 1)
    pivot = [None] * n
    ratio = [None] * n
    pivot[n - 1] = membrane_diag + row[n - 1]
    ratio[n - 1] = row[n - 1] / pivot[n - 1]
    for i in range(n - 2, -1, -1):
        pivot[i] = membrane_diag + row[i] + row[i + 1] - row[i + 1] * ratio[i + 1]
        ratio[i] = row[i] / pivot[i]
    upper = [None] * n
    upper[n - 1] = jnp.where(lane == n - 1, 1.0, 0.0)
    for i in range(n - 2, -1, -1):
        upper[i] = jnp.where(lane == i, 1.0, 0.0) + ratio[i + 1] * upper[i + 1]
    result = upper[0] / pivot[0]
    inverse_ref[0:1, :] = result
    for i in range(1, n):
        result = upper[i] / pivot[i] + ratio[i] * result
        inverse_ref[i : i + 1, :] = result
    each = (lane >= n) & (lane < n + branches)
    total = soma_diag + jnp.sum(jnp.where(each, row[0], 0.0), axis=1, keepdims=True)
    shared = jnp.sum(jnp.where(each, row[0] * ratio[0], 0.0), axis=1, keepdims=True)
    soma_ref[0:1, :] = jnp.broadcast_to(total - shared, (1, lanes))
    soma_ref[1:2, :] = jnp.broadcast_to(row[0][:, 0:1], (1, lanes))


def membrane(volts, gating, rate, cond):
    settle = jax.nn.sigmoid(2.0 * volts)
    gating = settle + (gating - settle) * jnp.exp(-rate * (1.0 + volts * volts))
    return gating, cond * gating * (volts - reversal)


def fill_table(table_ref, volts, comp_count, cell_dev):
    chunks = cell_dev // LOW
    high, low = halves(volts)
    for j in range(chunks):
        at = j * comp_count
        table_ref[at : at + comp_count, :] = high[:, j * LOW : (j + 1) * LOW]
        at += chunks * comp_count
        table_ref[at : at + comp_count, :] = low[:, j * LOW : (j + 1) * LOW]


def pick_rows(table_ref, source, comp_count, cell_dev):
    size = table_ref.shape[0] // 2
    pieces = []
    for at in range(0, source.shape[1], STEP):
        high, low = comp_digits(source[:, at : at + STEP], cell_dev, comp_count)
        found = jnp.dot(table_ref[...], hot(low, LOW), preferred_element_type=f32)
        rows = lax.broadcasted_iota(jnp.int32, (size, STEP), 0)
        both = jnp.where(rows == high, found[:size] + found[size:], 0.0)
        pieces.append(jnp.sum(both, axis=0, keepdims=True))
    return jnp.concatenate(pieces, axis=1)


def put_voxels(send_ref, vox, current, devices, stride):
    block_count = vox.shape[0]
    block_size = current.shape[0] // block_count
    owners, voxels = [], []
    for k in range(block_count):
        index = vox[k : k + 1, :]
        rows = slice(k * block_size, (k + 1) * block_size)
        high, low = halves(jnp.sum(current[rows], axis=0, keepdims=True))
        mask = hits(index // LOW, devices)
        owners.append(jnp.concatenate([chosen(mask, high), chosen(mask, low)], axis=0))
        voxels.append(hot(index % LOW, LOW))
    sums = lax.dot_general(
        jnp.concatenate(owners, axis=1),
        jnp.concatenate(voxels, axis=1),
        LANES,
        preferred_element_type=f32,
    )
    sums = sums[:devices] + sums[devices:]
    for j in range(LOW // 128):
        send_ref[pl.ds(j, devices, stride=stride), :] = sums[:, j * 128 : (j + 1) * 128]


def slot_rows(values, dest_hot, rank_mask):
    parts = []
    for value in values:
        high, low = halves(value)
        parts += [chosen(rank_mask, high), chosen(rank_mask, low)]
    laid = lax.dot_general(
        jnp.concatenate(parts, axis=0), dest_hot, LANES, preferred_element_type=f32
    )
    return [
        laid[(2 * q) * CAP : (2 * q + 1) * CAP] + laid[(2 * q + 1) * CAP : (2 * q + 2) * CAP]
        for q in range(len(values))
    ]


def first_kernel(
    devices, stride,
    volts_hbm, rate_hbm, cond_hbm, stim_hbm, vox_hbm, source_hbm, route_hbm, weight_hbm,
    soma_v_hbm, soma_stim_hbm, resist_hbm, gate_hbm, target_hbm, axial_hbm,
    volts_ref, rate_ref, cond_ref, stim_ref, vox_ref, source_ref, route_ref, weight_ref,
    soma_v_ref, soma_stim_ref, resist_ref,
    send_ref, rank_ref, gate_out, current_out, inverse_ref, soma_ref,
    gate_ref, target_ref, axial_ref, table_ref, sems,
):
    pairs = [
        (axial_hbm, axial_ref), (route_hbm, route_ref), (volts_hbm, volts_ref),
        (source_hbm, source_ref), (target_hbm, target_ref), (weight_hbm, weight_ref),
        (gate_hbm, gate_ref), (rate_hbm, rate_ref), (cond_hbm, cond_ref), (vox_hbm, vox_ref),
        (stim_hbm, stim_ref), (soma_v_hbm, soma_v_ref), (soma_stim_hbm, soma_stim_ref),
        (resist_hbm, resist_ref),
    ]
    copies = [pltpu.make_async_copy(a, b, sems.at[i]) for i, (a, b) in enumerate(pairs)]
    for copy in copies:
        copy.start()
    comp_count, cell_dev = volts_ref.shape
    rows = source_ref.shape[1]
    copies[0].wait()
    write_inverse(axial_ref[...], lax.axis_index("split"), inverse_ref, soma_ref)
    span = 256
    earlier = jnp.where(
        lax.broadcasted_iota(jnp.int32, (span, span), 0)
        < lax.broadcasted_iota(jnp.int32, (span, span), 1),
        1.0, 0.0,
    ).astype(bf16)
    before = jnp.zeros((devices, 1), f32)
    ranks, dests = [], []
    copies[1].wait()
    for at in range(0, rows, span):
        dest = hot(route_ref[:, at : at + span], devices)
        count = jnp.dot(dest, earlier, preferred_element_type=f32) + before
        full = dest.astype(f32)
        ranks.append(jnp.sum(full * count, axis=0, keepdims=True))
        before = count[:, span - 1 : span] + full[:, span - 1 : span]
        dests.append(dest)
    rank = jnp.concatenate(ranks, axis=1).astype(jnp.int32)
    rank_ref[...] = rank
    dest_hot = jnp.concatenate(dests, axis=1)
    for copy in copies[2:6]:
        copy.wait()
    volts = volts_ref[...]
    fill_table(table_ref, volts, comp_count, cell_dev)
    weight = weight_ref[...]
    sent = weight * pick_rows(table_ref, source_ref[...], comp_count, cell_dev)
    slots = slot_rows([target_ref[...].astype(f32), weight, sent], dest_hot, hits(rank, CAP))
    slots.append(jnp.zeros((128 - 3 * CAP, devices), f32))
    send_ref[pl.ds(LOW // 128, devices, stride=stride), :] = jnp.concatenate(slots, axis=0).T
    for copy in copies[6:10]:
        copy.wait()
    gating, current = membrane(volts, gate_ref[...], rate_ref[...], cond_ref[...])
    gate_out[...] = gating
    current_out[...] = current
    put_voxels(send_ref, vox_ref[...], current, devices, stride)
    for copy in copies[10:]:
        copy.wait()


def wide(slots):
    return jnp.concatenate([slots[k : k + 1] for k in range(slots.shape[0])], axis=1)


def add_heads(values, target, cell_dev):
    size = cell_dev // 128
    cell = target % cell_dev
    high, low = halves(values)
    mask = hits(cell // 128, size)
    left = jnp.concatenate([chosen(mask, high), chosen(mask, low)], axis=0)
    laid = lax.dot_general(left, hot(cell % 128, 128), LANES, preferred_element_type=f32)
    return wide(laid[:size] + laid[size:])


def add_slots(values, target, comp_count, cell_dev):
    size = cell_dev // LOW * comp_count
    row, column = comp_digits(target, cell_dev, comp_count)
    high, low = halves(values)
    mask = hits(row, size)
    left = jnp.concatenate([chosen(mask, high), chosen(mask, low)], axis=0)
    laid = lax.dot_general(left, hot(column, LOW), LANES, preferred_element_type=f32)
    return as_cells(laid[:size] + laid[size:], comp_count)


def as_cells(total, comp_count):
    chunks = total.shape[0] // comp_count
    return jnp.concatenate(
        [total[j * comp_count : (j + 1) * comp_count] for j in range(chunks)], axis=1
    )


def head_term(inverse_ref, rhs):
    return jnp.sum(inverse_ref[:, 0:1] * rhs, axis=0, keepdims=True)


def second_kernel(
    devices, stride, field_scale,
    recv_ref, volts_ref, stim_ref, current_ref, inverse_ref, soma_ref, resist_ref,
    base_ref, partial_ref, target_ref, weight_ref, factor_ref, gap_ref, potential_ref,
    table_ref,
):
    comp_count, cell_dev = volts_ref.shape
    slots = recv_ref[pl.ds(LOW // 128, devices, stride=stride), :].T
    target = wide(slots[:CAP].astype(jnp.int32))
    target_ref[...] = target
    weight = wide(slots[CAP : 2 * CAP])
    weight_ref[...] = weight
    volts = volts_ref[...]
    base = membrane_diag * volts + stim_ref[...] - current_ref[...]
    base_ref[...] = base
    comps = lax.broadcasted_iota(jnp.int32, (comp_count, CAP * devices), 0)
    factor = jnp.sum(
        jnp.where(comps == target // cell_dev, inverse_ref[:, 0:1], 0.0),
        axis=0, keepdims=True,
    )
    factor_ref[...] = factor
    fill_table(table_ref, volts, comp_count, cell_dev)
    here = pick_rows(table_ref, target, comp_count, cell_dev)
    gap = wide(slots[2 * CAP : 3 * CAP]) - weight * here
    gap_ref[...] = gap
    first = head_term(inverse_ref, base) + add_heads(factor * gap, target, cell_dev)
    partial_ref[...] = soma_ref[1:2, 0:1] * first
    for j in range(LOW // 128):
        own = jnp.sum(recv_ref[pl.ds(j, devices, stride=stride), :], axis=0, keepdims=True)
        potential_ref[j : j + 1, :] = resist_ref[j : j + 1, :] * own * field_scale


def solve(inverse_ref, rhs):
    return jnp.dot(
        inverse_ref[:, : rhs.shape[0]], rhs, precision=lax.Precision.HIGHEST,
        preferred_element_type=f32,
    )


def solve_kernel(base_ref, target_ref, gap_ref, inverse_ref, solved_ref):
    comp_count, cell_dev = base_ref.shape
    gap_in = add_slots(gap_ref[...], target_ref[...], comp_count, cell_dev)
    solved_ref[...] = solve(inverse_ref, base_ref[...] + gap_in)


def pick_kernel(table_ref, target_ref, cells_ref, here_ref):
    comp_count, cell_dev = cells_ref.shape
    here_ref[...] = pick_rows(table_ref, target_ref[...], comp_count, cell_dev)


def next_soma(soma, stimulus, partials, total):
    partial = (partials[0] + partials[1]) + (partials[2] + partials[3])
    return (soma_diag * soma + stimulus + partial) / total


def third_kernel(
    devices, stride,
    solved_ref, p0_ref, p1_ref, p2_ref, p3_ref, soma_v_ref, soma_stim_ref,
    inverse_ref, soma_ref, gate_ref, rate_ref, cond_ref, stim_ref,
    vox_ref, source_ref, route_ref, rank_ref, weight_ref, potential_ref,
    send_ref, gate_hbm, soma_out, base_ref, table_ref,
    gate_out, sem,
):
    comp_count, cell_dev = solved_ref.shape
    soma = next_soma(
        soma_v_ref[...], soma_stim_ref[...],
        [p0_ref[...], p1_ref[...], p2_ref[...], p3_ref[...]], soma_ref[0:1, 0:1],
    )
    soma_out[...] = soma
    volts = solved_ref[...] + soma_ref[1:2, 0:1] * inverse_ref[:, 0:1] * soma
    fill_table(table_ref, volts, comp_count, cell_dev)
    gating, current = membrane(volts, gate_ref[...], rate_ref[...], cond_ref[...])
    gate_out[...] = gating
    copy = pltpu.make_async_copy(gate_out, gate_hbm, sem)
    copy.start()
    base_ref[...] = membrane_diag * volts + stim_ref[...] - current
    sent = weight_ref[...] * pick_rows(table_ref, source_ref[...], comp_count, cell_dev)
    slots = slot_rows([sent], hot(route_ref[...], devices), hits(rank_ref[...], CAP))
    slots.append(jnp.zeros((128 - CAP, devices), f32))
    parts = LOW // 128
    send_ref[pl.ds(2 * parts, devices, stride=stride), :] = jnp.concatenate(slots, axis=0).T
    put_voxels(send_ref, vox_ref[...], current, devices, stride)
    for j in range(parts):
        send_ref[pl.ds(parts + j, devices, stride=stride), :] = jnp.broadcast_to(
            potential_ref[j : j + 1, :], (devices, 128)
        )
    copy.wait()


def fourth_kernel(
    devices, stride, field_scale,
    recv_ref, here_ref, target_ref, weight_ref, factor_ref, base_ref, vox_ref,
    inverse_ref, soma_ref, resist_ref,
    rhs_ref, partial_ref, gap_ref, potential_ref,
):
    comp_count, cell_dev = base_ref.shape
    block_count = vox_ref.shape[0]
    block_size = comp_count // block_count
    parts = LOW // 128
    slots = recv_ref[pl.ds(2 * parts, devices, stride=stride), :].T
    gap = wide(slots[:CAP]) - weight_ref[...] * here_ref[...]
    gap_ref[...] = gap
    table = jnp.concatenate(
        [recv_ref[pl.ds(parts + j, devices, stride=stride), :] for j in range(parts)], axis=1
    )
    table = jnp.concatenate(halves(table), axis=0)
    looked = []
    for k in range(block_count):
        index = vox_ref[k : k + 1, :]
        found = jnp.dot(table, hot(index % LOW, LOW), preferred_element_type=f32)
        owners = lax.broadcasted_iota(jnp.int32, (devices, cell_dev), 0)
        both = jnp.where(owners == index // LOW, found[:devices] + found[devices:], 0.0)
        phi = jnp.sum(both, axis=0, keepdims=True)
        looked.append(jnp.broadcast_to(phi, (block_size, cell_dev)))
    rhs = base_ref[...] - ephaptic * jnp.concatenate(looked, axis=0)
    rhs_ref[...] = rhs
    heads = add_heads(factor_ref[...] * gap, target_ref[...], cell_dev)
    partial_ref[...] = soma_ref[1:2, 0:1] * (head_term(inverse_ref, rhs) + heads)
    for j in range(parts):
        own = jnp.sum(recv_ref[pl.ds(j, devices, stride=stride), :], axis=0, keepdims=True)
        potential_ref[j : j + 1, :] = resist_ref[j : j + 1, :] * own * field_scale


def last_kernel(
    solved_ref, p0_ref, p1_ref, p2_ref, p3_ref, soma_v_ref, soma_stim_ref,
    inverse_ref, soma_ref, volts_ref, soma_out,
):
    soma = next_soma(
        soma_v_ref[...], soma_stim_ref[...],
        [p0_ref[...], p1_ref[...], p2_ref[...], p3_ref[...]], soma_ref[0:1, 0:1],
    )
    soma_out[...] = soma
    volts_ref[...] = solved_ref[...] + soma_ref[1:2, 0:1] * inverse_ref[:, 0:1] * soma


def call(kernel, ins, outs, scratch=(), flops=0):
    space = lambda stays: pl.BlockSpec(memory_space=pltpu.HBM if stays else pltpu.VMEM)
    run = pl.pallas_call(
        kernel,
        in_specs=[space(stays) for stays in ins],
        out_specs=[space(out[2]) for out in outs],
        out_shape=[jax.ShapeDtypeStruct(out[0], out[1]) for out in outs],
        scratch_shapes=list(scratch),
        compiler_params=pltpu.CompilerParams(vmem_limit_bytes=VMEM_BYTES),
        cost_estimate=pl.CostEstimate(flops=flops, bytes_accessed=2**20, transcendentals=0),
    )

    def placed(*operands):
        return run(*[
            pltpu.with_memory_space_constraint(x, pltpu.HBM) if stays else x
            for x, stays in zip(operands, ins, strict=True)
        ])

    return placed


def bind(kernel, *sizes):
    def bound(*refs):
        kernel(*sizes, *refs)

    return bound


def exchange(send, devices):
    flat = lax.all_to_all(
        send.reshape(devices, send.size // devices), AXES, split_axis=0, concat_axis=0, tiled=True
    )
    return flat.reshape(send.shape)


def split_terms(partial, n_split):
    terms = [partial]
    for k in range(n_split - 1, 0, -1):
        pairs = [(i, (i + k) % n_split) for i in range(n_split)]
        terms.append(lax.ppermute(partial, "split", pairs))
    return terms


def per_device(
    voltage, gate_state, stimulus, gate_rate, gate_conductance, soma_voltage, soma_stimulus,
    axial_conductance, gap_source, gap_route, gap_target, gap_conductance, vox_index, field_resist,
):
    n_split = lax.axis_size("split")
    devices = lax.axis_size("cells") * n_split
    comp_count, cell_dev = voltage.shape[1:]
    rows = gap_source.shape[0]
    vox_dev = field_resist.shape[0]
    field_scale = vox_dev / (comp_count * cell_dev)
    volts, gate, stim = voltage[0], gate_state[0], stimulus[0]
    rate, cond, vox = gate_rate[0], gate_conductance[0], vox_index[0]
    source = gap_source.reshape(1, rows)
    route = gap_route.reshape(1, rows)
    target = gap_target.reshape(1, rows)
    weight = gap_conductance.reshape(1, rows)
    soma_v = soma_voltage.reshape(1, cell_dev)
    soma_stim = soma_stimulus.reshape(1, cell_dev)
    resist = field_resist.reshape(vox_dev // 128, 128)

    i32 = jnp.int32
    shape = (comp_count, cell_dev)
    full = (shape, f32, False)
    full_hbm = (shape, f32, True)
    line = ((1, cell_dev), f32, False)
    parts = vox_dev // 128
    quads = ((parts, 128), f32, False)
    table = pltpu.VMEM((2 * cell_dev // LOW * comp_count, LOW), bf16)
    field = pltpu.VMEM(shape, f32)

    row = ((1, CAP * devices), f32, False)
    row_i32 = ((1, CAP * devices), i32, False)

    stride = parts + 1
    kept = (volts, rate, cond, stim, vox, source, route, weight, soma_v, soma_stim, resist)
    used = (gate, target, axial_conductance)
    outs = call(
        bind(first_kernel, devices, stride),
        [True] * (len(kept) + len(used)),
        [(x.shape, x.dtype, False) for x in kept]
        + [
            ((devices * stride, 128), f32, False), ((1, rows), i32, False), full, full,
            ((comp_count, 128), f32, False), ((2, 128), f32, False),
        ],
        [pltpu.VMEM(x.shape, x.dtype) for x in used]
        + [table, pltpu.SemaphoreType.DMA((len(kept) + len(used),))],
    )(*kept, *used)
    volts, rate, cond, stim, vox, source, route, weight, soma_v, soma_stim, resist = outs[: len(kept)]
    send, rank, gate, current, inverse, soma_consts = outs[len(kept) :]
    received = exchange(send, devices)
    base, partial, slot_target, slot_weight, factor, gap, potential = call(
        bind(second_kernel, devices, stride, field_scale),
        [False] * 7,
        [full, line, row_i32, row, row, row, quads],
        [table],
    )(received, volts, stim, current, inverse, soma_consts, resist)
    terms = split_terms(partial, n_split)
    solve = call(solve_kernel, [False] * 4, [full], flops=3 * 10**9)
    (solved,) = solve(base, slot_target, gap, inverse)

    stride = 2 * parts + 1
    operands = (
        solved, *terms, soma_v, soma_stim, inverse, soma_consts,
        gate, rate, cond, stim, vox, source, route, rank, weight, potential,
    )
    send, gate, soma, base, volts_table = call(
        bind(third_kernel, devices, stride),
        [False] * len(operands),
        [((devices * stride, 128), f32, False), full_hbm, line, full, (table.shape, bf16, False)],
        [field, pltpu.SemaphoreType.DMA],
    )(*operands)
    received = exchange(send, devices)
    (here,) = call(pick_kernel, [False] * 3, [row], flops=3 * 10**9)(volts_table, slot_target, base)
    rhs, partial, gap, potential = call(
        bind(fourth_kernel, devices, stride, field_scale),
        [False] * 10,
        [full, line, row, quads],
    )(
        received, here, slot_target, slot_weight, factor, base, vox,
        inverse, soma_consts, resist,
    )
    terms = split_terms(partial, n_split)
    (solved,) = solve(rhs, slot_target, gap, inverse)

    operands = (solved, *terms, soma, soma_stim, inverse, soma_consts)
    volts, soma = call(
        last_kernel,
        [False] * len(operands),
        [full, line],
    )(*operands)
    return volts[None], gate[None], soma.reshape(cell_dev), potential.reshape(vox_dev)


def solution(mesh):
    wide = P("split", None, "cells")
    every = P(AXES)
    in_specs = (
        wide, wide, wide, wide, wide, P("cells"), P("cells"), P(),
        every, P(AXES, None), every, every, wide, every,
    )
    out_specs = (wide, wide, P("cells"), every)
    return jax.shard_map(
        per_device, mesh=mesh, in_specs=in_specs, out_specs=out_specs, check_vma=False
    )
```

```python
import jax
import jax.numpy as jnp
from jax import lax
from jax.experimental import pallas as pl
from jax.experimental.pallas import tpu as pltpu
from jax.sharding import PartitionSpec as P

SUB = 2
CAP = 32
LOW = 512
STEP = 4096

membrane_diag = 4.0
soma_diag = 8.0
reversal = -1.0
ephaptic = 0.5

f32 = jnp.float32
bf16 = jnp.bfloat16
AXES = ("cells", "split")
VMEM_BYTES = 48 * 2**20
LANES = (((1,), (1,)), ((), ()))


def halves(x):
    high = x.astype(bf16)
    return high, (x - high.astype(f32)).astype(bf16)


def hits(row, size):
    rows = lax.broadcasted_iota(jnp.int16, (size, row.shape[1]), 0)
    return rows == row.astype(jnp.int16)


def chosen(mask, row):
    return jnp.where(mask, row, jnp.zeros((), bf16))


def hot(row, size):
    return jnp.where(hits(row, size), jnp.ones((), bf16), jnp.zeros((), bf16))


def comp_digits(index, cell_dev, comp_count):
    chunks = cell_dev // LOW
    low = index % LOW
    chunk = (index // LOW) % chunks
    return chunk * comp_count + index // cell_dev, low


def write_inverse(axial, branch, inverse_ref, soma_ref):
    branches, n = axial.shape
    lanes = 128
    index = lax.broadcasted_iota(jnp.int32, (lanes, n), 0)
    table = jnp.zeros((lanes, n), f32)
    for b in range(branches):
        mine = (index == n + b) | ((index < n) | (index >= n + branches)) & (branch == b)
        table = jnp.where(mine, axial[b : b + 1, :], table)
    table = jnp.concatenate([table, jnp.zeros((lanes, lanes - n), f32)], axis=1).T
    row = [table[i : i + 1, :] for i in range(n)]
    lane = lax.broadcasted_iota(jnp.int32, (1, lanes), 1)
    pivot = [None] * n
    ratio = [None] * n
    pivot[n - 1] = membrane_diag + row[n - 1]
    ratio[n - 1] = row[n - 1] / pivot[n - 1]
    for i in range(n - 2, -1, -1):
        pivot[i] = membrane_diag + row[i] + row[i + 1] - row[i + 1] * ratio[i + 1]
        ratio[i] = row[i] / pivot[i]
    upper = [None] * n
    upper[n - 1] = jnp.where(lane == n - 1, 1.0, 0.0)
    for i in range(n - 2, -1, -1):
        upper[i] = jnp.where(lane == i, 1.0, 0.0) + ratio[i + 1] * upper[i + 1]
    result = upper[0] / pivot[0]
    inverse_ref[0:1, :] = result
    for i in range(1, n):
        result = upper[i] / pivot[i] + ratio[i] * result
        inverse_ref[i : i + 1, :] = result
    each = (lane >= n) & (lane < n + branches)
    total = soma_diag + jnp.sum(jnp.where(each, row[0], 0.0), axis=1, keepdims=True)
    shared = jnp.sum(jnp.where(each, row[0] * ratio[0], 0.0), axis=1, keepdims=True)
    soma_ref[0:1, :] = jnp.broadcast_to(total - shared, (1, lanes))
    soma_ref[1:2, :] = jnp.broadcast_to(row[0][:, 0:1], (1, lanes))


def membrane(volts, gating, rate, cond):
    settle = jax.nn.sigmoid(2.0 * volts)
    gating = settle + (gating - settle) * jnp.exp(-rate * (1.0 + volts * volts))
    return gating, cond * gating * (volts - reversal)


def fill_table(table_ref, volts, comp_count, cell_dev):
    chunks = cell_dev // LOW
    high, low = halves(volts)
    for j in range(chunks):
        at = j * comp_count
        table_ref[at : at + comp_count, :] = high[:, j * LOW : (j + 1) * LOW]
        at += chunks * comp_count
        table_ref[at : at + comp_count, :] = low[:, j * LOW : (j + 1) * LOW]


def pick_rows(table_ref, source, comp_count, cell_dev):
    size = table_ref.shape[0] // 2
    pieces = []
    for at in range(0, source.shape[1], STEP):
        high, low = comp_digits(source[:, at : at + STEP], cell_dev, comp_count)
        found = jnp.dot(table_ref[...], hot(low, LOW), preferred_element_type=f32)
        rows = lax.broadcasted_iota(jnp.int32, (size, high.shape[1]), 0)
        both = jnp.where(rows == high, found[:size] + found[size:], 0.0)
        pieces.append(jnp.sum(both, axis=0, keepdims=True))
    return jnp.concatenate(pieces, axis=1)


def put_voxels(send_ref, vox, current, devices, stride):
    block_count = vox.shape[0]
    block_size = current.shape[0] // block_count
    owners, voxels = [], []
    for k in range(block_count):
        index = vox[k : k + 1, :]
        rows = slice(k * block_size, (k + 1) * block_size)
        high, low = halves(jnp.sum(current[rows], axis=0, keepdims=True))
        mask = hits(index // LOW, devices)
        owners.append(jnp.concatenate([chosen(mask, high), chosen(mask, low)], axis=0))
        voxels.append(hot(index % LOW, LOW))
    sums = lax.dot_general(
        jnp.concatenate(owners, axis=1),
        jnp.concatenate(voxels, axis=1),
        LANES,
        preferred_element_type=f32,
    )
    sums = sums[:devices] + sums[devices:]
    for j in range(LOW // 128):
        send_ref[pl.ds(j, devices, stride=stride), :] = sums[:, j * 128 : (j + 1) * 128]


def slot_rows(values, dest_hot, rank_mask):
    parts = []
    for value in values:
        high, low = halves(value)
        parts += [chosen(rank_mask, high), chosen(rank_mask, low)]
    laid = lax.dot_general(
        jnp.concatenate(parts, axis=0), dest_hot, LANES, preferred_element_type=f32
    )
    return [
        laid[(2 * q) * CAP : (2 * q + 1) * CAP] + laid[(2 * q + 1) * CAP : (2 * q + 2) * CAP]
        for q in range(len(values))
    ]


def ranks_of(owner, devices):
    span = 256
    index = lax.broadcasted_iota(jnp.int32, (2 * span, span), 0)
    earlier = jnp.where(
        (index < lax.broadcasted_iota(jnp.int32, (2 * span, span), 1)) | (index >= span), 1.0, 0.0
    ).astype(bf16)
    before = jnp.zeros((devices, span), bf16)
    ranks, owners = [], []
    for at in range(0, owner.shape[1], span):
        one = hot(owner[:, at : at + span], devices)
        both = jnp.concatenate([one, before], axis=1)
        count = jnp.dot(both, earlier, preferred_element_type=f32)
        ranks.append(jnp.sum(one.astype(f32) * count, axis=0, keepdims=True))
        before = before + one
        owners.append(one)
    return jnp.concatenate(ranks, axis=1).astype(jnp.int32), jnp.concatenate(owners, axis=1)


def first_kernel(
    devices, stride,
    volts_hbm, rate_hbm, cond_hbm, stim_hbm, vox_hbm, source_hbm, route_hbm, weight_hbm,
    soma_v_hbm, soma_stim_hbm, resist_hbm, gate_hbm, target_hbm, axial_hbm,
    volts_ref, rate_ref, cond_ref, stim_ref, vox_ref, source_ref, route_ref, weight_ref,
    soma_v_ref, soma_stim_ref, resist_ref,
    send_ref, rank_ref, gate_out, current_out, inverse_ref, soma_ref,
    gate_ref, target_ref, axial_ref, table_ref, sems,
):
    pairs = [
        (axial_hbm, axial_ref), (route_hbm, route_ref), (volts_hbm, volts_ref),
        (source_hbm, source_ref), (target_hbm, target_ref), (weight_hbm, weight_ref),
        (gate_hbm, gate_ref), (rate_hbm, rate_ref), (cond_hbm, cond_ref), (vox_hbm, vox_ref),
        (stim_hbm, stim_ref), (soma_v_hbm, soma_v_ref), (soma_stim_hbm, soma_stim_ref),
        (resist_hbm, resist_ref),
    ]
    copies = [pltpu.make_async_copy(a, b, sems.at[i]) for i, (a, b) in enumerate(pairs)]
    for copy in copies:
        copy.start()
    comp_count, cell_dev = volts_ref.shape
    rows = source_ref.shape[1]
    copies[0].wait()
    write_inverse(axial_ref[...], lax.axis_index("split"), inverse_ref, soma_ref)
    copies[1].wait()
    rank, dest_hot = ranks_of(route_ref[...], devices)
    rank_ref[...] = rank
    for copy in copies[2:10]:
        copy.wait()
    volts = volts_ref[...]
    gating, current = membrane(volts, gate_ref[...], rate_ref[...], cond_ref[...])
    gate_out[...] = gating
    current_out[...] = current
    put_voxels(send_ref, vox_ref[...], current, devices, stride)
    fill_table(table_ref, volts, comp_count, cell_dev)
    weight = weight_ref[...]
    sent = weight * pick_rows(table_ref, source_ref[...], comp_count, cell_dev)
    slots = slot_rows([target_ref[...].astype(f32), weight, sent], dest_hot, hits(rank, CAP))
    slots.append(jnp.zeros((128 - 3 * CAP, devices), f32))
    send_ref[pl.ds(LOW // 128, devices, stride=stride), :] = jnp.concatenate(slots, axis=0).T
    for copy in copies[10:]:
        copy.wait()


def wide(slots):
    return jnp.concatenate([slots[k : k + 1] for k in range(slots.shape[0])], axis=1)


def add_heads(values, target, cell_dev):
    size = cell_dev // 128
    cell = target % cell_dev
    high, low = halves(values)
    mask = hits(cell // 128, size)
    left = jnp.concatenate([chosen(mask, high), chosen(mask, low)], axis=0)
    laid = lax.dot_general(left, hot(cell % 128, 128), LANES, preferred_element_type=f32)
    return wide(laid[:size] + laid[size:])


def add_slots(values, target, comp_count, cell_dev):
    size = cell_dev // LOW * comp_count
    row, column = comp_digits(target, cell_dev, comp_count)
    high, low = halves(values)
    mask = hits(row, size)
    left = jnp.concatenate([chosen(mask, high), chosen(mask, low)], axis=0)
    laid = lax.dot_general(left, hot(column, LOW), LANES, preferred_element_type=f32)
    return as_cells(laid[:size] + laid[size:], comp_count)


def as_cells(total, comp_count):
    chunks = total.shape[0] // comp_count
    return jnp.concatenate(
        [total[j * comp_count : (j + 1) * comp_count] for j in range(chunks)], axis=1
    )


def head_term(inverse_ref, rhs):
    return jnp.sum(inverse_ref[:, 0:1] * rhs, axis=0, keepdims=True)


def second_kernel(
    devices, stride, field_scale,
    recv_ref, volts_ref, stim_ref, current_ref, inverse_ref, soma_ref, resist_ref,
    base_ref, partial_ref, target_ref, weight_ref, factor_ref, gap_ref, potential_ref,
    table_ref,
):
    comp_count, cell_dev = volts_ref.shape
    slots = recv_ref[pl.ds(LOW // 128, devices, stride=stride), :].T
    target = wide(slots[:CAP].astype(jnp.int32))
    target_ref[...] = target
    weight = wide(slots[CAP : 2 * CAP])
    weight_ref[...] = weight
    volts = volts_ref[...]
    base = membrane_diag * volts + stim_ref[...] - current_ref[...]
    base_ref[...] = base
    comps = lax.broadcasted_iota(jnp.int32, (comp_count, CAP * devices), 0)
    factor = jnp.sum(
        jnp.where(comps == target // cell_dev, inverse_ref[:, 0:1], 0.0),
        axis=0, keepdims=True,
    )
    factor_ref[...] = factor
    fill_table(table_ref, volts, comp_count, cell_dev)
    here = pick_rows(table_ref, target, comp_count, cell_dev)
    gap = wide(slots[2 * CAP : 3 * CAP]) - weight * here
    gap_ref[...] = gap
    first = head_term(inverse_ref, base) + add_heads(factor * gap, target, cell_dev)
    partial_ref[...] = soma_ref[1:2, 0:1] * first
    for j in range(LOW // 128):
        own = jnp.sum(recv_ref[pl.ds(j, devices, stride=stride), :], axis=0, keepdims=True)
        potential_ref[j : j + 1, :] = resist_ref[j : j + 1, :] * own * field_scale


def solve(inverse_ref, rhs):
    return jnp.dot(
        inverse_ref[:, : rhs.shape[0]], rhs, precision=lax.Precision.HIGHEST,
        preferred_element_type=f32,
    )


def solve_kernel(base_ref, target_ref, gap_ref, inverse_ref, solved_ref):
    comp_count, cell_dev = base_ref.shape
    gap_in = add_slots(gap_ref[...], target_ref[...], comp_count, cell_dev)
    solved_ref[...] = solve(inverse_ref, base_ref[...] + gap_in)


def beside_kernel(
    devices,
    table_ref, target_ref, cells_ref, vox_ref,
    here_ref, group_ref, column_ref, within_ref, heavy_ref,
):
    comp_count, cell_dev = cells_ref.shape
    here_ref[...] = pick_rows(table_ref, target_ref[...], comp_count, cell_dev)
    block_count = vox_ref.shape[0]
    vox = jnp.concatenate([vox_ref[k : k + 1, :] for k in range(block_count)], axis=1)
    owner = vox // LOW
    rank, unused = ranks_of(owner, devices)
    over = rank >= 128
    group = jnp.where(over, devices // 2, owner // 2)
    column = jnp.where(over, rank - 128, owner % 2 * 128 + rank)
    for k in range(block_count):
        group_ref[k : k + 1, :] = group[:, k * cell_dev : (k + 1) * cell_dev]
        column_ref[k : k + 1, :] = column[:, k * cell_dev : (k + 1) * cell_dev]
    heavy_ref[...] = jnp.max(jnp.where(over, owner, -1), axis=1, keepdims=True)
    size = within_ref.shape[0]
    mask = hits(group, size)
    high, low = halves((vox % LOW).astype(f32))
    left = jnp.concatenate([chosen(mask, high), chosen(mask, low)], axis=0)
    laid = lax.dot_general(left, hot(column, 256), LANES, preferred_element_type=f32)
    within_ref[...] = (laid[:size] + laid[size:]).astype(jnp.int32)


def look_up(parts, index):
    found = jnp.zeros(index.shape, f32)
    for j, part in enumerate(parts):
        there = jnp.take_along_axis(part, index % 128, axis=1, mode="promise_in_bounds")
        found = jnp.where(index // 128 == j, there, found)
    return found


def next_soma(soma, stimulus, partials, total):
    partial = (partials[0] + partials[1]) + (partials[2] + partials[3])
    return (soma_diag * soma + stimulus + partial) / total


def third_kernel(
    devices, stride,
    solved_ref, p0_ref, p1_ref, p2_ref, p3_ref, soma_v_ref, soma_stim_ref,
    inverse_ref, soma_ref, gate_ref, rate_ref, cond_ref, stim_ref,
    vox_ref, source_ref, route_ref, rank_ref, weight_ref, potential_ref,
    send_ref, gate_hbm, soma_out, base_ref, table_ref,
    gate_out, sem,
):
    comp_count, cell_dev = solved_ref.shape
    soma = next_soma(
        soma_v_ref[...], soma_stim_ref[...],
        [p0_ref[...], p1_ref[...], p2_ref[...], p3_ref[...]], soma_ref[0:1, 0:1],
    )
    soma_out[...] = soma
    volts = solved_ref[...] + soma_ref[1:2, 0:1] * inverse_ref[:, 0:1] * soma
    fill_table(table_ref, volts, comp_count, cell_dev)
    gating, current = membrane(volts, gate_ref[...], rate_ref[...], cond_ref[...])
    gate_out[...] = gating
    copy = pltpu.make_async_copy(gate_out, gate_hbm, sem)
    copy.start()
    base_ref[...] = membrane_diag * volts + stim_ref[...] - current
    sent = weight_ref[...] * pick_rows(table_ref, source_ref[...], comp_count, cell_dev)
    slots = slot_rows([sent], hot(route_ref[...], devices), hits(rank_ref[...], CAP))
    slots.append(jnp.zeros((128 - CAP, devices), f32))
    parts = LOW // 128
    send_ref[pl.ds(2 * parts, devices, stride=stride), :] = jnp.concatenate(slots, axis=0).T
    put_voxels(send_ref, vox_ref[...], current, devices, stride)
    for j in range(parts):
        send_ref[pl.ds(parts + j, devices, stride=stride), :] = jnp.broadcast_to(
            potential_ref[j : j + 1, :], (devices, 128)
        )
    copy.wait()


def fourth_kernel(
    devices, stride, field_scale,
    recv_ref, here_ref, group_ref, column_ref, within_ref, heavy_ref,
    target_ref, weight_ref, factor_ref, base_ref, inverse_ref, soma_ref, resist_ref,
    rhs_ref, partial_ref, gap_ref, potential_ref,
):
    comp_count, cell_dev = base_ref.shape
    block_count = group_ref.shape[0]
    block_size = comp_count // block_count
    parts = LOW // 128
    slots = recv_ref[pl.ds(2 * parts, devices, stride=stride), :].T
    gap = wide(slots[:CAP]) - weight_ref[...] * here_ref[...]
    gap_ref[...] = gap
    half = devices // 2
    size = within_ref.shape[0]
    sides = []
    for side in range(2):
        owners = [
            recv_ref[pl.ds(side * stride + parts + j, half, stride=2 * stride), :]
            for j in range(parts)
        ]
        sides.append(look_up(owners, within_ref[:half, side * 128 : (side + 1) * 128]))
    heavy = lax.broadcasted_iota(jnp.int32, (devices, 128), 0) == heavy_ref[...]
    owner = []
    for j in range(parts):
        rows = recv_ref[pl.ds(parts + j, devices, stride=stride), :]
        one = jnp.sum(jnp.where(heavy, rows, 0.0), axis=0, keepdims=True)
        owner.append(jnp.broadcast_to(one, (size - half, 128)))
    rest = look_up(owner, within_ref[half:, :128])
    table = jnp.concatenate(
        [
            jnp.concatenate([sides[0], rest], axis=0),
            jnp.concatenate([sides[1], jnp.zeros_like(rest)], axis=0),
        ],
        axis=1,
    )
    table = jnp.concatenate(halves(table), axis=0)
    column = jnp.concatenate([column_ref[k : k + 1, :] for k in range(block_count)], axis=1)
    group = jnp.concatenate([group_ref[k : k + 1, :] for k in range(block_count)], axis=1)
    found = jnp.dot(table, hot(column, 256), preferred_element_type=f32)
    groups = lax.broadcasted_iota(jnp.int32, (size, group.shape[1]), 0)
    both = jnp.where(groups == group, found[:size] + found[size:], 0.0)
    phi = jnp.sum(both, axis=0, keepdims=True)
    looked = [
        jnp.broadcast_to(phi[:, k * cell_dev : (k + 1) * cell_dev], (block_size, cell_dev))
        for k in range(block_count)
    ]
    rhs = base_ref[...] - ephaptic * jnp.concatenate(looked, axis=0)
    rhs_ref[...] = rhs
    heads = add_heads(factor_ref[...] * gap, target_ref[...], cell_dev)
    partial_ref[...] = soma_ref[1:2, 0:1] * (head_term(inverse_ref, rhs) + heads)
    for j in range(parts):
        own = jnp.sum(recv_ref[pl.ds(j, devices, stride=stride), :], axis=0, keepdims=True)
        potential_ref[j : j + 1, :] = resist_ref[j : j + 1, :] * own * field_scale


def last_kernel(
    solved_ref, p0_ref, p1_ref, p2_ref, p3_ref, soma_v_ref, soma_stim_ref,
    inverse_ref, soma_ref, volts_ref, soma_out,
):
    soma = next_soma(
        soma_v_ref[...], soma_stim_ref[...],
        [p0_ref[...], p1_ref[...], p2_ref[...], p3_ref[...]], soma_ref[0:1, 0:1],
    )
    soma_out[...] = soma
    volts_ref[...] = solved_ref[...] + soma_ref[1:2, 0:1] * inverse_ref[:, 0:1] * soma


def call(kernel, ins, outs, scratch=(), flops=0):
    space = lambda stays: pl.BlockSpec(memory_space=pltpu.HBM if stays else pltpu.VMEM)
    run = pl.pallas_call(
        kernel,
        in_specs=[space(stays) for stays in ins],
        out_specs=[space(out[2]) for out in outs],
        out_shape=[jax.ShapeDtypeStruct(out[0], out[1]) for out in outs],
        scratch_shapes=list(scratch),
        compiler_params=pltpu.CompilerParams(vmem_limit_bytes=VMEM_BYTES),
        cost_estimate=pl.CostEstimate(flops=flops, bytes_accessed=2**20, transcendentals=0),
    )

    def placed(*operands):
        return run(*[
            pltpu.with_memory_space_constraint(x, pltpu.HBM) if stays else x
            for x, stays in zip(operands, ins, strict=True)
        ])

    return placed


def bind(kernel, *sizes):
    def bound(*refs):
        kernel(*sizes, *refs)

    return bound


def exchange(send, devices):
    flat = lax.all_to_all(
        send.reshape(devices, send.size // devices), AXES, split_axis=0, concat_axis=0, tiled=True
    )
    return flat.reshape(send.shape)


def split_terms(partial, n_split):
    terms = [partial]
    for k in range(n_split - 1, 0, -1):
        pairs = [(i, (i + k) % n_split) for i in range(n_split)]
        terms.append(lax.ppermute(partial, "split", pairs))
    return terms


def per_device(
    voltage, gate_state, stimulus, gate_rate, gate_conductance, soma_voltage, soma_stimulus,
    axial_conductance, gap_source, gap_route, gap_target, gap_conductance, vox_index, field_resist,
):
    n_split = lax.axis_size("split")
    devices = lax.axis_size("cells") * n_split
    comp_count, cell_dev = voltage.shape[1:]
    rows = gap_source.shape[0]
    vox_dev = field_resist.shape[0]
    field_scale = vox_dev / (comp_count * cell_dev)
    volts, gate, stim = voltage[0], gate_state[0], stimulus[0]
    rate, cond, vox = gate_rate[0], gate_conductance[0], vox_index[0]
    source = gap_source.reshape(1, rows)
    route = gap_route.reshape(1, rows)
    target = gap_target.reshape(1, rows)
    weight = gap_conductance.reshape(1, rows)
    soma_v = soma_voltage.reshape(1, cell_dev)
    soma_stim = soma_stimulus.reshape(1, cell_dev)
    resist = field_resist.reshape(vox_dev // 128, 128)

    i32 = jnp.int32
    shape = (comp_count, cell_dev)
    full = (shape, f32, False)
    full_hbm = (shape, f32, True)
    line = ((1, cell_dev), f32, False)
    parts = vox_dev // 128
    quads = ((parts, 128), f32, False)
    table = pltpu.VMEM((2 * cell_dev // LOW * comp_count, LOW), bf16)
    field = pltpu.VMEM(shape, f32)

    row = ((1, CAP * devices), f32, False)
    row_i32 = ((1, CAP * devices), i32, False)

    stride = parts + 1
    kept = (volts, rate, cond, stim, vox, source, route, weight, soma_v, soma_stim, resist)
    used = (gate, target, axial_conductance)
    outs = call(
        bind(first_kernel, devices, stride),
        [True] * (len(kept) + len(used)),
        [(x.shape, x.dtype, False) for x in kept]
        + [
            ((devices * stride, 128), f32, False), ((1, rows), i32, False), full, full,
            ((comp_count, 128), f32, False), ((2, 128), f32, False),
        ],
        [pltpu.VMEM(x.shape, x.dtype) for x in used]
        + [table, pltpu.SemaphoreType.DMA((len(kept) + len(used),))],
    )(*kept, *used)
    volts, rate, cond, stim, vox, source, route, weight, soma_v, soma_stim, resist = outs[: len(kept)]
    send, rank, gate, current, inverse, soma_consts = outs[len(kept) :]
    received = exchange(send, devices)
    base, partial, slot_target, slot_weight, factor, gap, potential = call(
        bind(second_kernel, devices, stride, field_scale),
        [False] * 7,
        [full, line, row_i32, row, row, row, quads],
        [table],
    )(received, volts, stim, current, inverse, soma_consts, resist)
    terms = split_terms(partial, n_split)
    solve = call(solve_kernel, [False] * 4, [full], flops=3 * 10**9)
    (solved,) = solve(base, slot_target, gap, inverse)

    stride = 2 * parts + 1
    operands = (
        solved, *terms, soma_v, soma_stim, inverse, soma_consts,
        gate, rate, cond, stim, vox, source, route, rank, weight, potential,
    )
    send, gate, soma, base, volts_table = call(
        bind(third_kernel, devices, stride),
        [False] * len(operands),
        [((devices * stride, 128), f32, False), full_hbm, line, full, (table.shape, bf16, False)],
        [field, pltpu.SemaphoreType.DMA],
    )(*operands)
    received = exchange(send, devices)
    groups = devices // 2 + 8
    here, group, column, within, heavy = call(
        bind(beside_kernel, devices),
        [False] * 4,
        [
            row, (vox.shape, i32, False), (vox.shape, i32, False),
            ((groups, 256), i32, False), ((1, 1), i32, False),
        ],
        flops=8 * 10**9,
    )(volts_table, slot_target, base, vox)
    rhs, partial, gap, potential = call(
        bind(fourth_kernel, devices, stride, field_scale),
        [False] * 13,
        [full, line, row, quads],
    )(
        received, here, group, column, within, heavy,
        slot_target, slot_weight, factor, base, inverse, soma_consts, resist,
    )
    terms = split_terms(partial, n_split)
    (solved,) = solve(rhs, slot_target, gap, inverse)

    operands = (solved, *terms, soma, soma_stim, inverse, soma_consts)
    volts, soma = call(
        last_kernel,
        [False] * len(operands),
        [full, line],
    )(*operands)
    return volts[None], gate[None], soma.reshape(cell_dev), potential.reshape(vox_dev)


def solution(mesh):
    wide = P("split", None, "cells")
    every = P(AXES)
    in_specs = (
        wide, wide, wide, wide, wide, P("cells"), P("cells"), P(),
        every, P(AXES, None), every, every, wide, every,
    )
    out_specs = (wide, wide, P("cells"), every)
    return jax.shard_map(
        per_device, mesh=mesh, in_specs=in_specs, out_specs=out_specs, check_vma=False
    )
```

```python
import jax
import jax.numpy as jnp
from jax import lax
from jax.experimental import pallas as pl
from jax.experimental.pallas import tpu as pltpu
from jax.sharding import PartitionSpec as P

SUB = 2
CAP = 32
LOW = 512

membrane_diag = 4.0
soma_diag = 8.0
reversal = -1.0
ephaptic = 0.5

f32 = jnp.float32
bf16 = jnp.bfloat16
AXES = ("cells", "split")
VMEM_BYTES = 48 * 2**20
LANES = (((1,), (1,)), ((), ()))


def halves(x):
    high = x.astype(bf16)
    return high, (x - high.astype(f32)).astype(bf16)


def hits(row, size):
    rows = lax.broadcasted_iota(jnp.int16, (size, row.shape[1]), 0)
    return rows == row.astype(jnp.int16)


def chosen(mask, row):
    return jnp.where(mask, row, jnp.zeros((), bf16))


def hot(row, size):
    return jnp.where(hits(row, size), jnp.ones((), bf16), jnp.zeros((), bf16))


def comp_digits(index, cell_dev, comp_count):
    chunks = cell_dev // LOW
    low = index % LOW
    chunk = (index // LOW) % chunks
    return chunk * comp_count + index // cell_dev, low


def write_inverse(axial, branch, inverse_ref, soma_ref):
    branches, n = axial.shape
    lanes = 128
    index = lax.broadcasted_iota(jnp.int32, (lanes, n), 0)
    table = jnp.zeros((lanes, n), f32)
    for b in range(branches):
        mine = (index == n + b) | ((index < n) | (index >= n + branches)) & (branch == b)
        table = jnp.where(mine, axial[b : b + 1, :], table)
    table = jnp.concatenate([table, jnp.zeros((lanes, lanes - n), f32)], axis=1).T
    row = [table[i : i + 1, :] for i in range(n)]
    lane = lax.broadcasted_iota(jnp.int32, (1, lanes), 1)
    pivot = [None] * n
    ratio = [None] * n
    pivot[n - 1] = membrane_diag + row[n - 1]
    ratio[n - 1] = row[n - 1] / pivot[n - 1]
    for i in range(n - 2, -1, -1):
        pivot[i] = membrane_diag + row[i] + row[i + 1] - row[i + 1] * ratio[i + 1]
        ratio[i] = row[i] / pivot[i]
    upper = [None] * n
    upper[n - 1] = jnp.where(lane == n - 1, 1.0, 0.0)
    for i in range(n - 2, -1, -1):
        upper[i] = jnp.where(lane == i, 1.0, 0.0) + ratio[i + 1] * upper[i + 1]
    result = upper[0] / pivot[0]
    inverse_ref[0:1, :] = result
    for i in range(1, n):
        result = upper[i] / pivot[i] + ratio[i] * result
        inverse_ref[i : i + 1, :] = result
    each = (lane >= n) & (lane < n + branches)
    total = soma_diag + jnp.sum(jnp.where(each, row[0], 0.0), axis=1, keepdims=True)
    shared = jnp.sum(jnp.where(each, row[0] * ratio[0], 0.0), axis=1, keepdims=True)
    soma_ref[0:1, :] = jnp.broadcast_to(total - shared, (1, lanes))
    soma_ref[1:2, :] = jnp.broadcast_to(row[0][:, 0:1], (1, lanes))


def membrane(volts, gating, rate, cond):
    settle = jax.nn.sigmoid(2.0 * volts)
    gating = settle + (gating - settle) * jnp.exp(-rate * (1.0 + volts * volts))
    return gating, cond * gating * (volts - reversal)


def fill_table(table_ref, volts, comp_count, cell_dev):
    chunks = cell_dev // LOW
    high, low = halves(volts)
    for j in range(chunks):
        at = j * comp_count
        table_ref[at : at + comp_count, :] = high[:, j * LOW : (j + 1) * LOW]
        at += chunks * comp_count
        table_ref[at : at + comp_count, :] = low[:, j * LOW : (j + 1) * LOW]


def pick_rows(table_ref, source, comp_count, cell_dev):
    high, low = comp_digits(source, cell_dev, comp_count)
    return pick_hot(table_ref, high, hot(low, LOW))


def pick_hot(table_ref, high, low_hot):
    size = table_ref.shape[0] // 2
    found = jnp.dot(table_ref[...], low_hot, preferred_element_type=f32)
    rows = lax.broadcasted_iota(jnp.int32, (size, high.shape[1]), 0)
    both = jnp.where(rows == high, found[:size] + found[size:], 0.0)
    return jnp.sum(both, axis=0, keepdims=True)


def block_sums(current, block_count):
    size = current.shape[0] // block_count
    return jnp.concatenate(
        [
            jnp.sum(current[k * size : (k + 1) * size], axis=0, keepdims=True)
            for k in range(block_count)
        ],
        axis=0,
    )


def half_sums(vox, blocks, devices, half):
    owners, voxels = [], []
    for k in range(vox.shape[0]):
        index = vox[k : k + 1, :]
        high, low = halves(blocks[k : k + 1, :])
        mask = hits(index // LOW, devices)
        owners.append(jnp.concatenate([chosen(mask, high), chosen(mask, low)], axis=0))
        voxels.append(hot(index % LOW - half * (LOW // 2), LOW // 2))
    sums = lax.dot_general(
        jnp.concatenate(owners, axis=1),
        jnp.concatenate(voxels, axis=1),
        LANES,
        preferred_element_type=f32,
    )
    return sums[:devices] + sums[devices:]


def core():
    return lax.axis_index("cells") % 2


def put_rows(send_ref, first, values, devices, stride):
    for j in range(values.shape[1] // 128):
        send_ref[pl.ds(first + j, devices, stride=stride), :] = values[:, j * 128 : (j + 1) * 128]


def own_potential(potential_ref, recv_ref, resist_ref, devices, stride, n_split, field_scale):
    source = lax.broadcasted_iota(jnp.int32, (devices, 128), 0)
    odd = (source // n_split) % 2 == 1
    rows = LOW // 256
    for j in range(rows):
        each = recv_ref[pl.ds(j, devices, stride=stride), :]
        for half in range(2):
            mine = jnp.where(odd if half else ~odd, each, 0.0)
            own = jnp.sum(mine, axis=0, keepdims=True)
            at = half * rows + j
            potential_ref[at : at + 1, :] = resist_ref[at : at + 1, :] * own * field_scale


def slot_rows(values, dest_hot, rank_mask):
    parts = []
    for value in values:
        high, low = halves(value)
        parts += [chosen(rank_mask, high), chosen(rank_mask, low)]
    laid = lax.dot_general(
        jnp.concatenate(parts, axis=0), dest_hot, LANES, preferred_element_type=f32
    )
    return [
        laid[(2 * q) * CAP : (2 * q + 1) * CAP] + laid[(2 * q + 1) * CAP : (2 * q + 2) * CAP]
        for q in range(len(values))
    ]


def ranks_of(owner, devices):
    span = 256
    index = lax.broadcasted_iota(jnp.int32, (2 * span, span), 0)
    earlier = jnp.where(
        (index < lax.broadcasted_iota(jnp.int32, (2 * span, span), 1)) | (index >= span), 1.0, 0.0
    ).astype(bf16)
    before = jnp.zeros((devices, span), bf16)
    ranks, owners = [], []
    for at in range(0, owner.shape[1], span):
        one = hot(owner[:, at : at + span], devices)
        both = jnp.concatenate([one, before], axis=1)
        count = jnp.dot(both, earlier, preferred_element_type=f32)
        ranks.append(jnp.sum(one.astype(f32) * count, axis=0, keepdims=True))
        before = before + one
        owners.append(one)
    return jnp.concatenate(ranks, axis=1).astype(jnp.int32), jnp.concatenate(owners, axis=1)


def first_kernel(
    devices,
    volts_hbm, rate_hbm, cond_hbm, stim_hbm, vox_hbm, source_hbm, route_hbm, weight_hbm,
    target_hbm, soma_v_hbm, soma_stim_hbm, resist_hbm, gate_hbm, axial_hbm,
    volts_ref, rate_ref, cond_ref, stim_ref, vox_ref, source_ref, route_ref, weight_ref,
    target_ref, soma_v_ref, soma_stim_ref, resist_ref,
    rank_ref, gate_out, base_ref, blocks_ref, inverse_ref, soma_ref, other_ref,
    gate_ref, axial_ref, sems,
):
    pairs = [
        (axial_hbm, axial_ref), (route_hbm, route_ref), (volts_hbm, volts_ref),
        (gate_hbm, gate_ref), (rate_hbm, rate_ref), (cond_hbm, cond_ref), (vox_hbm, vox_ref),
        (stim_hbm, stim_ref), (source_hbm, source_ref), (target_hbm, target_ref),
        (weight_hbm, weight_ref), (soma_v_hbm, soma_v_ref), (soma_stim_hbm, soma_stim_ref),
        (resist_hbm, resist_ref),
    ]
    copies = [pltpu.make_async_copy(a, b, sems.at[i]) for i, (a, b) in enumerate(pairs)]
    for copy in copies:
        copy.start()
    copies[0].wait()
    write_inverse(axial_ref[...], lax.axis_index("split"), inverse_ref, soma_ref)
    copies[1].wait()
    rank_ref[...], unused = ranks_of(route_ref[...], devices)
    for copy in copies[2:8]:
        copy.wait()
    volts = volts_ref[...]
    gating, current = membrane(volts, gate_ref[...], rate_ref[...], cond_ref[...])
    gate_out[...] = gating
    base_ref[...] = membrane_diag * volts + stim_ref[...] - current
    blocks = block_sums(current, vox_ref.shape[0])
    blocks_ref[...] = blocks
    other_ref[...] = half_sums(vox_ref[...], blocks, devices, 1 - core())
    for copy in copies[8:]:
        copy.wait()


def first_rows_kernel(
    devices,
    vox_ref, blocks_ref, volts_ref, source_ref, route_ref, target_ref, weight_ref, rank_ref,
    own_ref, rows_ref, table_ref,
):
    comp_count, cell_dev = volts_ref.shape
    own_ref[...] = half_sums(vox_ref[...], blocks_ref[...], devices, core())
    fill_table(table_ref, volts_ref[...], comp_count, cell_dev)
    weight = weight_ref[...]
    sent = weight * pick_rows(table_ref, source_ref[...], comp_count, cell_dev)
    values = [target_ref[...].astype(f32), weight, sent]
    slots = slot_rows(values, hot(route_ref[...], devices), hits(rank_ref[...], CAP))
    slots.append(jnp.zeros((128 - 3 * CAP, devices), f32))
    rows_ref[...] = jnp.concatenate(slots, axis=0).T


def first_send_kernel(devices, stride, own_ref, other_ref, rows_ref, send_ref):
    put_rows(send_ref, 0, own_ref[...] + other_ref[...], devices, stride)
    put_rows(send_ref, stride - 1, rows_ref[...], devices, stride)


def wide(slots):
    return jnp.concatenate([slots[k : k + 1] for k in range(slots.shape[0])], axis=1)


def add_heads(values, target, cell_dev):
    size = cell_dev // 128
    cell = target % cell_dev
    high, low = halves(values)
    mask = hits(cell // 128, size)
    left = jnp.concatenate([chosen(mask, high), chosen(mask, low)], axis=0)
    laid = lax.dot_general(left, hot(cell % 128, 128), LANES, preferred_element_type=f32)
    return wide(laid[:size] + laid[size:])


def add_slots(values, target, comp_count, cell_dev):
    size = cell_dev // LOW * comp_count
    row, column = comp_digits(target, cell_dev, comp_count)
    high, low = halves(values)
    mask = hits(row, size)
    left = jnp.concatenate([chosen(mask, high), chosen(mask, low)], axis=0)
    laid = lax.dot_general(left, hot(column, LOW), LANES, preferred_element_type=f32)
    return as_cells(laid[:size] + laid[size:], comp_count)


def as_cells(total, comp_count):
    chunks = total.shape[0] // comp_count
    return jnp.concatenate(
        [total[j * comp_count : (j + 1) * comp_count] for j in range(chunks)], axis=1
    )


def head_term(inverse_ref, rhs):
    return jnp.sum(inverse_ref[:, 0:1] * rhs, axis=0, keepdims=True)


def second_kernel(
    devices, stride, n_split, field_scale,
    recv_ref, base_ref, table_ref, inverse_ref, soma_ref, resist_ref,
    partial_ref, target_ref, weight_ref, factor_ref, gap_ref, potential_ref,
):
    comp_count, cell_dev = base_ref.shape
    slots = recv_ref[pl.ds(stride - 1, devices, stride=stride), :].T
    target = wide(slots[:CAP].astype(jnp.int32))
    target_ref[...] = target
    weight = wide(slots[CAP : 2 * CAP])
    weight_ref[...] = weight
    comps = lax.broadcasted_iota(jnp.int32, (comp_count, CAP * devices), 0)
    factor = jnp.sum(
        jnp.where(comps == target // cell_dev, inverse_ref[:, 0:1], 0.0),
        axis=0, keepdims=True,
    )
    factor_ref[...] = factor
    here = pick_rows(table_ref, target, comp_count, cell_dev)
    gap = wide(slots[2 * CAP : 3 * CAP]) - weight * here
    gap_ref[...] = gap
    first = head_term(inverse_ref, base_ref[...]) + add_heads(factor * gap, target, cell_dev)
    partial_ref[...] = soma_ref[1:2, 0:1] * first
    own_potential(potential_ref, recv_ref, resist_ref, devices, stride, n_split, field_scale)


def solve(inverse_ref, rhs):
    return jnp.dot(
        inverse_ref[:, : rhs.shape[0]], rhs, precision=lax.Precision.HIGHEST,
        preferred_element_type=f32,
    )


def solve_kernel(base_ref, target_ref, gap_ref, inverse_ref, solved_ref):
    comp_count, cell_dev = base_ref.shape
    gap_in = add_slots(gap_ref[...], target_ref[...], comp_count, cell_dev)
    solved_ref[...] = solve(inverse_ref, base_ref[...] + gap_in)


def beside_kernel(
    devices,
    table_ref, target_ref, cells_ref, vox_ref,
    here_ref, group_ref, column_ref, within_ref, heavy_ref,
):
    comp_count, cell_dev = cells_ref.shape
    here_ref[...] = pick_rows(table_ref, target_ref[...], comp_count, cell_dev)
    block_count = vox_ref.shape[0]
    vox = jnp.concatenate([vox_ref[k : k + 1, :] for k in range(block_count)], axis=1)
    owner = vox // LOW
    rank, unused = ranks_of(owner, devices)
    over = rank >= 128
    group = jnp.where(over, devices // 2, owner // 2)
    column = jnp.where(over, rank - 128, owner % 2 * 128 + rank)
    for k in range(block_count):
        group_ref[k : k + 1, :] = group[:, k * cell_dev : (k + 1) * cell_dev]
        column_ref[k : k + 1, :] = column[:, k * cell_dev : (k + 1) * cell_dev]
    heavy_ref[...] = jnp.max(jnp.where(over, owner, -1), axis=1, keepdims=True)
    size = within_ref.shape[0]
    mask = hits(group, size)
    high, low = halves((vox % LOW).astype(f32))
    left = jnp.concatenate([chosen(mask, high), chosen(mask, low)], axis=0)
    laid = lax.dot_general(left, hot(column, 256), LANES, preferred_element_type=f32)
    within_ref[...] = (laid[:size] + laid[size:]).astype(jnp.int32)


def look_up(parts, index):
    found = jnp.zeros(index.shape, f32)
    for j, part in enumerate(parts):
        there = jnp.take_along_axis(part, index % 128, axis=1, mode="promise_in_bounds")
        found = jnp.where(index // 128 == j, there, found)
    return found


def next_soma(soma, stimulus, partials, total):
    partial = (partials[0] + partials[1]) + (partials[2] + partials[3])
    return (soma_diag * soma + stimulus + partial) / total


def third_kernel(
    devices,
    solved_ref, p0_ref, p1_ref, p2_ref, p3_ref, soma_v_ref, soma_stim_ref,
    inverse_ref, soma_ref, gate_ref, rate_ref, cond_ref, stim_ref, vox_ref,
    gate_hbm, soma_out, base_ref, blocks_ref, volts_ref, other_ref,
    gate_out, sem,
):
    soma = next_soma(
        soma_v_ref[...], soma_stim_ref[...],
        [p0_ref[...], p1_ref[...], p2_ref[...], p3_ref[...]], soma_ref[0:1, 0:1],
    )
    soma_out[...] = soma
    volts = solved_ref[...] + soma_ref[1:2, 0:1] * inverse_ref[:, 0:1] * soma
    volts_ref[...] = volts
    gating, current = membrane(volts, gate_ref[...], rate_ref[...], cond_ref[...])
    gate_out[...] = gating
    copy = pltpu.make_async_copy(gate_out, gate_hbm, sem)
    copy.start()
    base_ref[...] = membrane_diag * volts + stim_ref[...] - current
    blocks = block_sums(current, vox_ref.shape[0])
    blocks_ref[...] = blocks
    other_ref[...] = half_sums(vox_ref[...], blocks, devices, 1 - core())
    copy.wait()


def third_rows_kernel(
    devices,
    vox_ref, blocks_ref, volts_ref, source_ref, route_ref, weight_ref, rank_ref,
    own_ref, rows_ref, table_ref,
):
    comp_count, cell_dev = volts_ref.shape
    own_ref[...] = half_sums(vox_ref[...], blocks_ref[...], devices, core())
    fill_table(table_ref, volts_ref[...], comp_count, cell_dev)
    sent = weight_ref[...] * pick_rows(table_ref, source_ref[...], comp_count, cell_dev)
    slots = slot_rows([sent], hot(route_ref[...], devices), hits(rank_ref[...], CAP))
    slots.append(jnp.zeros((128 - CAP, devices), f32))
    rows_ref[...] = jnp.concatenate(slots, axis=0).T


def third_send_kernel(
    devices, stride, own_ref, other_ref, rows_ref, potential_ref, target_ref,
    send_ref, target_out,
):
    target_out[...] = target_ref[...]
    put_rows(send_ref, 0, own_ref[...] + other_ref[...], devices, stride)
    for j in range(LOW // 128):
        each = jnp.broadcast_to(potential_ref[j : j + 1, :], (devices, 128))
        put_rows(send_ref, LOW // 256 + j, each, devices, stride)
    put_rows(send_ref, stride - 1, rows_ref[...], devices, stride)


def fourth_kernel(
    devices, stride, n_split, field_scale,
    recv_ref, here_ref, group_ref, column_ref, within_ref, heavy_ref,
    target_ref, weight_ref, factor_ref, base_ref, inverse_ref, soma_ref, resist_ref,
    rhs_ref, partial_ref, gap_ref, potential_ref,
):
    comp_count, cell_dev = base_ref.shape
    block_count = group_ref.shape[0]
    block_size = comp_count // block_count
    parts = LOW // 128
    first = LOW // 256
    slots = recv_ref[pl.ds(stride - 1, devices, stride=stride), :].T
    gap = wide(slots[:CAP]) - weight_ref[...] * here_ref[...]
    gap_ref[...] = gap
    half = devices // 2
    size = within_ref.shape[0]
    sides = []
    for side in range(2):
        owners = [
            recv_ref[pl.ds(side * stride + first + j, half, stride=2 * stride), :]
            for j in range(parts)
        ]
        sides.append(look_up(owners, within_ref[:half, side * 128 : (side + 1) * 128]))
    heavy = lax.broadcasted_iota(jnp.int32, (devices, 128), 0) == heavy_ref[...]
    owner = []
    for j in range(parts):
        rows = recv_ref[pl.ds(first + j, devices, stride=stride), :]
        one = jnp.sum(jnp.where(heavy, rows, 0.0), axis=0, keepdims=True)
        owner.append(jnp.broadcast_to(one, (size - half, 128)))
    rest = look_up(owner, within_ref[half:, :128])
    table = jnp.concatenate(
        [
            jnp.concatenate([sides[0], rest], axis=0),
            jnp.concatenate([sides[1], jnp.zeros_like(rest)], axis=0),
        ],
        axis=1,
    )
    table = jnp.concatenate(halves(table), axis=0)
    column = jnp.concatenate([column_ref[k : k + 1, :] for k in range(block_count)], axis=1)
    group = jnp.concatenate([group_ref[k : k + 1, :] for k in range(block_count)], axis=1)
    found = jnp.dot(table, hot(column, 256), preferred_element_type=f32)
    groups = lax.broadcasted_iota(jnp.int32, (size, group.shape[1]), 0)
    both = jnp.where(groups == group, found[:size] + found[size:], 0.0)
    phi = jnp.sum(both, axis=0, keepdims=True)
    looked = [
        jnp.broadcast_to(phi[:, k * cell_dev : (k + 1) * cell_dev], (block_size, cell_dev))
        for k in range(block_count)
    ]
    rhs = base_ref[...] - ephaptic * jnp.concatenate(looked, axis=0)
    rhs_ref[...] = rhs
    heads = add_heads(factor_ref[...] * gap, target_ref[...], cell_dev)
    partial_ref[...] = soma_ref[1:2, 0:1] * (head_term(inverse_ref, rhs) + heads)
    own_potential(potential_ref, recv_ref, resist_ref, devices, stride, n_split, field_scale)


def last_kernel(
    solved_ref, p0_ref, p1_ref, p2_ref, p3_ref, soma_v_ref, soma_stim_ref,
    inverse_ref, soma_ref, volts_ref, soma_out,
):
    soma = next_soma(
        soma_v_ref[...], soma_stim_ref[...],
        [p0_ref[...], p1_ref[...], p2_ref[...], p3_ref[...]], soma_ref[0:1, 0:1],
    )
    soma_out[...] = soma
    volts_ref[...] = solved_ref[...] + soma_ref[1:2, 0:1] * inverse_ref[:, 0:1] * soma


def call(kernel, ins, outs, scratch=(), flops=0):
    space = lambda stays: pl.BlockSpec(memory_space=pltpu.HBM if stays else pltpu.VMEM)
    run = pl.pallas_call(
        kernel,
        in_specs=[space(stays) for stays in ins],
        out_specs=[space(out[2]) for out in outs],
        out_shape=[jax.ShapeDtypeStruct(out[0], out[1]) for out in outs],
        scratch_shapes=list(scratch),
        compiler_params=pltpu.CompilerParams(vmem_limit_bytes=VMEM_BYTES),
        cost_estimate=pl.CostEstimate(flops=flops, bytes_accessed=2**20, transcendentals=0),
    )

    def placed(*operands):
        return run(*[
            pltpu.with_memory_space_constraint(x, pltpu.HBM) if stays else x
            for x, stays in zip(operands, ins, strict=True)
        ])

    return placed


def bind(kernel, *sizes):
    def bound(*refs):
        kernel(*sizes, *refs)

    return bound


def exchange(send, devices):
    flat = lax.all_to_all(
        send.reshape(devices, send.size // devices), AXES, split_axis=0, concat_axis=0, tiled=True
    )
    return flat.reshape(send.shape)


def other_core(array, n_cells):
    return lax.ppermute(array, "cells", [(i, i ^ 1) for i in range(n_cells)])


def split_terms(partial, n_split):
    terms = [partial]
    for k in range(n_split - 1, 0, -1):
        pairs = [(i, (i + k) % n_split) for i in range(n_split)]
        terms.append(lax.ppermute(partial, "split", pairs))
    return terms


def per_device(
    voltage, gate_state, stimulus, gate_rate, gate_conductance, soma_voltage, soma_stimulus,
    axial_conductance, gap_source, gap_route, gap_target, gap_conductance, vox_index, field_resist,
):
    n_split = lax.axis_size("split")
    n_cells = lax.axis_size("cells")
    devices = n_cells * n_split
    comp_count, cell_dev = voltage.shape[1:]
    rows = gap_source.shape[0]
    vox_dev = field_resist.shape[0]
    field_scale = vox_dev / (comp_count * cell_dev)
    volts, gate, stim = voltage[0], gate_state[0], stimulus[0]
    rate, cond, vox = gate_rate[0], gate_conductance[0], vox_index[0]
    source = gap_source.reshape(1, rows)
    route = gap_route.reshape(1, rows)
    target = gap_target.reshape(1, rows)
    weight = gap_conductance.reshape(1, rows)
    soma_v = soma_voltage.reshape(1, cell_dev)
    soma_stim = soma_stimulus.reshape(1, cell_dev)
    resist = field_resist.reshape(vox_dev // 128, 128)

    i32 = jnp.int32
    shape = (comp_count, cell_dev)
    full = (shape, f32, False)
    full_hbm = (shape, f32, True)
    line = ((1, cell_dev), f32, False)
    parts = vox_dev // 128
    quads = ((parts, 128), f32, False)
    table = pltpu.VMEM((2 * cell_dev // LOW * comp_count, LOW), bf16)
    field = pltpu.VMEM(shape, f32)

    row = ((1, CAP * devices), f32, False)
    row_i32 = ((1, CAP * devices), i32, False)

    blocks_shape = (vox.shape, f32, False)
    sums = ((devices, vox_dev // 2), f32, False)
    gap_rows = ((devices, 128), f32, False)
    table_out = (table.shape, bf16, False)

    stride = parts // 2 + 1
    kept = (
        volts, rate, cond, stim, vox, source, route, weight, target, soma_v, soma_stim, resist,
    )
    used = (gate, axial_conductance)
    outs = call(
        bind(first_kernel, devices),
        [True] * (len(kept) + len(used)),
        [(x.shape, x.dtype, False) for x in kept]
        + [
            ((1, rows), i32, False), full, full, blocks_shape,
            ((comp_count, 128), f32, False), ((2, 128), f32, False), sums,
        ],
        [pltpu.VMEM(x.shape, x.dtype) for x in used]
        + [pltpu.SemaphoreType.DMA((len(kept) + len(used),))],
    )(*kept, *used)
    (
        volts, rate, cond, stim, vox, source, route, weight, target, soma_v, soma_stim, resist,
    ) = outs[: len(kept)]
    rank, gate, base, blocks, inverse, soma_consts, other = outs[len(kept) :]
    other = other_core(other, n_cells)
    own, slot_rows_out, volts_table = call(
        bind(first_rows_kernel, devices), [False] * 8, [sums, gap_rows, table_out], flops=4 * 10**9
    )(vox, blocks, volts, source, route, target, weight, rank)
    (send,) = call(
        bind(first_send_kernel, devices, stride), [False] * 3,
        [((devices * stride, 128), f32, False)],
    )(own, other, slot_rows_out)
    received = exchange(send, devices)
    partial, slot_target, slot_weight, factor, gap, potential = call(
        bind(second_kernel, devices, stride, n_split, field_scale),
        [False] * 6,
        [line, row_i32, row, row, row, quads],
    )(received, base, volts_table, inverse, soma_consts, resist)
    terms = split_terms(partial, n_split)
    solve = call(solve_kernel, [False] * 4, [full], flops=3 * 10**9)
    (solved,) = solve(base, slot_target, gap, inverse)

    stride = parts // 2 + parts + 1
    operands = (
        solved, *terms, soma_v, soma_stim, inverse, soma_consts, gate, rate, cond, stim, vox,
    )
    gate, soma, base, blocks, volts, other = call(
        bind(third_kernel, devices),
        [False] * len(operands),
        [full_hbm, line, full, blocks_shape, full, sums],
        [field, pltpu.SemaphoreType.DMA],
    )(*operands)
    other = other_core(other, n_cells)
    own, slot_rows_out, volts_table = call(
        bind(third_rows_kernel, devices), [False] * 7, [sums, gap_rows, table_out], flops=4 * 10**9
    )(vox, blocks, volts, source, route, weight, rank)
    send, slot_target = call(
        bind(third_send_kernel, devices, stride), [False] * 5,
        [((devices * stride, 128), f32, False), row_i32],
    )(own, other, slot_rows_out, potential, slot_target)
    received = exchange(send, devices)
    groups = devices // 2 + 16
    here, group, column, within, heavy = call(
        bind(beside_kernel, devices),
        [False] * 4,
        [
            row, (vox.shape, i32, False), (vox.shape, i32, False),
            ((groups, 256), i32, False), ((1, 1), i32, False),
        ],
        flops=8 * 10**9,
    )(volts_table, slot_target, base, vox)
    rhs, partial, gap, potential = call(
        bind(fourth_kernel, devices, stride, n_split, field_scale),
        [False] * 13,
        [full, line, row, quads],
    )(
        received, here, group, column, within, heavy,
        slot_target, slot_weight, factor, base, inverse, soma_consts, resist,
    )
    terms = split_terms(partial, n_split)
    (solved,) = solve(rhs, slot_target, gap, inverse)

    operands = (solved, *terms, soma, soma_stim, inverse, soma_consts)
    volts, soma = call(
        last_kernel,
        [False] * len(operands),
        [full, line],
    )(*operands)
    return volts[None], gate[None], soma.reshape(cell_dev), potential.reshape(vox_dev)


def solution(mesh):
    wide = P("split", None, "cells")
    every = P(AXES)
    in_specs = (
        wide, wide, wide, wide, wide, P("cells"), P("cells"), P(),
        every, P(AXES, None), every, every, wide, every,
    )
    out_specs = (wide, wide, P("cells"), every)
    return jax.shard_map(
        per_device, mesh=mesh, in_specs=in_specs, out_specs=out_specs, check_vma=False
    )
```

```python
import jax
import jax.numpy as jnp
from jax import lax
from jax.experimental import pallas as pl
from jax.experimental.pallas import tpu as pltpu
from jax.sharding import PartitionSpec as P

SUB = 2
CAP = 32
LOW = 512

membrane_diag = 4.0
soma_diag = 8.0
reversal = -1.0
ephaptic = 0.5

f32 = jnp.float32
bf16 = jnp.bfloat16
AXES = ("cells", "split")
VMEM_BYTES = 48 * 2**20
LANES = (((1,), (1,)), ((), ()))


def halves(x):
    high = x.astype(bf16)
    return high, (x - high.astype(f32)).astype(bf16)


def hits(row, size):
    rows = lax.broadcasted_iota(jnp.int16, (size, row.shape[1]), 0)
    return rows == row.astype(jnp.int16)


def chosen(mask, row):
    return jnp.where(mask, row, jnp.zeros((), bf16))


def hot(row, size):
    return jnp.where(hits(row, size), jnp.ones((), bf16), jnp.zeros((), bf16))


def comp_digits(index, cell_dev, comp_count):
    chunks = cell_dev // LOW
    low = index % LOW
    chunk = (index // LOW) % chunks
    return chunk * comp_count + index // cell_dev, low


def write_inverse(axial, branch, inverse_ref, soma_ref):
    branches, n = axial.shape
    lanes = 128
    index = lax.broadcasted_iota(jnp.int32, (lanes, n), 0)
    table = jnp.zeros((lanes, n), f32)
    for b in range(branches):
        mine = (index == n + b) | ((index < n) | (index >= n + branches)) & (branch == b)
        table = jnp.where(mine, axial[b : b + 1, :], table)
    table = jnp.concatenate([table, jnp.zeros((lanes, lanes - n), f32)], axis=1).T
    row = [table[i : i + 1, :] for i in range(n)]
    lane = lax.broadcasted_iota(jnp.int32, (1, lanes), 1)
    pivot = [None] * n
    ratio = [None] * n
    pivot[n - 1] = membrane_diag + row[n - 1]
    ratio[n - 1] = row[n - 1] / pivot[n - 1]
    for i in range(n - 2, -1, -1):
        pivot[i] = membrane_diag + row[i] + row[i + 1] - row[i + 1] * ratio[i + 1]
        ratio[i] = row[i] / pivot[i]
    upper = [None] * n
    upper[n - 1] = jnp.where(lane == n - 1, 1.0, 0.0)
    for i in range(n - 2, -1, -1):
        upper[i] = jnp.where(lane == i, 1.0, 0.0) + ratio[i + 1] * upper[i + 1]
    result = upper[0] / pivot[0]
    inverse_ref[0:1, :] = result
    for i in range(1, n):
        result = upper[i] / pivot[i] + ratio[i] * result
        inverse_ref[i : i + 1, :] = result
    each = (lane >= n) & (lane < n + branches)
    total = soma_diag + jnp.sum(jnp.where(each, row[0], 0.0), axis=1, keepdims=True)
    shared = jnp.sum(jnp.where(each, row[0] * ratio[0], 0.0), axis=1, keepdims=True)
    soma_ref[0:1, :] = jnp.broadcast_to(total - shared, (1, lanes))
    soma_ref[1:2, :] = jnp.broadcast_to(row[0][:, 0:1], (1, lanes))


def membrane(volts, gating, rate, cond):
    settle = jax.nn.sigmoid(2.0 * volts)
    gating = settle + (gating - settle) * jnp.exp(-rate * (1.0 + volts * volts))
    return gating, cond * gating * (volts - reversal)


def fill_table(table_ref, volts, comp_count, cell_dev):
    chunks = cell_dev // LOW
    high, low = halves(volts)
    for j in range(chunks):
        at = j * comp_count
        table_ref[at : at + comp_count, :] = high[:, j * LOW : (j + 1) * LOW]
        at += chunks * comp_count
        table_ref[at : at + comp_count, :] = low[:, j * LOW : (j + 1) * LOW]


def pick_rows(table_ref, source, comp_count, cell_dev):
    high, low = comp_digits(source, cell_dev, comp_count)
    return pick_hot(table_ref, high, hot(low, LOW))


def pick_hot(table_ref, high, low_hot):
    size = table_ref.shape[0] // 2
    found = jnp.dot(table_ref[...], low_hot, preferred_element_type=f32)
    rows = lax.broadcasted_iota(jnp.int32, (size, high.shape[1]), 0)
    both = jnp.where(rows == high, found[:size] + found[size:], 0.0)
    return jnp.sum(both, axis=0, keepdims=True)


def block_sums(current, block_count):
    size = current.shape[0] // block_count
    return jnp.concatenate(
        [
            jnp.sum(current[k * size : (k + 1) * size], axis=0, keepdims=True)
            for k in range(block_count)
        ],
        axis=0,
    )


def half_sums(vox, blocks, devices, half):
    owners, voxels = [], []
    for k in range(vox.shape[0]):
        index = vox[k : k + 1, :]
        high, low = halves(blocks[k : k + 1, :])
        mask = hits(index // LOW, devices)
        owners.append(jnp.concatenate([chosen(mask, high), chosen(mask, low)], axis=0))
        voxels.append(hot(index % LOW - half * (LOW // 2), LOW // 2))
    sums = lax.dot_general(
        jnp.concatenate(owners, axis=1),
        jnp.concatenate(voxels, axis=1),
        LANES,
        preferred_element_type=f32,
    )
    return sums[:devices] + sums[devices:]


def core():
    return lax.axis_index("cells") % 2


def put_rows(send_ref, first, values, devices, stride):
    for j in range(values.shape[1] // 128):
        send_ref[pl.ds(first + j, devices, stride=stride), :] = values[:, j * 128 : (j + 1) * 128]


def own_potential(potential_ref, recv_ref, resist_ref, devices, stride, n_split, field_scale):
    source = lax.broadcasted_iota(jnp.int32, (devices, 128), 0)
    odd = (source // n_split) % 2 == 1
    rows = LOW // 256
    for j in range(rows):
        each = recv_ref[pl.ds(j, devices, stride=stride), :]
        for half in range(2):
            mine = jnp.where(odd if half else ~odd, each, 0.0)
            own = jnp.sum(mine, axis=0, keepdims=True)
            at = half * rows + j
            potential_ref[at : at + 1, :] = resist_ref[at : at + 1, :] * own * field_scale


def slot_rows(values, dest_hot, rank_mask):
    parts = []
    for value in values:
        high, low = halves(value)
        parts += [chosen(rank_mask, high), chosen(rank_mask, low)]
    laid = lax.dot_general(
        jnp.concatenate(parts, axis=0), dest_hot, LANES, preferred_element_type=f32
    )
    return [
        laid[(2 * q) * CAP : (2 * q + 1) * CAP] + laid[(2 * q + 1) * CAP : (2 * q + 2) * CAP]
        for q in range(len(values))
    ]


def ranks_of(owner, devices):
    span = 256
    index = lax.broadcasted_iota(jnp.int32, (2 * span, span), 0)
    earlier = jnp.where(
        (index < lax.broadcasted_iota(jnp.int32, (2 * span, span), 1)) | (index >= span), 1.0, 0.0
    ).astype(bf16)
    before = jnp.zeros((devices, span), bf16)
    ranks, owners = [], []
    for at in range(0, owner.shape[1], span):
        one = hot(owner[:, at : at + span], devices)
        both = jnp.concatenate([one, before], axis=1)
        count = jnp.dot(both, earlier, preferred_element_type=f32)
        ranks.append(jnp.sum(one.astype(f32) * count, axis=0, keepdims=True))
        before = before + one
        owners.append(one)
    return jnp.concatenate(ranks, axis=1).astype(jnp.int32), jnp.concatenate(owners, axis=1)


def first_kernel(
    devices,
    volts_hbm, rate_hbm, cond_hbm, stim_hbm, vox_hbm, source_hbm, route_hbm, weight_hbm,
    target_hbm, soma_v_hbm, soma_stim_hbm, resist_hbm, gate_hbm, axial_hbm,
    volts_ref, rate_ref, cond_ref, stim_ref, vox_ref, source_ref, route_ref, weight_ref,
    target_ref, soma_v_ref, soma_stim_ref, resist_ref,
    rank_ref, gate_out, base_ref, blocks_ref, inverse_ref, soma_ref, other_ref,
    gate_ref, axial_ref, sems,
):
    pairs = [
        (axial_hbm, axial_ref), (route_hbm, route_ref), (volts_hbm, volts_ref),
        (gate_hbm, gate_ref), (rate_hbm, rate_ref), (cond_hbm, cond_ref), (vox_hbm, vox_ref),
        (stim_hbm, stim_ref), (source_hbm, source_ref), (target_hbm, target_ref),
        (weight_hbm, weight_ref), (soma_v_hbm, soma_v_ref), (soma_stim_hbm, soma_stim_ref),
        (resist_hbm, resist_ref),
    ]
    copies = [pltpu.make_async_copy(a, b, sems.at[i]) for i, (a, b) in enumerate(pairs)]
    for copy in copies:
        copy.start()
    copies[0].wait()
    write_inverse(axial_ref[...], lax.axis_index("split"), inverse_ref, soma_ref)
    copies[1].wait()
    rank_ref[...], unused = ranks_of(route_ref[...], devices)
    for copy in copies[2:8]:
        copy.wait()
    volts = volts_ref[...]
    gating, current = membrane(volts, gate_ref[...], rate_ref[...], cond_ref[...])
    gate_out[...] = gating
    base_ref[...] = membrane_diag * volts + stim_ref[...] - current
    blocks = block_sums(current, vox_ref.shape[0])
    blocks_ref[...] = blocks
    other_ref[...] = half_sums(vox_ref[...], blocks, devices, 1 - core())
    for copy in copies[8:]:
        copy.wait()


def first_rows_kernel(
    devices,
    vox_ref, blocks_ref, volts_ref, source_ref, route_ref, target_ref, weight_ref, rank_ref,
    own_ref, rows_ref, table_ref,
):
    comp_count, cell_dev = volts_ref.shape
    own_ref[...] = half_sums(vox_ref[...], blocks_ref[...], devices, core())
    fill_table(table_ref, volts_ref[...], comp_count, cell_dev)
    weight = weight_ref[...]
    sent = weight * pick_rows(table_ref, source_ref[...], comp_count, cell_dev)
    values = [target_ref[...].astype(f32), weight, sent]
    slots = slot_rows(values, hot(route_ref[...], devices), hits(rank_ref[...], CAP))
    slots.append(jnp.zeros((128 - 3 * CAP, devices), f32))
    rows_ref[...] = jnp.concatenate(slots, axis=0).T


def first_send_kernel(devices, stride, own_ref, other_ref, rows_ref, send_ref):
    put_rows(send_ref, 0, own_ref[...] + other_ref[...], devices, stride)
    put_rows(send_ref, stride - 1, rows_ref[...], devices, stride)


def wide(slots):
    return jnp.concatenate([slots[k : k + 1] for k in range(slots.shape[0])], axis=1)


def add_heads(values, target, cell_dev):
    size = cell_dev // 128
    cell = target % cell_dev
    high, low = halves(values)
    mask = hits(cell // 128, size)
    left = jnp.concatenate([chosen(mask, high), chosen(mask, low)], axis=0)
    laid = lax.dot_general(left, hot(cell % 128, 128), LANES, preferred_element_type=f32)
    return wide(laid[:size] + laid[size:])


def add_slots(values, target, comp_count, cell_dev):
    size = cell_dev // LOW * comp_count
    row, column = comp_digits(target, cell_dev, comp_count)
    high, low = halves(values)
    mask = hits(row, size)
    left = jnp.concatenate([chosen(mask, high), chosen(mask, low)], axis=0)
    laid = lax.dot_general(left, hot(column, LOW), LANES, preferred_element_type=f32)
    return as_cells(laid[:size] + laid[size:], comp_count)


def as_cells(total, comp_count):
    chunks = total.shape[0] // comp_count
    return jnp.concatenate(
        [total[j * comp_count : (j + 1) * comp_count] for j in range(chunks)], axis=1
    )


def head_term(inverse_ref, rhs):
    return jnp.sum(inverse_ref[:, 0:1] * rhs, axis=0, keepdims=True)


def second_kernel(
    devices, stride, n_split, field_scale,
    recv_ref, base_ref, table_ref, inverse_ref, soma_ref, resist_ref,
    partial_ref, target_ref, weight_ref, factor_ref, gap_ref, potential_ref,
):
    comp_count, cell_dev = base_ref.shape
    slots = recv_ref[pl.ds(stride - 1, devices, stride=stride), :].T
    target = wide(slots[:CAP].astype(jnp.int32))
    target_ref[...] = target
    weight = wide(slots[CAP : 2 * CAP])
    weight_ref[...] = weight
    comps = lax.broadcasted_iota(jnp.int32, (comp_count, CAP * devices), 0)
    factor = jnp.sum(
        jnp.where(comps == target // cell_dev, inverse_ref[:, 0:1], 0.0),
        axis=0, keepdims=True,
    )
    factor_ref[...] = factor
    here = pick_rows(table_ref, target, comp_count, cell_dev)
    gap = wide(slots[2 * CAP : 3 * CAP]) - weight * here
    gap_ref[...] = gap
    first = head_term(inverse_ref, base_ref[...]) + add_heads(factor * gap, target, cell_dev)
    partial_ref[...] = soma_ref[1:2, 0:1] * first
    own_potential(potential_ref, recv_ref, resist_ref, devices, stride, n_split, field_scale)


def solve(inverse_ref, rhs):
    return jnp.dot(
        inverse_ref[:, : rhs.shape[0]], rhs, precision=lax.Precision.HIGHEST,
        preferred_element_type=f32,
    )


def solve_kernel(base_ref, target_ref, gap_ref, inverse_ref, solved_ref):
    comp_count, cell_dev = base_ref.shape
    gap_in = add_slots(gap_ref[...], target_ref[...], comp_count, cell_dev)
    solved_ref[...] = solve(inverse_ref, base_ref[...] + gap_in)


def beside_kernel(
    devices,
    table_ref, target_ref, cells_ref, vox_ref,
    here_ref, group_ref, column_ref, within_ref,
):
    comp_count, cell_dev = cells_ref.shape
    here_ref[...] = pick_rows(table_ref, target_ref[...], comp_count, cell_dev)
    block_count = vox_ref.shape[0]
    vox = jnp.concatenate([vox_ref[k : k + 1, :] for k in range(block_count)], axis=1)
    owner = vox // LOW
    rank, unused = ranks_of(owner, devices)
    over = rank >= 128
    group = jnp.where(over, devices // 2, owner // 2)
    column = jnp.where(over, rank - 128, owner % 2 * 128 + rank)
    for k in range(block_count):
        group_ref[k : k + 1, :] = group[:, k * cell_dev : (k + 1) * cell_dev]
        column_ref[k : k + 1, :] = column[:, k * cell_dev : (k + 1) * cell_dev]
    heavy = jnp.max(jnp.where(over, owner, -1), axis=1, keepdims=True)
    size = within_ref.shape[0]
    mask = hits(group, size)
    high, low = halves((vox % LOW).astype(f32))
    left = jnp.concatenate([chosen(mask, high), chosen(mask, low)], axis=0)
    laid = lax.dot_general(left, hot(column, 256), LANES, preferred_element_type=f32)
    half = devices // 2
    within_ref[...] = (laid[:size] + laid[size:]).astype(jnp.int32)
    within_ref[half:, 128:] = jnp.broadcast_to(heavy, (size - half, 128))


def look_up(parts, index):
    found = jnp.zeros(index.shape, f32)
    for j, part in enumerate(parts):
        there = jnp.take_along_axis(part, index % 128, axis=1, mode="promise_in_bounds")
        found = jnp.where(index // 128 == j, there, found)
    return found


def next_soma(soma, stimulus, partials, total):
    partial = (partials[0] + partials[1]) + (partials[2] + partials[3])
    return (soma_diag * soma + stimulus + partial) / total


def third_kernel(
    devices,
    solved_ref, p0_ref, p1_ref, p2_ref, p3_ref, soma_v_ref, soma_stim_ref,
    inverse_ref, soma_ref, gate_ref, rate_ref, cond_ref, stim_ref, vox_ref,
    gate_hbm, soma_out, base_ref, blocks_ref, volts_ref, other_ref,
    gate_out, sem,
):
    soma = next_soma(
        soma_v_ref[...], soma_stim_ref[...],
        [p0_ref[...], p1_ref[...], p2_ref[...], p3_ref[...]], soma_ref[0:1, 0:1],
    )
    soma_out[...] = soma
    volts = solved_ref[...] + soma_ref[1:2, 0:1] * inverse_ref[:, 0:1] * soma
    volts_ref[...] = volts
    gating, current = membrane(volts, gate_ref[...], rate_ref[...], cond_ref[...])
    gate_out[...] = gating
    copy = pltpu.make_async_copy(gate_out, gate_hbm, sem)
    copy.start()
    base_ref[...] = membrane_diag * volts + stim_ref[...] - current
    blocks = block_sums(current, vox_ref.shape[0])
    blocks_ref[...] = blocks
    other_ref[...] = half_sums(vox_ref[...], blocks, devices, 1 - core())
    copy.wait()


def third_rows_kernel(
    devices,
    vox_ref, blocks_ref, volts_ref, source_ref, route_ref, weight_ref, rank_ref,
    own_ref, rows_ref, table_ref,
):
    comp_count, cell_dev = volts_ref.shape
    own_ref[...] = half_sums(vox_ref[...], blocks_ref[...], devices, core())
    fill_table(table_ref, volts_ref[...], comp_count, cell_dev)
    sent = weight_ref[...] * pick_rows(table_ref, source_ref[...], comp_count, cell_dev)
    slots = slot_rows([sent], hot(route_ref[...], devices), hits(rank_ref[...], CAP))
    slots.append(jnp.zeros((128 - CAP, devices), f32))
    rows_ref[...] = jnp.concatenate(slots, axis=0).T


def third_send_kernel(
    devices, stride, own_ref, other_ref, rows_ref, potential_ref, target_ref,
    send_ref, target_out,
):
    target_out[...] = target_ref[...]
    put_rows(send_ref, 0, own_ref[...] + other_ref[...], devices, stride)
    for j in range(LOW // 128):
        each = jnp.broadcast_to(potential_ref[j : j + 1, :], (devices, 128))
        put_rows(send_ref, LOW // 256 + j, each, devices, stride)
    put_rows(send_ref, stride - 1, rows_ref[...], devices, stride)


def fourth_kernel(
    devices, stride, n_split, field_scale,
    recv_ref, here_ref, group_ref, column_ref, within_ref,
    target_ref, weight_ref, factor_ref, base_ref, inverse_ref, soma_ref, resist_ref,
    rhs_ref, partial_ref, gap_ref, potential_ref,
):
    comp_count, cell_dev = base_ref.shape
    block_count = group_ref.shape[0]
    block_size = comp_count // block_count
    parts = LOW // 128
    first = LOW // 256
    slots = recv_ref[pl.ds(stride - 1, devices, stride=stride), :].T
    gap = wide(slots[:CAP]) - weight_ref[...] * here_ref[...]
    gap_ref[...] = gap
    half = devices // 2
    size = within_ref.shape[0]
    sides = []
    for side in range(2):
        owners = [
            recv_ref[pl.ds(side * stride + first + j, half, stride=2 * stride), :]
            for j in range(parts)
        ]
        sides.append(look_up(owners, within_ref[:half, side * 128 : (side + 1) * 128]))
    heavy = lax.broadcasted_iota(jnp.int32, (devices, 128), 0) == within_ref[half : half + 1, 128:129]
    owner = []
    for j in range(parts):
        rows = recv_ref[pl.ds(first + j, devices, stride=stride), :]
        one = jnp.sum(jnp.where(heavy, rows, 0.0), axis=0, keepdims=True)
        owner.append(jnp.broadcast_to(one, (size - half, 128)))
    rest = look_up(owner, within_ref[half:, :128])
    table = jnp.concatenate(
        [
            jnp.concatenate([sides[0], rest], axis=0),
            jnp.concatenate([sides[1], jnp.zeros_like(rest)], axis=0),
        ],
        axis=1,
    )
    table = jnp.concatenate(halves(table), axis=0)
    column = jnp.concatenate([column_ref[k : k + 1, :] for k in range(block_count)], axis=1)
    group = jnp.concatenate([group_ref[k : k + 1, :] for k in range(block_count)], axis=1)
    found = jnp.dot(table, hot(column, 256), preferred_element_type=f32)
    groups = lax.broadcasted_iota(jnp.int32, (size, group.shape[1]), 0)
    both = jnp.where(groups == group, found[:size] + found[size:], 0.0)
    phi = jnp.sum(both, axis=0, keepdims=True)
    looked = [
        jnp.broadcast_to(phi[:, k * cell_dev : (k + 1) * cell_dev], (block_size, cell_dev))
        for k in range(block_count)
    ]
    rhs = base_ref[...] - ephaptic * jnp.concatenate(looked, axis=0)
    rhs_ref[...] = rhs
    heads = add_heads(factor_ref[...] * gap, target_ref[...], cell_dev)
    partial_ref[...] = soma_ref[1:2, 0:1] * (head_term(inverse_ref, rhs) + heads)
    own_potential(potential_ref, recv_ref, resist_ref, devices, stride, n_split, field_scale)


def last_kernel(
    solved_ref, p0_ref, p1_ref, p2_ref, p3_ref, soma_v_ref, soma_stim_ref,
    inverse_ref, soma_ref, potential_ref, volts_ref, soma_out, potential_out,
):
    potential_out[...] = potential_ref[...]
    soma = next_soma(
        soma_v_ref[...], soma_stim_ref[...],
        [p0_ref[...], p1_ref[...], p2_ref[...], p3_ref[...]], soma_ref[0:1, 0:1],
    )
    soma_out[...] = soma
    volts_ref[...] = solved_ref[...] + soma_ref[1:2, 0:1] * inverse_ref[:, 0:1] * soma


def call(kernel, ins, outs, scratch=(), flops=0):
    space = lambda stays: pl.BlockSpec(memory_space=pltpu.HBM if stays else pltpu.VMEM)
    run = pl.pallas_call(
        kernel,
        in_specs=[space(stays) for stays in ins],
        out_specs=[space(out[2]) for out in outs],
        out_shape=[jax.ShapeDtypeStruct(out[0], out[1]) for out in outs],
        scratch_shapes=list(scratch),
        compiler_params=pltpu.CompilerParams(vmem_limit_bytes=VMEM_BYTES),
        cost_estimate=pl.CostEstimate(flops=flops, bytes_accessed=2**20, transcendentals=0),
    )

    def placed(*operands):
        return run(*[
            pltpu.with_memory_space_constraint(x, pltpu.HBM) if stays else x
            for x, stays in zip(operands, ins, strict=True)
        ])

    return placed


def bind(kernel, *sizes):
    def bound(*refs):
        kernel(*sizes, *refs)

    return bound


def exchange(send, devices):
    flat = lax.all_to_all(
        send.reshape(devices, send.size // devices), AXES, split_axis=0, concat_axis=0, tiled=True
    )
    return flat.reshape(send.shape)


def other_core(array, n_cells):
    return lax.ppermute(array, "cells", [(i, i ^ 1) for i in range(n_cells)])


def split_terms(partial, n_split):
    terms = [partial]
    for k in range(n_split - 1, 0, -1):
        pairs = [(i, (i + k) % n_split) for i in range(n_split)]
        terms.append(lax.ppermute(partial, "split", pairs))
    return terms


def per_device(
    voltage, gate_state, stimulus, gate_rate, gate_conductance, soma_voltage, soma_stimulus,
    axial_conductance, gap_source, gap_route, gap_target, gap_conductance, vox_index, field_resist,
):
    n_split = lax.axis_size("split")
    n_cells = lax.axis_size("cells")
    devices = n_cells * n_split
    comp_count, cell_dev = voltage.shape[1:]
    rows = gap_source.shape[0]
    vox_dev = field_resist.shape[0]
    field_scale = vox_dev / (comp_count * cell_dev)
    volts, gate, stim = voltage[0], gate_state[0], stimulus[0]
    rate, cond, vox = gate_rate[0], gate_conductance[0], vox_index[0]
    source = gap_source.reshape(1, rows)
    route = gap_route.reshape(1, rows)
    target = gap_target.reshape(1, rows)
    weight = gap_conductance.reshape(1, rows)
    soma_v = soma_voltage.reshape(1, cell_dev)
    soma_stim = soma_stimulus.reshape(1, cell_dev)
    resist = field_resist.reshape(vox_dev // 128, 128)

    i32 = jnp.int32
    shape = (comp_count, cell_dev)
    full = (shape, f32, False)
    full_hbm = (shape, f32, True)
    line = ((1, cell_dev), f32, False)
    parts = vox_dev // 128
    quads = ((parts, 128), f32, False)
    table = pltpu.VMEM((2 * cell_dev // LOW * comp_count, LOW), bf16)
    field = pltpu.VMEM(shape, f32)

    row = ((1, CAP * devices), f32, False)
    row_i32 = ((1, CAP * devices), i32, False)

    blocks_shape = (vox.shape, f32, False)
    sums = ((devices, vox_dev // 2), f32, False)
    gap_rows = ((devices, 128), f32, False)
    table_out = (table.shape, bf16, False)

    stride = parts // 2 + 1
    kept = (
        volts, rate, cond, stim, vox, source, route, weight, target, soma_v, soma_stim, resist,
    )
    used = (gate, axial_conductance)
    outs = call(
        bind(first_kernel, devices),
        [True] * (len(kept) + len(used)),
        [(x.shape, x.dtype, False) for x in kept]
        + [
            ((1, rows), i32, False), full, full, blocks_shape,
            ((comp_count, 128), f32, False), ((2, 128), f32, False), sums,
        ],
        [pltpu.VMEM(x.shape, x.dtype) for x in used]
        + [pltpu.SemaphoreType.DMA((len(kept) + len(used),))],
    )(*kept, *used)
    (
        volts, rate, cond, stim, vox, source, route, weight, target, soma_v, soma_stim, resist,
    ) = outs[: len(kept)]
    rank, gate, base, blocks, inverse, soma_consts, other = outs[len(kept) :]
    other = other_core(other, n_cells)
    own, slot_rows_out, volts_table = call(
        bind(first_rows_kernel, devices), [False] * 8, [sums, gap_rows, table_out], flops=4 * 10**9
    )(vox, blocks, volts, source, route, target, weight, rank)
    (send,) = call(
        bind(first_send_kernel, devices, stride), [False] * 3,
        [((devices * stride, 128), f32, False)],
    )(own, other, slot_rows_out)
    received = exchange(send, devices)
    partial, slot_target, slot_weight, factor, gap, potential = call(
        bind(second_kernel, devices, stride, n_split, field_scale),
        [False] * 6,
        [line, row_i32, row, row, row, quads],
    )(received, base, volts_table, inverse, soma_consts, resist)
    terms = split_terms(partial, n_split)
    solve = call(solve_kernel, [False] * 4, [full], flops=3 * 10**9)
    (solved,) = solve(base, slot_target, gap, inverse)

    stride = parts // 2 + parts + 1
    operands = (
        solved, *terms, soma_v, soma_stim, inverse, soma_consts, gate, rate, cond, stim, vox,
    )
    gate, soma, base, blocks, volts, other = call(
        bind(third_kernel, devices),
        [False] * len(operands),
        [full_hbm, line, full, blocks_shape, full, sums],
        [field, pltpu.SemaphoreType.DMA],
    )(*operands)
    other = other_core(other, n_cells)
    own, slot_rows_out, volts_table = call(
        bind(third_rows_kernel, devices), [False] * 7, [sums, gap_rows, table_out], flops=4 * 10**9
    )(vox, blocks, volts, source, route, weight, rank)
    send, slot_target = call(
        bind(third_send_kernel, devices, stride), [False] * 5,
        [((devices * stride, 128), f32, False), row_i32],
    )(own, other, slot_rows_out, potential, slot_target)
    received = exchange(send, devices)
    groups = devices // 2 + 16
    here, group, column, within = call(
        bind(beside_kernel, devices),
        [False] * 4,
        [
            row, (vox.shape, i32, False), (vox.shape, i32, False),
            ((groups, 256), i32, False),
        ],
        flops=8 * 10**9,
    )(volts_table, slot_target, base, vox)
    rhs, partial, gap, potential = call(
        bind(fourth_kernel, devices, stride, n_split, field_scale),
        [False] * 12,
        [full, line, row, quads],
    )(
        received, here, group, column, within,
        slot_target, slot_weight, factor, base, inverse, soma_consts, resist,
    )
    terms = split_terms(partial, n_split)
    (solved,) = solve(rhs, slot_target, gap, inverse)

    operands = (solved, *terms, soma, soma_stim, inverse, soma_consts, potential)
    volts, soma, potential = call(
        last_kernel,
        [False] * len(operands),
        [full, line, quads],
    )(*operands)
    return volts[None], gate[None], soma.reshape(cell_dev), potential.reshape(vox_dev)


def solution(mesh):
    wide = P("split", None, "cells")
    every = P(AXES)
    in_specs = (
        wide, wide, wide, wide, wide, P("cells"), P("cells"), P(),
        every, P(AXES, None), every, every, wide, every,
    )
    out_specs = (wide, wide, P("cells"), every)
    return jax.shard_map(
        per_device, mesh=mesh, in_specs=in_specs, out_specs=out_specs, check_vma=False
    )
```

```python
import jax
import jax.numpy as jnp
from jax import lax
from jax.experimental import pallas as pl
from jax.experimental.pallas import tpu as pltpu
from jax.sharding import PartitionSpec as P

SUB = 2
CAP = 32
LOW = 512

membrane_diag = 4.0
soma_diag = 8.0
reversal = -1.0
ephaptic = 0.5

f32 = jnp.float32
bf16 = jnp.bfloat16
AXES = ("cells", "split")
VMEM_BYTES = 48 * 2**20
LANES = (((1,), (1,)), ((), ()))


def halves(x):
    high = x.astype(bf16)
    return high, (x - high.astype(f32)).astype(bf16)


def hits(row, size):
    rows = lax.broadcasted_iota(jnp.int16, (size, row.shape[1]), 0)
    return rows == row.astype(jnp.int16)


def chosen(mask, row):
    return jnp.where(mask, row, jnp.zeros((), bf16))


def hot(row, size):
    return jnp.where(hits(row, size), jnp.ones((), bf16), jnp.zeros((), bf16))


def comp_digits(index, cell_dev, comp_count):
    chunks = cell_dev // LOW
    low = index % LOW
    chunk = (index // LOW) % chunks
    return chunk * comp_count + index // cell_dev, low


def write_inverse(axial, branch, inverse_ref, soma_ref):
    branches, n = axial.shape
    lanes = 128
    index = lax.broadcasted_iota(jnp.int32, (lanes, n), 0)
    table = jnp.zeros((lanes, n), f32)
    for b in range(branches):
        mine = (index == n + b) | ((index < n) | (index >= n + branches)) & (branch == b)
        table = jnp.where(mine, axial[b : b + 1, :], table)
    table = jnp.concatenate([table, jnp.zeros((lanes, lanes - n), f32)], axis=1).T
    row = [table[i : i + 1, :] for i in range(n)]
    lane = lax.broadcasted_iota(jnp.int32, (1, lanes), 1)
    pivot = [None] * n
    ratio = [None] * n
    pivot[n - 1] = membrane_diag + row[n - 1]
    ratio[n - 1] = row[n - 1] / pivot[n - 1]
    for i in range(n - 2, -1, -1):
        pivot[i] = membrane_diag + row[i] + row[i + 1] - row[i + 1] * ratio[i + 1]
        ratio[i] = row[i] / pivot[i]
    upper = [None] * n
    upper[n - 1] = jnp.where(lane == n - 1, 1.0, 0.0)
    for i in range(n - 2, -1, -1):
        upper[i] = jnp.where(lane == i, 1.0, 0.0) + ratio[i + 1] * upper[i + 1]
    result = upper[0] / pivot[0]
    inverse_ref[0:1, :] = result
    for i in range(1, n):
        result = upper[i] / pivot[i] + ratio[i] * result
        inverse_ref[i : i + 1, :] = result
    each = (lane >= n) & (lane < n + branches)
    total = soma_diag + jnp.sum(jnp.where(each, row[0], 0.0), axis=1, keepdims=True)
    shared = jnp.sum(jnp.where(each, row[0] * ratio[0], 0.0), axis=1, keepdims=True)
    soma_ref[0:1, :] = jnp.broadcast_to(total - shared, (1, lanes))
    soma_ref[1:2, :] = jnp.broadcast_to(row[0][:, 0:1], (1, lanes))


def membrane(volts, gating, rate, cond):
    settle = jax.nn.sigmoid(2.0 * volts)
    gating = settle + (gating - settle) * jnp.exp(-rate * (1.0 + volts * volts))
    return gating, cond * gating * (volts - reversal)


def fill_table(table_ref, volts, comp_count, cell_dev):
    chunks = cell_dev // LOW
    high, low = halves(volts)
    for j in range(chunks):
        at = j * comp_count
        table_ref[at : at + comp_count, :] = high[:, j * LOW : (j + 1) * LOW]
        at += chunks * comp_count
        table_ref[at : at + comp_count, :] = low[:, j * LOW : (j + 1) * LOW]


def pick_rows(table_ref, source, comp_count, cell_dev):
    high, low = comp_digits(source, cell_dev, comp_count)
    return pick_hot(table_ref, high, hot(low, LOW))


def pick_hot(table_ref, high, low_hot):
    size = table_ref.shape[0] // 2
    found = jnp.dot(table_ref[...], low_hot, preferred_element_type=f32)
    rows = lax.broadcasted_iota(jnp.int32, (size, high.shape[1]), 0)
    both = jnp.where(rows == high, found[:size] + found[size:], 0.0)
    return jnp.sum(both, axis=0, keepdims=True)


def block_sums(current, block_count):
    size = current.shape[0] // block_count
    return jnp.concatenate(
        [
            jnp.sum(current[k * size : (k + 1) * size], axis=0, keepdims=True)
            for k in range(block_count)
        ],
        axis=0,
    )


def half_sums(vox, blocks, devices, half):
    owners, voxels = [], []
    for k in range(vox.shape[0]):
        index = vox[k : k + 1, :]
        high, low = halves(blocks[k : k + 1, :])
        mask = hits(index // LOW, devices)
        owners.append(jnp.concatenate([chosen(mask, high), chosen(mask, low)], axis=0))
        voxels.append(hot(index % LOW - half * (LOW // 2), LOW // 2))
    sums = lax.dot_general(
        jnp.concatenate(owners, axis=1),
        jnp.concatenate(voxels, axis=1),
        LANES,
        preferred_element_type=f32,
    )
    return sums[:devices] + sums[devices:]


def core():
    return lax.axis_index("cells") % 2


def put_rows(send_ref, first, values, devices, stride):
    for j in range(values.shape[1] // 128):
        send_ref[pl.ds(first + j, devices, stride=stride), :] = values[:, j * 128 : (j + 1) * 128]


def own_potential(potential_ref, recv_ref, resist_ref, devices, stride, n_split, field_scale):
    source = lax.broadcasted_iota(jnp.int32, (devices, 128), 0)
    odd = (source // n_split) % 2 == 1
    rows = LOW // 256
    for j in range(rows):
        each = recv_ref[pl.ds(j, devices, stride=stride), :]
        for half in range(2):
            mine = jnp.where(odd if half else ~odd, each, 0.0)
            own = jnp.sum(mine, axis=0, keepdims=True)
            at = half * rows + j
            potential_ref[at : at + 1, :] = resist_ref[at : at + 1, :] * own * field_scale


def slot_rows(values, dest_hot, rank_mask):
    parts = []
    for value in values:
        high, low = halves(value)
        parts += [chosen(rank_mask, high), chosen(rank_mask, low)]
    laid = lax.dot_general(
        jnp.concatenate(parts, axis=0), dest_hot, LANES, preferred_element_type=f32
    )
    return [
        laid[(2 * q) * CAP : (2 * q + 1) * CAP] + laid[(2 * q + 1) * CAP : (2 * q + 2) * CAP]
        for q in range(len(values))
    ]


def ranks_of(owner, devices):
    span = 256
    index = lax.broadcasted_iota(jnp.int32, (2 * span, span), 0)
    earlier = jnp.where(
        (index < lax.broadcasted_iota(jnp.int32, (2 * span, span), 1)) | (index >= span), 1.0, 0.0
    ).astype(bf16)
    before = jnp.zeros((devices, span), bf16)
    ranks, owners = [], []
    for at in range(0, owner.shape[1], span):
        one = hot(owner[:, at : at + span], devices)
        both = jnp.concatenate([one, before], axis=1)
        count = jnp.dot(both, earlier, preferred_element_type=f32)
        ranks.append(jnp.sum(one.astype(f32) * count, axis=0, keepdims=True))
        before = before + one
        owners.append(one)
    return jnp.concatenate(ranks, axis=1).astype(jnp.int32), jnp.concatenate(owners, axis=1)


def first_kernel(
    devices,
    volts_hbm, rate_hbm, cond_hbm, stim_hbm, vox_hbm, source_hbm, route_hbm, weight_hbm,
    target_hbm, soma_v_hbm, soma_stim_hbm, resist_hbm, gate_hbm, axial_hbm,
    volts_ref, rate_ref, cond_ref, stim_ref, vox_ref, source_ref, route_ref, weight_ref,
    target_ref, soma_v_ref, soma_stim_ref, resist_ref,
    rank_ref, gate_out, base_ref, blocks_ref, inverse_ref, soma_ref, other_ref,
    gate_ref, axial_ref, sems,
):
    pairs = [
        (axial_hbm, axial_ref), (route_hbm, route_ref), (volts_hbm, volts_ref),
        (gate_hbm, gate_ref), (rate_hbm, rate_ref), (cond_hbm, cond_ref), (vox_hbm, vox_ref),
        (stim_hbm, stim_ref), (source_hbm, source_ref), (target_hbm, target_ref),
        (weight_hbm, weight_ref), (soma_v_hbm, soma_v_ref), (soma_stim_hbm, soma_stim_ref),
        (resist_hbm, resist_ref),
    ]
    copies = [pltpu.make_async_copy(a, b, sems.at[i]) for i, (a, b) in enumerate(pairs)]
    for copy in copies:
        copy.start()
    copies[0].wait()
    write_inverse(axial_ref[...], lax.axis_index("split"), inverse_ref, soma_ref)
    copies[1].wait()
    rank_ref[...], unused = ranks_of(route_ref[...], devices)
    for copy in copies[2:8]:
        copy.wait()
    volts = volts_ref[...]
    gating, current = membrane(volts, gate_ref[...], rate_ref[...], cond_ref[...])
    gate_out[...] = gating
    base_ref[...] = membrane_diag * volts + stim_ref[...] - current
    blocks = block_sums(current, vox_ref.shape[0])
    blocks_ref[...] = blocks
    other_ref[...] = half_sums(vox_ref[...], blocks, devices, 1 - core())
    for copy in copies[8:]:
        copy.wait()


def first_rows_kernel(
    devices,
    vox_ref, blocks_ref, volts_ref, source_ref, route_ref, target_ref, weight_ref, rank_ref,
    own_ref, rows_ref, table_ref,
):
    comp_count, cell_dev = volts_ref.shape
    own_ref[...] = half_sums(vox_ref[...], blocks_ref[...], devices, core())
    fill_table(table_ref, volts_ref[...], comp_count, cell_dev)
    weight = weight_ref[...]
    sent = weight * pick_rows(table_ref, source_ref[...], comp_count, cell_dev)
    values = [target_ref[...].astype(f32), weight, sent]
    slots = slot_rows(values, hot(route_ref[...], devices), hits(rank_ref[...], CAP))
    slots.append(jnp.zeros((128 - 3 * CAP, devices), f32))
    rows_ref[...] = jnp.concatenate(slots, axis=0).T


def first_send_kernel(devices, stride, own_ref, other_ref, rows_ref, send_ref):
    put_rows(send_ref, 0, own_ref[...] + other_ref[...], devices, stride)
    put_rows(send_ref, stride - 1, rows_ref[...], devices, stride)


def wide(slots):
    return jnp.concatenate([slots[k : k + 1] for k in range(slots.shape[0])], axis=1)


def add_heads(values, target, cell_dev):
    size = cell_dev // 128
    cell = target % cell_dev
    high, low = halves(values)
    mask = hits(cell // 128, size)
    left = jnp.concatenate([chosen(mask, high), chosen(mask, low)], axis=0)
    laid = lax.dot_general(left, hot(cell % 128, 128), LANES, preferred_element_type=f32)
    return wide(laid[:size] + laid[size:])


def add_slots(values, target, comp_count, cell_dev):
    size = cell_dev // LOW * comp_count
    row, column = comp_digits(target, cell_dev, comp_count)
    high, low = halves(values)
    mask = hits(row, size)
    left = jnp.concatenate([chosen(mask, high), chosen(mask, low)], axis=0)
    laid = lax.dot_general(left, hot(column, LOW), LANES, preferred_element_type=f32)
    return as_cells(laid[:size] + laid[size:], comp_count)


def as_cells(total, comp_count):
    chunks = total.shape[0] // comp_count
    return jnp.concatenate(
        [total[j * comp_count : (j + 1) * comp_count] for j in range(chunks)], axis=1
    )


def head_term(inverse_ref, rhs):
    return jnp.sum(inverse_ref[:, 0:1] * rhs, axis=0, keepdims=True)


def second_kernel(
    devices, stride, n_split, field_scale,
    recv_ref, base_ref, table_ref, inverse_ref, soma_ref, resist_ref,
    partial_ref, target_ref, weight_ref, factor_ref, gap_ref, potential_ref,
):
    comp_count, cell_dev = base_ref.shape
    slots = recv_ref[pl.ds(stride - 1, devices, stride=stride), :].T
    target = wide(slots[:CAP].astype(jnp.int32))
    target_ref[...] = target
    weight = wide(slots[CAP : 2 * CAP])
    weight_ref[...] = weight
    comps = lax.broadcasted_iota(jnp.int32, (comp_count, CAP * devices), 0)
    factor = jnp.sum(
        jnp.where(comps == target // cell_dev, inverse_ref[:, 0:1], 0.0),
        axis=0, keepdims=True,
    )
    factor_ref[...] = factor
    here = pick_rows(table_ref, target, comp_count, cell_dev)
    gap = wide(slots[2 * CAP : 3 * CAP]) - weight * here
    gap_ref[...] = gap
    first = head_term(inverse_ref, base_ref[...]) + add_heads(factor * gap, target, cell_dev)
    partial_ref[...] = soma_ref[1:2, 0:1] * first
    own_potential(potential_ref, recv_ref, resist_ref, devices, stride, n_split, field_scale)


def thirds(x):
    high = x.astype(bf16)
    rest = x - high.astype(f32)
    middle = rest.astype(bf16)
    return high, middle, (rest - middle.astype(f32)).astype(bf16)


def solve(inverse_ref, rhs):
    high, middle, low = thirds(inverse_ref[:, : rhs.shape[0]])
    left = jnp.concatenate([high, high, middle, middle, high, low], axis=1)
    high, middle, low = thirds(rhs)
    right = jnp.concatenate([high, middle, high, middle, low, high], axis=0)
    return jnp.dot(left, right, preferred_element_type=f32)


def solve_kernel(base_ref, target_ref, gap_ref, inverse_ref, solved_ref):
    comp_count, cell_dev = base_ref.shape
    gap_in = add_slots(gap_ref[...], target_ref[...], comp_count, cell_dev)
    solved_ref[...] = solve(inverse_ref, base_ref[...] + gap_in)


def beside_kernel(
    devices,
    table_ref, target_ref, cells_ref, vox_ref,
    here_ref, group_ref, column_ref, within_ref,
):
    comp_count, cell_dev = cells_ref.shape
    here_ref[...] = pick_rows(table_ref, target_ref[...], comp_count, cell_dev)
    block_count = vox_ref.shape[0]
    vox = jnp.concatenate([vox_ref[k : k + 1, :] for k in range(block_count)], axis=1)
    owner = vox // LOW
    rank, unused = ranks_of(owner, devices)
    over = rank >= 128
    group = jnp.where(over, devices // 2, owner // 2)
    column = jnp.where(over, rank - 128, owner % 2 * 128 + rank)
    for k in range(block_count):
        group_ref[k : k + 1, :] = group[:, k * cell_dev : (k + 1) * cell_dev]
        column_ref[k : k + 1, :] = column[:, k * cell_dev : (k + 1) * cell_dev]
    heavy = jnp.max(jnp.where(over, owner, -1), axis=1, keepdims=True)
    size = within_ref.shape[0]
    mask = hits(group, size)
    high, low = halves((vox % LOW).astype(f32))
    left = jnp.concatenate([chosen(mask, high), chosen(mask, low)], axis=0)
    laid = lax.dot_general(left, hot(column, 256), LANES, preferred_element_type=f32)
    half = devices // 2
    within_ref[...] = (laid[:size] + laid[size:]).astype(jnp.int32)
    within_ref[half:, 128:] = jnp.broadcast_to(heavy, (size - half, 128))


def look_up(parts, index):
    found = jnp.zeros(index.shape, f32)
    for j, part in enumerate(parts):
        there = jnp.take_along_axis(part, index % 128, axis=1, mode="promise_in_bounds")
        found = jnp.where(index // 128 == j, there, found)
    return found


def next_soma(soma, stimulus, partials, total):
    partial = (partials[0] + partials[1]) + (partials[2] + partials[3])
    return (soma_diag * soma + stimulus + partial) / total


def third_kernel(
    devices,
    solved_ref, p0_ref, p1_ref, p2_ref, p3_ref, soma_v_ref, soma_stim_ref,
    inverse_ref, soma_ref, gate_ref, rate_ref, cond_ref, stim_ref, vox_ref,
    gate_hbm, soma_out, base_ref, blocks_ref, volts_ref, other_ref,
    gate_out, sem,
):
    soma = next_soma(
        soma_v_ref[...], soma_stim_ref[...],
        [p0_ref[...], p1_ref[...], p2_ref[...], p3_ref[...]], soma_ref[0:1, 0:1],
    )
    soma_out[...] = soma
    volts = solved_ref[...] + soma_ref[1:2, 0:1] * inverse_ref[:, 0:1] * soma
    volts_ref[...] = volts
    gating, current = membrane(volts, gate_ref[...], rate_ref[...], cond_ref[...])
    gate_out[...] = gating
    copy = pltpu.make_async_copy(gate_out, gate_hbm, sem)
    copy.start()
    base_ref[...] = membrane_diag * volts + stim_ref[...] - current
    blocks = block_sums(current, vox_ref.shape[0])
    blocks_ref[...] = blocks
    other_ref[...] = half_sums(vox_ref[...], blocks, devices, 1 - core())
    copy.wait()


def third_rows_kernel(
    devices,
    vox_ref, blocks_ref, volts_ref, source_ref, route_ref, weight_ref, rank_ref,
    own_ref, rows_ref, table_ref,
):
    comp_count, cell_dev = volts_ref.shape
    own_ref[...] = half_sums(vox_ref[...], blocks_ref[...], devices, core())
    fill_table(table_ref, volts_ref[...], comp_count, cell_dev)
    sent = weight_ref[...] * pick_rows(table_ref, source_ref[...], comp_count, cell_dev)
    slots = slot_rows([sent], hot(route_ref[...], devices), hits(rank_ref[...], CAP))
    slots.append(jnp.zeros((128 - CAP, devices), f32))
    rows_ref[...] = jnp.concatenate(slots, axis=0).T


def third_send_kernel(
    devices, stride, n_split, own_ref, other_ref, rows_ref, potential_ref, target_ref,
    send_ref, target_out,
):
    target_out[...] = target_ref[...]
    put_rows(send_ref, 0, own_ref[...] + other_ref[...], devices, stride)
    rows = LOW // 256
    target = lax.broadcasted_iota(jnp.int32, (devices, 128), 0)
    odd = (target // n_split) % 2 == 1
    for j in range(rows):
        each = jnp.where(
            odd, potential_ref[rows + j : rows + j + 1, :], potential_ref[j : j + 1, :]
        )
        put_rows(send_ref, rows + j, each, devices, stride)
    put_rows(send_ref, stride - 1, rows_ref[...], devices, stride)


def fourth_half_kernel(devices, stride, recv_ref, within_ref, half_ref, within_out):
    within_out[...] = within_ref[...]
    rows = LOW // 256
    for j in range(rows):
        half_ref[j * devices : (j + 1) * devices, :] = recv_ref[
            pl.ds(rows + j, devices, stride=stride), :
        ]


def fourth_rows_kernel(
    devices, stride, n_split, field_scale,
    recv_ref, half_ref, here_ref, target_ref, weight_ref, factor_ref, base_ref,
    inverse_ref, resist_ref,
    first_ref, gap_ref, potential_ref,
):
    cell_dev = base_ref.shape[1]
    slots = recv_ref[pl.ds(stride - 1, devices, stride=stride), :].T
    gap = wide(slots[:CAP]) - weight_ref[...] * here_ref[...]
    gap_ref[...] = gap
    heads = add_heads(factor_ref[...] * gap, target_ref[...], cell_dev)
    first_ref[...] = head_term(inverse_ref, base_ref[...]) + heads
    own_potential(potential_ref, recv_ref, resist_ref, devices, stride, n_split, field_scale)


def fourth_kernel(
    devices,
    half_ref, other_ref, group_ref, column_ref, within_ref,
    base_ref, first_ref, inverse_ref, soma_ref,
    rhs_ref, partial_ref,
):
    comp_count, cell_dev = base_ref.shape
    block_count = group_ref.shape[0]
    block_size = comp_count // block_count
    even = core() == 0

    def owners(first, count, step):
        mine, other = (
            [ref[pl.ds(j * devices + first, count, stride=step), :] for j in range(LOW // 256)]
            for ref in (half_ref, other_ref)
        )
        low = [jnp.where(even, a, b) for a, b in zip(mine, other)]
        return low + [jnp.where(even, b, a) for a, b in zip(mine, other)]

    half = devices // 2
    size = within_ref.shape[0]
    sides = [
        look_up(
            owners(side, half, 2),
            within_ref[:half, side * 128 : (side + 1) * 128],
        )
        for side in range(2)
    ]
    heavy = lax.broadcasted_iota(jnp.int32, (devices, 128), 0) == within_ref[half : half + 1, 128:129]
    owner = []
    for rows in owners(0, devices, 1):
        one = jnp.sum(jnp.where(heavy, rows, 0.0), axis=0, keepdims=True)
        owner.append(jnp.broadcast_to(one, (size - half, 128)))
    rest = look_up(owner, within_ref[half:, :128])
    table = jnp.concatenate(
        [
            jnp.concatenate([sides[0], rest], axis=0),
            jnp.concatenate([sides[1], jnp.zeros_like(rest)], axis=0),
        ],
        axis=1,
    )
    table = jnp.concatenate(halves(table), axis=0)
    column = jnp.concatenate([column_ref[k : k + 1, :] for k in range(block_count)], axis=1)
    group = jnp.concatenate([group_ref[k : k + 1, :] for k in range(block_count)], axis=1)
    found = jnp.dot(table, hot(column, 256), preferred_element_type=f32)
    groups = lax.broadcasted_iota(jnp.int32, (size, group.shape[1]), 0)
    both = jnp.where(groups == group, found[:size] + found[size:], 0.0)
    phi = jnp.sum(both, axis=0, keepdims=True)
    looked = [
        jnp.broadcast_to(phi[:, k * cell_dev : (k + 1) * cell_dev], (block_size, cell_dev))
        for k in range(block_count)
    ]
    field = ephaptic * jnp.concatenate(looked, axis=0)
    rhs_ref[...] = base_ref[...] - field
    partial_ref[...] = soma_ref[1:2, 0:1] * (first_ref[...] - head_term(inverse_ref, field))


def last_kernel(
    solved_ref, p0_ref, p1_ref, p2_ref, p3_ref, soma_v_ref, soma_stim_ref,
    inverse_ref, soma_ref, potential_ref, volts_ref, soma_out, potential_out,
):
    potential_out[...] = potential_ref[...]
    soma = next_soma(
        soma_v_ref[...], soma_stim_ref[...],
        [p0_ref[...], p1_ref[...], p2_ref[...], p3_ref[...]], soma_ref[0:1, 0:1],
    )
    soma_out[...] = soma
    volts_ref[...] = solved_ref[...] + soma_ref[1:2, 0:1] * inverse_ref[:, 0:1] * soma


def call(kernel, ins, outs, scratch=(), flops=0):
    space = lambda stays: pl.BlockSpec(memory_space=pltpu.HBM if stays else pltpu.VMEM)
    run = pl.pallas_call(
        kernel,
        in_specs=[space(stays) for stays in ins],
        out_specs=[space(out[2]) for out in outs],
        out_shape=[jax.ShapeDtypeStruct(out[0], out[1]) for out in outs],
        scratch_shapes=list(scratch),
        compiler_params=pltpu.CompilerParams(vmem_limit_bytes=VMEM_BYTES),
        cost_estimate=pl.CostEstimate(flops=flops, bytes_accessed=2**20, transcendentals=0),
    )

    def placed(*operands):
        return run(*[
            pltpu.with_memory_space_constraint(x, pltpu.HBM) if stays else x
            for x, stays in zip(operands, ins, strict=True)
        ])

    return placed


def bind(kernel, *sizes):
    def bound(*refs):
        kernel(*sizes, *refs)

    return bound


def exchange(send, devices):
    flat = lax.all_to_all(
        send.reshape(devices, send.size // devices), AXES, split_axis=0, concat_axis=0, tiled=True
    )
    return flat.reshape(send.shape)


def other_core(array, n_cells):
    return lax.ppermute(array, "cells", [(i, i ^ 1) for i in range(n_cells)])


def split_terms(partial, n_split):
    terms = [partial]
    for k in range(n_split - 1, 0, -1):
        pairs = [(i, (i + k) % n_split) for i in range(n_split)]
        terms.append(lax.ppermute(partial, "split", pairs))
    return terms


def per_device(
    voltage, gate_state, stimulus, gate_rate, gate_conductance, soma_voltage, soma_stimulus,
    axial_conductance, gap_source, gap_route, gap_target, gap_conductance, vox_index, field_resist,
):
    n_split = lax.axis_size("split")
    n_cells = lax.axis_size("cells")
    devices = n_cells * n_split
    comp_count, cell_dev = voltage.shape[1:]
    rows = gap_source.shape[0]
    vox_dev = field_resist.shape[0]
    field_scale = vox_dev / (comp_count * cell_dev)
    volts, gate, stim = voltage[0], gate_state[0], stimulus[0]
    rate, cond, vox = gate_rate[0], gate_conductance[0], vox_index[0]
    source = gap_source.reshape(1, rows)
    route = gap_route.reshape(1, rows)
    target = gap_target.reshape(1, rows)
    weight = gap_conductance.reshape(1, rows)
    soma_v = soma_voltage.reshape(1, cell_dev)
    soma_stim = soma_stimulus.reshape(1, cell_dev)
    resist = field_resist.reshape(vox_dev // 128, 128)

    i32 = jnp.int32
    shape = (comp_count, cell_dev)
    full = (shape, f32, False)
    full_hbm = (shape, f32, True)
    line = ((1, cell_dev), f32, False)
    parts = vox_dev // 128
    quads = ((parts, 128), f32, False)
    table = pltpu.VMEM((2 * cell_dev // LOW * comp_count, LOW), bf16)
    field = pltpu.VMEM(shape, f32)

    row = ((1, CAP * devices), f32, False)
    row_i32 = ((1, CAP * devices), i32, False)

    blocks_shape = (vox.shape, f32, False)
    sums = ((devices, vox_dev // 2), f32, False)
    gap_rows = ((devices, 128), f32, False)
    table_out = (table.shape, bf16, False)

    stride = parts // 2 + 1
    kept = (
        volts, rate, cond, stim, vox, source, route, weight, target, soma_v, soma_stim, resist,
    )
    used = (gate, axial_conductance)
    outs = call(
        bind(first_kernel, devices),
        [True] * (len(kept) + len(used)),
        [(x.shape, x.dtype, False) for x in kept]
        + [
            ((1, rows), i32, False), full, full, blocks_shape,
            ((comp_count, 128), f32, False), ((2, 128), f32, False), sums,
        ],
        [pltpu.VMEM(x.shape, x.dtype) for x in used]
        + [pltpu.SemaphoreType.DMA((len(kept) + len(used),))],
    )(*kept, *used)
    (
        volts, rate, cond, stim, vox, source, route, weight, target, soma_v, soma_stim, resist,
    ) = outs[: len(kept)]
    rank, gate, base, blocks, inverse, soma_consts, other = outs[len(kept) :]
    other = other_core(other, n_cells)
    own, slot_rows_out, volts_table = call(
        bind(first_rows_kernel, devices), [False] * 8, [sums, gap_rows, table_out], flops=4 * 10**9
    )(vox, blocks, volts, source, route, target, weight, rank)
    (send,) = call(
        bind(first_send_kernel, devices, stride), [False] * 3,
        [((devices * stride, 128), f32, False)],
    )(own, other, slot_rows_out)
    received = exchange(send, devices)
    partial, slot_target, slot_weight, factor, gap, potential = call(
        bind(second_kernel, devices, stride, n_split, field_scale),
        [False] * 6,
        [line, row_i32, row, row, row, quads],
    )(received, base, volts_table, inverse, soma_consts, resist)
    terms = split_terms(partial, n_split)
    solve = call(solve_kernel, [False] * 4, [full], flops=3 * 10**9)
    (solved,) = solve(base, slot_target, gap, inverse)

    stride = parts // 2 + parts // 2 + 1
    operands = (
        solved, *terms, soma_v, soma_stim, inverse, soma_consts, gate, rate, cond, stim, vox,
    )
    gate, soma, base, blocks, volts, other = call(
        bind(third_kernel, devices),
        [False] * len(operands),
        [full_hbm, line, full, blocks_shape, full, sums],
        [field, pltpu.SemaphoreType.DMA],
    )(*operands)
    other = other_core(other, n_cells)
    own, slot_rows_out, volts_table = call(
        bind(third_rows_kernel, devices), [False] * 7, [sums, gap_rows, table_out], flops=4 * 10**9
    )(vox, blocks, volts, source, route, weight, rank)
    send, slot_target = call(
        bind(third_send_kernel, devices, stride, n_split), [False] * 5,
        [((devices * stride, 128), f32, False), row_i32],
    )(own, other, slot_rows_out, potential, slot_target)
    received = exchange(send, devices)
    groups = devices // 2 + 16
    here, group, column, within = call(
        bind(beside_kernel, devices),
        [False] * 4,
        [
            row, (vox.shape, i32, False), (vox.shape, i32, False),
            ((groups, 256), i32, False),
        ],
        flops=8 * 10**9,
    )(volts_table, slot_target, base, vox)
    half, within = call(
        bind(fourth_half_kernel, devices, stride), [False] * 2,
        [((parts // 2 * devices, 128), f32, False), (within.shape, i32, False)],
    )(received, within)
    other = other_core(half, n_cells)
    first, gap, potential = call(
        bind(fourth_rows_kernel, devices, stride, n_split, field_scale),
        [False] * 9,
        [line, row, quads],
        flops=10**9,
    )(received, half, here, slot_target, slot_weight, factor, base, inverse, resist)
    rhs, partial = call(bind(fourth_kernel, devices), [False] * 9, [full, line])(
        half, other, group, column, within, base, first, inverse, soma_consts
    )
    terms = split_terms(partial, n_split)
    (solved,) = solve(rhs, slot_target, gap, inverse)

    operands = (solved, *terms, soma, soma_stim, inverse, soma_consts, potential)
    volts, soma, potential = call(
        last_kernel,
        [False] * len(operands),
        [full, line, quads],
    )(*operands)
    return volts[None], gate[None], soma.reshape(cell_dev), potential.reshape(vox_dev)


def solution(mesh):
    wide = P("split", None, "cells")
    every = P(AXES)
    in_specs = (
        wide, wide, wide, wide, wide, P("cells"), P("cells"), P(),
        every, P(AXES, None), every, every, wide, every,
    )
    out_specs = (wide, wide, P("cells"), every)
    return jax.shard_map(
        per_device, mesh=mesh, in_specs=in_specs, out_specs=out_specs, check_vma=False
    )
```

```python
import jax
import jax.numpy as jnp
from jax import lax
from jax.experimental import pallas as pl
from jax.experimental.pallas import tpu as pltpu
from jax.sharding import PartitionSpec as P

SUB = 2
CAP = 32
LOW = 512

membrane_diag = 4.0
soma_diag = 8.0
reversal = -1.0
ephaptic = 0.5

f32 = jnp.float32
bf16 = jnp.bfloat16
AXES = ("cells", "split")
VMEM_BYTES = 48 * 2**20
LANES = (((1,), (1,)), ((), ()))


def halves(x):
    high = x.astype(bf16)
    return high, (x - high.astype(f32)).astype(bf16)


def hits(row, size):
    rows = lax.broadcasted_iota(jnp.int16, (size, row.shape[1]), 0)
    return rows == row.astype(jnp.int16)


def chosen(mask, row):
    return jnp.where(mask, row, jnp.zeros((), bf16))


def hot(row, size):
    return jnp.where(hits(row, size), jnp.ones((), bf16), jnp.zeros((), bf16))


def comp_digits(index, cell_dev, comp_count):
    chunks = cell_dev // LOW
    low = index % LOW
    chunk = (index // LOW) % chunks
    return chunk * comp_count + index // cell_dev, low


def write_inverse(axial, branch, inverse_ref, soma_ref):
    branches, n = axial.shape
    lanes = 128
    index = lax.broadcasted_iota(jnp.int32, (lanes, n), 0)
    table = jnp.zeros((lanes, n), f32)
    for b in range(branches):
        mine = (index == n + b) | ((index < n) | (index >= n + branches)) & (branch == b)
        table = jnp.where(mine, axial[b : b + 1, :], table)
    table = jnp.concatenate([table, jnp.zeros((lanes, lanes - n), f32)], axis=1).T
    row = [table[i : i + 1, :] for i in range(n)]
    lane = lax.broadcasted_iota(jnp.int32, (1, lanes), 1)
    pivot = [None] * n
    ratio = [None] * n
    pivot[n - 1] = membrane_diag + row[n - 1]
    ratio[n - 1] = row[n - 1] / pivot[n - 1]
    for i in range(n - 2, -1, -1):
        pivot[i] = membrane_diag + row[i] + row[i + 1] - row[i + 1] * ratio[i + 1]
        ratio[i] = row[i] / pivot[i]
    upper = [None] * n
    upper[n - 1] = jnp.where(lane == n - 1, 1.0, 0.0)
    for i in range(n - 2, -1, -1):
        upper[i] = jnp.where(lane == i, 1.0, 0.0) + ratio[i + 1] * upper[i + 1]
    result = upper[0] / pivot[0]
    inverse_ref[0:1, :] = result
    for i in range(1, n):
        result = upper[i] / pivot[i] + ratio[i] * result
        inverse_ref[i : i + 1, :] = result
    each = (lane >= n) & (lane < n + branches)
    total = soma_diag + jnp.sum(jnp.where(each, row[0], 0.0), axis=1, keepdims=True)
    shared = jnp.sum(jnp.where(each, row[0] * ratio[0], 0.0), axis=1, keepdims=True)
    soma_ref[0:1, :] = jnp.broadcast_to(total - shared, (1, lanes))
    soma_ref[1:2, :] = jnp.broadcast_to(row[0][:, 0:1], (1, lanes))


def membrane(volts, gating, rate, cond):
    settle = jax.nn.sigmoid(2.0 * volts)
    gating = settle + (gating - settle) * jnp.exp(-rate * (1.0 + volts * volts))
    return gating, cond * gating * (volts - reversal)


def fill_table(table_ref, volts, comp_count, cell_dev):
    chunks = cell_dev // LOW
    high, low = halves(volts)
    for j in range(chunks):
        at = j * comp_count
        table_ref[at : at + comp_count, :] = high[:, j * LOW : (j + 1) * LOW]
        at += chunks * comp_count
        table_ref[at : at + comp_count, :] = low[:, j * LOW : (j + 1) * LOW]


def pick_rows(table_ref, source, comp_count, cell_dev):
    high, low = comp_digits(source, cell_dev, comp_count)
    return pick_hot(table_ref, high, hot(low, LOW))


def pick_hot(table_ref, high, low_hot):
    size = table_ref.shape[0] // 2
    found = jnp.dot(table_ref[...], low_hot, preferred_element_type=f32)
    rows = lax.broadcasted_iota(jnp.int32, (size, high.shape[1]), 0)
    both = jnp.where(rows == high, found[:size] + found[size:], 0.0)
    return jnp.sum(both, axis=0, keepdims=True)


def block_sums(current, block_count):
    size = current.shape[0] // block_count
    return jnp.concatenate(
        [
            jnp.sum(current[k * size : (k + 1) * size], axis=0, keepdims=True)
            for k in range(block_count)
        ],
        axis=0,
    )


def half_sums(vox, blocks, devices, half):
    owners, voxels = [], []
    for k in range(vox.shape[0]):
        index = vox[k : k + 1, :]
        high, low = halves(blocks[k : k + 1, :])
        mask = hits(index // LOW, devices)
        owners.append(jnp.concatenate([chosen(mask, high), chosen(mask, low)], axis=0))
        voxels.append(hot(index % LOW - half * (LOW // 2), LOW // 2))
    sums = lax.dot_general(
        jnp.concatenate(owners, axis=1),
        jnp.concatenate(voxels, axis=1),
        LANES,
        preferred_element_type=f32,
    )
    return sums[:devices] + sums[devices:]


def core():
    return lax.axis_index("cells") % 2


def put_rows(send_ref, first, values, devices, stride):
    for j in range(values.shape[1] // 128):
        send_ref[pl.ds(first + j, devices, stride=stride), :] = values[:, j * 128 : (j + 1) * 128]


def own_potential(potential_ref, recv_ref, resist_ref, devices, stride, n_split, field_scale):
    source = lax.broadcasted_iota(jnp.int32, (devices, 128), 0)
    odd = (source // n_split) % 2 == 1
    rows = LOW // 256
    for j in range(rows):
        each = recv_ref[pl.ds(j, devices, stride=stride), :]
        for half in range(2):
            mine = jnp.where(odd if half else ~odd, each, 0.0)
            own = jnp.sum(mine, axis=0, keepdims=True)
            at = half * rows + j
            potential_ref[at : at + 1, :] = resist_ref[at : at + 1, :] * own * field_scale


def slot_rows(values, dest_hot, rank_mask):
    parts = []
    for value in values:
        high, low = halves(value)
        parts += [chosen(rank_mask, high), chosen(rank_mask, low)]
    laid = lax.dot_general(
        jnp.concatenate(parts, axis=0), dest_hot, LANES, preferred_element_type=f32
    )
    return [
        laid[(2 * q) * CAP : (2 * q + 1) * CAP] + laid[(2 * q + 1) * CAP : (2 * q + 2) * CAP]
        for q in range(len(values))
    ]


def ranks_of(owner, devices):
    span = 256
    index = lax.broadcasted_iota(jnp.int32, (2 * span, span), 0)
    earlier = jnp.where(
        (index < lax.broadcasted_iota(jnp.int32, (2 * span, span), 1)) | (index >= span), 1.0, 0.0
    ).astype(bf16)
    before = jnp.zeros((devices, span), bf16)
    ranks, owners = [], []
    for at in range(0, owner.shape[1], span):
        one = hot(owner[:, at : at + span], devices)
        both = jnp.concatenate([one, before], axis=1)
        count = jnp.dot(both, earlier, preferred_element_type=f32)
        ranks.append(jnp.sum(one.astype(f32) * count, axis=0, keepdims=True))
        before = before + one
        owners.append(one)
    return jnp.concatenate(ranks, axis=1).astype(jnp.int32), jnp.concatenate(owners, axis=1)


def first_kernel(
    devices,
    volts_hbm, rate_hbm, cond_hbm, stim_hbm, vox_hbm, source_hbm, route_hbm, weight_hbm,
    target_hbm, soma_v_hbm, soma_stim_hbm, resist_hbm, gate_hbm, axial_hbm,
    volts_ref, rate_ref, cond_ref, stim_ref, vox_ref, source_ref, route_ref, weight_ref,
    target_ref, soma_v_ref, soma_stim_ref, resist_ref,
    rank_ref, gate_out, base_ref, blocks_ref, inverse_ref, soma_ref, other_ref,
    gate_ref, axial_ref, sems,
):
    pairs = [
        (axial_hbm, axial_ref), (route_hbm, route_ref), (volts_hbm, volts_ref),
        (gate_hbm, gate_ref), (rate_hbm, rate_ref), (cond_hbm, cond_ref), (vox_hbm, vox_ref),
        (stim_hbm, stim_ref), (source_hbm, source_ref), (target_hbm, target_ref),
        (weight_hbm, weight_ref), (soma_v_hbm, soma_v_ref), (soma_stim_hbm, soma_stim_ref),
        (resist_hbm, resist_ref),
    ]
    copies = [pltpu.make_async_copy(a, b, sems.at[i]) for i, (a, b) in enumerate(pairs)]
    for copy in copies:
        copy.start()
    copies[0].wait()
    write_inverse(axial_ref[...], lax.axis_index("split"), inverse_ref, soma_ref)
    copies[1].wait()
    rank_ref[...], unused = ranks_of(route_ref[...], devices)
    for copy in copies[2:8]:
        copy.wait()
    volts = volts_ref[...]
    gating, current = membrane(volts, gate_ref[...], rate_ref[...], cond_ref[...])
    gate_out[...] = gating
    base_ref[...] = membrane_diag * volts + stim_ref[...] - current
    blocks = block_sums(current, vox_ref.shape[0])
    blocks_ref[...] = blocks
    other_ref[...] = half_sums(vox_ref[...], blocks, devices, 1 - core())
    for copy in copies[8:]:
        copy.wait()


def first_rows_kernel(
    devices,
    vox_ref, blocks_ref, volts_ref, source_ref, route_ref, target_ref, weight_ref, rank_ref,
    own_ref, rows_ref, table_ref,
):
    comp_count, cell_dev = volts_ref.shape
    own_ref[...] = half_sums(vox_ref[...], blocks_ref[...], devices, core())
    fill_table(table_ref, volts_ref[...], comp_count, cell_dev)
    weight = weight_ref[...]
    sent = weight * pick_rows(table_ref, source_ref[...], comp_count, cell_dev)
    values = [target_ref[...].astype(f32), weight, sent]
    slots = slot_rows(values, hot(route_ref[...], devices), hits(rank_ref[...], CAP))
    slots.append(jnp.zeros((128 - 3 * CAP, devices), f32))
    rows_ref[...] = jnp.concatenate(slots, axis=0).T


def first_send_kernel(devices, stride, own_ref, other_ref, rows_ref, send_ref):
    put_rows(send_ref, 0, own_ref[...] + other_ref[...], devices, stride)
    put_rows(send_ref, stride - 1, rows_ref[...], devices, stride)


def wide(slots):
    return jnp.concatenate([slots[k : k + 1] for k in range(slots.shape[0])], axis=1)


def add_heads(values, target, cell_dev):
    size = cell_dev // 128
    cell = target % cell_dev
    high, low = halves(values)
    mask = hits(cell // 128, size)
    left = jnp.concatenate([chosen(mask, high), chosen(mask, low)], axis=0)
    laid = lax.dot_general(left, hot(cell % 128, 128), LANES, preferred_element_type=f32)
    return wide(laid[:size] + laid[size:])


def add_slots(values, target, comp_count, cell_dev):
    size = cell_dev // LOW * comp_count
    row, column = comp_digits(target, cell_dev, comp_count)
    high, low = halves(values)
    mask = hits(row, size)
    left = jnp.concatenate([chosen(mask, high), chosen(mask, low)], axis=0)
    laid = lax.dot_general(left, hot(column, LOW), LANES, preferred_element_type=f32)
    return as_cells(laid[:size] + laid[size:], comp_count)


def as_cells(total, comp_count):
    chunks = total.shape[0] // comp_count
    return jnp.concatenate(
        [total[j * comp_count : (j + 1) * comp_count] for j in range(chunks)], axis=1
    )


def head_term(inverse_ref, rhs):
    return jnp.sum(inverse_ref[:, 0:1] * rhs, axis=0, keepdims=True)


def second_kernel(
    devices, stride, n_split, field_scale,
    recv_ref, base_ref, table_ref, inverse_ref, soma_ref, resist_ref,
    partial_ref, target_ref, weight_ref, factor_ref, gap_ref, potential_ref,
):
    comp_count, cell_dev = base_ref.shape
    slots = recv_ref[pl.ds(stride - 1, devices, stride=stride), :].T
    target = wide(slots[:CAP].astype(jnp.int32))
    target_ref[...] = target
    weight = wide(slots[CAP : 2 * CAP])
    weight_ref[...] = weight
    comps = lax.broadcasted_iota(jnp.int32, (comp_count, CAP * devices), 0)
    factor = jnp.sum(
        jnp.where(comps == target // cell_dev, inverse_ref[:, 0:1], 0.0),
        axis=0, keepdims=True,
    )
    factor_ref[...] = factor
    here = pick_rows(table_ref, target, comp_count, cell_dev)
    gap = wide(slots[2 * CAP : 3 * CAP]) - weight * here
    gap_ref[...] = gap
    first = head_term(inverse_ref, base_ref[...]) + add_heads(factor * gap, target, cell_dev)
    partial_ref[...] = soma_ref[1:2, 0:1] * first
    own_potential(potential_ref, recv_ref, resist_ref, devices, stride, n_split, field_scale)


def solve(inverse_ref, rhs):
    high, low = halves(inverse_ref[:, : rhs.shape[0]])
    left = jnp.concatenate([high, high, low, low], axis=1)
    high, low = halves(rhs)
    right = jnp.concatenate([high, low, high, low], axis=0)
    return jnp.dot(left, right, preferred_element_type=f32)


def solve_kernel(base_ref, target_ref, gap_ref, inverse_ref, solved_ref):
    comp_count, cell_dev = base_ref.shape
    gap_in = add_slots(gap_ref[...], target_ref[...], comp_count, cell_dev)
    solved_ref[...] = solve(inverse_ref, base_ref[...] + gap_in)


def beside_kernel(
    devices,
    table_ref, target_ref, cells_ref, vox_ref,
    here_ref, group_ref, column_ref, within_ref,
):
    comp_count, cell_dev = cells_ref.shape
    here_ref[...] = pick_rows(table_ref, target_ref[...], comp_count, cell_dev)
    block_count = vox_ref.shape[0]
    vox = jnp.concatenate([vox_ref[k : k + 1, :] for k in range(block_count)], axis=1)
    owner = vox // LOW
    rank, unused = ranks_of(owner, devices)
    over = rank >= 128
    group = jnp.where(over, devices // 2, owner // 2)
    column = jnp.where(over, rank - 128, owner % 2 * 128 + rank)
    for k in range(block_count):
        group_ref[k : k + 1, :] = group[:, k * cell_dev : (k + 1) * cell_dev]
        column_ref[k : k + 1, :] = column[:, k * cell_dev : (k + 1) * cell_dev]
    heavy = jnp.max(jnp.where(over, owner, -1), axis=1, keepdims=True)
    size = within_ref.shape[0]
    mask = hits(group, size)
    high, low = halves((vox % LOW).astype(f32))
    left = jnp.concatenate([chosen(mask, high), chosen(mask, low)], axis=0)
    laid = lax.dot_general(left, hot(column, 256), LANES, preferred_element_type=f32)
    half = devices // 2
    within_ref[...] = (laid[:size] + laid[size:]).astype(jnp.int32)
    within_ref[half:, 128:] = jnp.broadcast_to(heavy, (size - half, 128))


def look_up(parts, index):
    found = jnp.zeros(index.shape, f32)
    for j, part in enumerate(parts):
        there = jnp.take_along_axis(part, index % 128, axis=1, mode="promise_in_bounds")
        found = jnp.where(index // 128 == j, there, found)
    return found


def next_soma(soma, stimulus, partials, total):
    partial = (partials[0] + partials[1]) + (partials[2] + partials[3])
    return (soma_diag * soma + stimulus + partial) / total


def third_kernel(
    devices,
    solved_ref, p0_ref, p1_ref, p2_ref, p3_ref, soma_v_ref, soma_stim_ref,
    inverse_ref, soma_ref, gate_ref, rate_ref, cond_ref, stim_ref, vox_ref,
    gate_hbm, soma_out, base_ref, blocks_ref, volts_ref, other_ref,
    gate_out, sem,
):
    soma = next_soma(
        soma_v_ref[...], soma_stim_ref[...],
        [p0_ref[...], p1_ref[...], p2_ref[...], p3_ref[...]], soma_ref[0:1, 0:1],
    )
    soma_out[...] = soma
    volts = solved_ref[...] + soma_ref[1:2, 0:1] * inverse_ref[:, 0:1] * soma
    volts_ref[...] = volts
    gating, current = membrane(volts, gate_ref[...], rate_ref[...], cond_ref[...])
    gate_out[...] = gating
    copy = pltpu.make_async_copy(gate_out, gate_hbm, sem)
    copy.start()
    base_ref[...] = membrane_diag * volts + stim_ref[...] - current
    blocks = block_sums(current, vox_ref.shape[0])
    blocks_ref[...] = blocks
    other_ref[...] = half_sums(vox_ref[...], blocks, devices, 1 - core())
    copy.wait()


def third_rows_kernel(
    devices,
    vox_ref, blocks_ref, volts_ref, source_ref, route_ref, weight_ref, rank_ref,
    own_ref, rows_ref, table_ref,
):
    comp_count, cell_dev = volts_ref.shape
    own_ref[...] = half_sums(vox_ref[...], blocks_ref[...], devices, core())
    fill_table(table_ref, volts_ref[...], comp_count, cell_dev)
    sent = weight_ref[...] * pick_rows(table_ref, source_ref[...], comp_count, cell_dev)
    slots = slot_rows([sent], hot(route_ref[...], devices), hits(rank_ref[...], CAP))
    slots.append(jnp.zeros((128 - CAP, devices), f32))
    rows_ref[...] = jnp.concatenate(slots, axis=0).T


def third_send_kernel(
    devices, stride, n_split, own_ref, other_ref, rows_ref, potential_ref, target_ref,
    send_ref, target_out,
):
    target_out[...] = target_ref[...]
    put_rows(send_ref, 0, own_ref[...] + other_ref[...], devices, stride)
    rows = LOW // 256
    target = lax.broadcasted_iota(jnp.int32, (devices, 128), 0)
    odd = (target // n_split) % 2 == 1
    for j in range(rows):
        each = jnp.where(
            odd, potential_ref[rows + j : rows + j + 1, :], potential_ref[j : j + 1, :]
        )
        put_rows(send_ref, rows + j, each, devices, stride)
    put_rows(send_ref, stride - 1, rows_ref[...], devices, stride)


def fourth_half_kernel(devices, stride, recv_ref, within_ref, half_ref, within_out):
    within_out[...] = within_ref[...]
    rows = LOW // 256
    for j in range(rows):
        half_ref[j * devices : (j + 1) * devices, :] = recv_ref[
            pl.ds(rows + j, devices, stride=stride), :
        ]


def fourth_rows_kernel(
    devices, stride, n_split, field_scale,
    recv_ref, half_ref, here_ref, target_ref, weight_ref, factor_ref, base_ref,
    inverse_ref, resist_ref,
    first_ref, gap_ref, potential_ref,
):
    cell_dev = base_ref.shape[1]
    slots = recv_ref[pl.ds(stride - 1, devices, stride=stride), :].T
    gap = wide(slots[:CAP]) - weight_ref[...] * here_ref[...]
    gap_ref[...] = gap
    heads = add_heads(factor_ref[...] * gap, target_ref[...], cell_dev)
    first_ref[...] = head_term(inverse_ref, base_ref[...]) + heads
    own_potential(potential_ref, recv_ref, resist_ref, devices, stride, n_split, field_scale)


def fourth_kernel(
    devices,
    half_ref, other_ref, group_ref, column_ref, within_ref,
    base_ref, first_ref, inverse_ref, soma_ref,
    rhs_ref, partial_ref,
):
    comp_count, cell_dev = base_ref.shape
    block_count = group_ref.shape[0]
    block_size = comp_count // block_count
    even = core() == 0

    def owners(first, count, step):
        mine, other = (
            [ref[pl.ds(j * devices + first, count, stride=step), :] for j in range(LOW // 256)]
            for ref in (half_ref, other_ref)
        )
        low = [jnp.where(even, a, b) for a, b in zip(mine, other)]
        return low + [jnp.where(even, b, a) for a, b in zip(mine, other)]

    half = devices // 2
    size = within_ref.shape[0]
    sides = [
        look_up(
            owners(side, half, 2),
            within_ref[:half, side * 128 : (side + 1) * 128],
        )
        for side in range(2)
    ]
    heavy = lax.broadcasted_iota(jnp.int32, (devices, 128), 0) == within_ref[half : half + 1, 128:129]
    owner = []
    for rows in owners(0, devices, 1):
        one = jnp.sum(jnp.where(heavy, rows, 0.0), axis=0, keepdims=True)
        owner.append(jnp.broadcast_to(one, (size - half, 128)))
    rest = look_up(owner, within_ref[half:, :128])
    table = jnp.concatenate(
        [
            jnp.concatenate([sides[0], rest], axis=0),
            jnp.concatenate([sides[1], jnp.zeros_like(rest)], axis=0),
        ],
        axis=1,
    )
    table = jnp.concatenate(halves(table), axis=0)
    column = jnp.concatenate([column_ref[k : k + 1, :] for k in range(block_count)], axis=1)
    group = jnp.concatenate([group_ref[k : k + 1, :] for k in range(block_count)], axis=1)
    found = jnp.dot(table, hot(column, 256), preferred_element_type=f32)
    groups = lax.broadcasted_iota(jnp.int32, (size, group.shape[1]), 0)
    both = jnp.where(groups == group, found[:size] + found[size:], 0.0)
    phi = jnp.sum(both, axis=0, keepdims=True)
    looked = [
        jnp.broadcast_to(phi[:, k * cell_dev : (k + 1) * cell_dev], (block_size, cell_dev))
        for k in range(block_count)
    ]
    field = ephaptic * jnp.concatenate(looked, axis=0)
    rhs_ref[...] = base_ref[...] - field
    partial_ref[...] = soma_ref[1:2, 0:1] * (first_ref[...] - head_term(inverse_ref, field))


def last_kernel(
    solved_ref, p0_ref, p1_ref, p2_ref, p3_ref, soma_v_ref, soma_stim_ref,
    inverse_ref, soma_ref, potential_ref, volts_ref, soma_out, potential_out,
):
    potential_out[...] = potential_ref[...]
    soma = next_soma(
        soma_v_ref[...], soma_stim_ref[...],
        [p0_ref[...], p1_ref[...], p2_ref[...], p3_ref[...]], soma_ref[0:1, 0:1],
    )
    soma_out[...] = soma
    volts_ref[...] = solved_ref[...] + soma_ref[1:2, 0:1] * inverse_ref[:, 0:1] * soma


def call(kernel, ins, outs, scratch=(), flops=0):
    space = lambda stays: pl.BlockSpec(memory_space=pltpu.HBM if stays else pltpu.VMEM)
    run = pl.pallas_call(
        kernel,
        in_specs=[space(stays) for stays in ins],
        out_specs=[space(out[2]) for out in outs],
        out_shape=[jax.ShapeDtypeStruct(out[0], out[1]) for out in outs],
        scratch_shapes=list(scratch),
        compiler_params=pltpu.CompilerParams(vmem_limit_bytes=VMEM_BYTES),
        cost_estimate=pl.CostEstimate(flops=flops, bytes_accessed=2**20, transcendentals=0),
    )

    def placed(*operands):
        return run(*[
            pltpu.with_memory_space_constraint(x, pltpu.HBM) if stays else x
            for x, stays in zip(operands, ins, strict=True)
        ])

    return placed


def bind(kernel, *sizes):
    def bound(*refs):
        kernel(*sizes, *refs)

    return bound


def exchange(send, devices):
    flat = lax.all_to_all(
        send.reshape(devices, send.size // devices), AXES, split_axis=0, concat_axis=0, tiled=True
    )
    return flat.reshape(send.shape)


def other_core(array, n_cells):
    return lax.ppermute(array, "cells", [(i, i ^ 1) for i in range(n_cells)])


def split_terms(partial, n_split):
    terms = [partial]
    for k in range(n_split - 1, 0, -1):
        pairs = [(i, (i + k) % n_split) for i in range(n_split)]
        terms.append(lax.ppermute(partial, "split", pairs))
    return terms


def per_device(
    voltage, gate_state, stimulus, gate_rate, gate_conductance, soma_voltage, soma_stimulus,
    axial_conductance, gap_source, gap_route, gap_target, gap_conductance, vox_index, field_resist,
):
    n_split = lax.axis_size("split")
    n_cells = lax.axis_size("cells")
    devices = n_cells * n_split
    comp_count, cell_dev = voltage.shape[1:]
    rows = gap_source.shape[0]
    vox_dev = field_resist.shape[0]
    field_scale = vox_dev / (comp_count * cell_dev)
    volts, gate, stim = voltage[0], gate_state[0], stimulus[0]
    rate, cond, vox = gate_rate[0], gate_conductance[0], vox_index[0]
    source = gap_source.reshape(1, rows)
    route = gap_route.reshape(1, rows)
    target = gap_target.reshape(1, rows)
    weight = gap_conductance.reshape(1, rows)
    soma_v = soma_voltage.reshape(1, cell_dev)
    soma_stim = soma_stimulus.reshape(1, cell_dev)
    resist = field_resist.reshape(vox_dev // 128, 128)

    i32 = jnp.int32
    shape = (comp_count, cell_dev)
    full = (shape, f32, False)
    full_hbm = (shape, f32, True)
    line = ((1, cell_dev), f32, False)
    parts = vox_dev // 128
    quads = ((parts, 128), f32, False)
    table = pltpu.VMEM((2 * cell_dev // LOW * comp_count, LOW), bf16)
    field = pltpu.VMEM(shape, f32)

    row = ((1, CAP * devices), f32, False)
    row_i32 = ((1, CAP * devices), i32, False)

    blocks_shape = (vox.shape, f32, False)
    sums = ((devices, vox_dev // 2), f32, False)
    gap_rows = ((devices, 128), f32, False)
    table_out = (table.shape, bf16, False)

    stride = parts // 2 + 1
    kept = (
        volts, rate, cond, stim, vox, source, route, weight, target, soma_v, soma_stim, resist,
    )
    used = (gate, axial_conductance)
    outs = call(
        bind(first_kernel, devices),
        [True] * (len(kept) + len(used)),
        [(x.shape, x.dtype, False) for x in kept]
        + [
            ((1, rows), i32, False), full, full, blocks_shape,
            ((comp_count, 128), f32, False), ((2, 128), f32, False), sums,
        ],
        [pltpu.VMEM(x.shape, x.dtype) for x in used]
        + [pltpu.SemaphoreType.DMA((len(kept) + len(used),))],
    )(*kept, *used)
    (
        volts, rate, cond, stim, vox, source, route, weight, target, soma_v, soma_stim, resist,
    ) = outs[: len(kept)]
    rank, gate, base, blocks, inverse, soma_consts, other = outs[len(kept) :]
    other = other_core(other, n_cells)
    own, slot_rows_out, volts_table = call(
        bind(first_rows_kernel, devices), [False] * 8, [sums, gap_rows, table_out], flops=4 * 10**9
    )(vox, blocks, volts, source, route, target, weight, rank)
    (send,) = call(
        bind(first_send_kernel, devices, stride), [False] * 3,
        [((devices * stride, 128), f32, False)],
    )(own, other, slot_rows_out)
    received = exchange(send, devices)
    partial, slot_target, slot_weight, factor, gap, potential = call(
        bind(second_kernel, devices, stride, n_split, field_scale),
        [False] * 6,
        [line, row_i32, row, row, row, quads],
    )(received, base, volts_table, inverse, soma_consts, resist)
    terms = split_terms(partial, n_split)
    solve = call(solve_kernel, [False] * 4, [full], flops=3 * 10**9)
    (solved,) = solve(base, slot_target, gap, inverse)

    stride = parts // 2 + parts // 2 + 1
    operands = (
        solved, *terms, soma_v, soma_stim, inverse, soma_consts, gate, rate, cond, stim, vox,
    )
    gate, soma, base, blocks, volts, other = call(
        bind(third_kernel, devices),
        [False] * len(operands),
        [full_hbm, line, full, blocks_shape, full, sums],
        [field, pltpu.SemaphoreType.DMA],
    )(*operands)
    other = other_core(other, n_cells)
    own, slot_rows_out, volts_table = call(
        bind(third_rows_kernel, devices), [False] * 7, [sums, gap_rows, table_out], flops=4 * 10**9
    )(vox, blocks, volts, source, route, weight, rank)
    send, slot_target = call(
        bind(third_send_kernel, devices, stride, n_split), [False] * 5,
        [((devices * stride, 128), f32, False), row_i32],
    )(own, other, slot_rows_out, potential, slot_target)
    received = exchange(send, devices)
    groups = devices // 2 + 16
    here, group, column, within = call(
        bind(beside_kernel, devices),
        [False] * 4,
        [
            row, (vox.shape, i32, False), (vox.shape, i32, False),
            ((groups, 256), i32, False),
        ],
        flops=8 * 10**9,
    )(volts_table, slot_target, base, vox)
    half, within = call(
        bind(fourth_half_kernel, devices, stride), [False] * 2,
        [((parts // 2 * devices, 128), f32, False), (within.shape, i32, False)],
    )(received, within)
    other = other_core(half, n_cells)
    first, gap, potential = call(
        bind(fourth_rows_kernel, devices, stride, n_split, field_scale),
        [False] * 9,
        [line, row, quads],
        flops=10**9,
    )(received, half, here, slot_target, slot_weight, factor, base, inverse, resist)
    rhs, partial = call(bind(fourth_kernel, devices), [False] * 9, [full, line])(
        half, other, group, column, within, base, first, inverse, soma_consts
    )
    terms = split_terms(partial, n_split)
    (solved,) = solve(rhs, slot_target, gap, inverse)

    operands = (solved, *terms, soma, soma_stim, inverse, soma_consts, potential)
    volts, soma, potential = call(
        last_kernel,
        [False] * len(operands),
        [full, line, quads],
    )(*operands)
    return volts[None], gate[None], soma.reshape(cell_dev), potential.reshape(vox_dev)


def solution(mesh):
    wide = P("split", None, "cells")
    every = P(AXES)
    in_specs = (
        wide, wide, wide, wide, wide, P("cells"), P("cells"), P(),
        every, P(AXES, None), every, every, wide, every,
    )
    out_specs = (wide, wide, P("cells"), every)
    return jax.shard_map(
        per_device, mesh=mesh, in_specs=in_specs, out_specs=out_specs, check_vma=False
    )
```
